512 devices in a mesh: clip: 8 (over z), guide: 2 (over x_lo), seq: 32 (over y, x_hi, core).
Axes of the slice: x: 4 (x_hi: 2, x_lo: 2; x = x_hi * 2 + x_lo), y: 8, z: 8, core: 2. Of those that a mesh axis runs over, the one named last changes fastest.
Arguments:
- latents: bfloat16 [8, 2, 12288, 1536], P('clip', 'guide', 'seq'), may hold values from -6 to 6
- prompt: bfloat16 [8, 128, 1536], P('clip'), may hold values from -6 to 6
- null_embed: bfloat16 [128, 1536], replicated, may hold values from -6 to 6
- text_lengths: int32 [8], P('clip'), may hold values from 32 to 128, as said below
- timesteps: int32 [8], P('clip'), may hold values from 0 to 49
- head_mod: float32 [50, 2, 1536], replicated, may hold values from -3 to 3
- cross_gain: float32 [1536], replicated, may hold values from 0.1 to 1.9
- cross_bias: float32 [1536], replicated, may hold values from -3 to 3
- q_gain: float32 [1536], replicated, may hold values from 0.1 to 1.9
- k_gain: float32 [1536], replicated, may hold values from 0.1 to 1.9
- w_query: bfloat16 [1536, 1536], P(None, 'seq'), may hold values from -0.15625 to 0.15625
- w_key: bfloat16 [1536, 1536], P(None, 'seq'), may hold values from -0.15625 to 0.15625
- w_value: bfloat16 [1536, 1536], P(None, 'seq'), may hold values from -0.15625 to 0.15625
- w_out: bfloat16 [1536, 1536], P(None, 'seq'), may hold values from -0.15625 to 0.15625
- w_head: bfloat16 [1536, 64], replicated, may hold values from -0.15625 to 0.15625
- head_bias: float32 [64], replicated, may hold values from -3 to 3
- target: bfloat16 [8, 12288, 64], P('clip', 'seq'), may hold values from -6 to 6
Outputs:
- guided: float32 [8, 12288, 64], P('clip', 'seq')
- embed_grad: float32 [8, 2, 128, 1536], P('clip', 'guide', 'seq')
The draws below stay inside these ranges and needn't reach their ends.
Inputs may be any that keep to these rules, and one draw needn't show every extreme that they name: `text_lengths`: each clip has at least 32 visible prompt tokens; some clip has all 128.
All inputs are finite; a program needn't handle non-finite values.
Results may differ from the reference program's by a relative error of at most 0.0046.
Values may be sent and summed in bfloat16 or wider, within the bound.
A program may use at most 64 MiB of HBM per device.

```python
import math
import jax
import jax.numpy as jnp
from jax import lax

D = 1536
HEADS = 12
PATCH = 64
TEXT_LEN = 128
STEPS = 50
CLIPS = 8
TOKENS = 12288


def draw_text_lengths(key, part):
    key = jax.random.fold_in(key, 11)
    drawn = jax.random.randint(key, (CLIPS,), TEXT_LEN // 4, TEXT_LEN + 1)
    chosen = jax.random.randint(jax.random.fold_in(key, 5), (), 0, CLIPS)
    return jnp.where(jnp.arange(CLIPS) == chosen, TEXT_LEN, drawn).astype(jnp.int32)


def draw_timesteps(key, part):
    key = jax.random.fold_in(key, 23)
    middle = 1 + jax.random.permutation(key, STEPS - 2)[:CLIPS - 2]
    ordered = jnp.concatenate([jnp.array([0, STEPS - 1], dtype=jnp.int32), middle.astype(jnp.int32)])
    order = jax.random.permutation(jax.random.fold_in(key, 7), CLIPS)
    return ordered[order].astype(jnp.int32)


def block_scale(stream_key, extent, pieces, smallest, high):
    gain = 1.0
    for dim, parts in pieces:
        heights = jax.random.uniform(jax.random.fold_in(jax.random.fold_in(stream_key, 6), dim), (parts,), jnp.float32, smallest / len(pieces), high / len(pieces))
        gain = gain * jnp.repeat(jnp.exp(heights), extent[dim] // parts).reshape((-1,) + (1,) * (len(extent) - 1 - dim))
    return gain


def normal_values(own_key, dims, width, reach, split=(), held_as=jnp.bfloat16):
    values = width * jax.random.normal(own_key, dims, jnp.float32)
    if split:
        values = values * block_scale(own_key, dims, split, -0.22, 0.18)
    return jnp.clip(values, -reach, reach).astype(held_as)


def setup_inputs(seed: int = 0) -> dict:
    arg_keys = jax.random.split(jax.random.key(seed), 18)
    return {
        "latents": normal_values(arg_keys[0], (CLIPS, 2, TOKENS, D), 1.0, 6.0, ((0, 8), (1, 2), (2, 32))),
        "prompt": normal_values(arg_keys[1], (CLIPS, TEXT_LEN, D), 1.0, 6.0, ((0, 8),)),
        "null_embed": normal_values(arg_keys[2], (TEXT_LEN, D), 1.0, 6.0),
        "text_lengths": draw_text_lengths(jax.random.fold_in(arg_keys[17], 71), 0),
        "timesteps": draw_timesteps(jax.random.fold_in(arg_keys[17], 71), 0),
        "head_mod": normal_values(arg_keys[5], (STEPS, 2, D), 0.5, 3.0, (), jnp.float32),
        "cross_gain": jnp.clip(1.0 + 0.18 * jax.random.normal(arg_keys[6], (D,), jnp.float32), 0.1, 1.9),
        "cross_bias": normal_values(arg_keys[7], (D,), 0.5, 3.0, (), jnp.float32),
        "q_gain": jnp.clip(1.0 + 0.18 * jax.random.normal(arg_keys[8], (D,), jnp.float32), 0.1, 1.9),
        "k_gain": jnp.clip(1.0 + 0.18 * jax.random.normal(arg_keys[9], (D,), jnp.float32), 0.1, 1.9),
        "w_query": normal_values(arg_keys[10], (D, D), D ** -0.5, 0.15625, ((1, 32),)),
        "w_key": normal_values(arg_keys[11], (D, D), D ** -0.5, 0.15625, ((1, 32),)),
        "w_value": normal_values(arg_keys[12], (D, D), D ** -0.5, 0.15625, ((1, 32),)),
        "w_out": normal_values(arg_keys[13], (D, D), D ** -0.5, 0.15625, ((1, 32),)),
        "w_head": normal_values(arg_keys[14], (D, PATCH), D ** -0.5, 0.15625),
        "head_bias": normal_values(arg_keys[15], (PATCH,), 0.5, 3.0, (), jnp.float32),
        "target": normal_values(arg_keys[16], (CLIPS, TOKENS, PATCH), 1.0, 6.0, ((0, 8), (1, 32))),
    }


GUIDE_SCALE = 5.0
NORM_EPS = 1e-06

def layer_norm(values):
    row_mean = lax.optimization_barrier(jnp.mean(values, axis=-1, keepdims=True))
    centred = values - row_mean
    inverse = lax.rsqrt(lax.optimization_barrier(jnp.mean(centred * centred, axis=-1, keepdims=True)) + NORM_EPS)
    return (centred * inverse, inverse)

def rms_scale(values):
    return lax.rsqrt(lax.optimization_barrier(jnp.mean(values * values, axis=-1, keepdims=True)) + NORM_EPS)

def attend(query_normed, key_normed, value_rows, length):
    row_count = query_normed.shape[0]
    text_rows = key_normed.shape[0]
    head_size = query_normed.shape[1] // HEADS
    query_heads = query_normed.astype(jnp.float32).reshape(row_count, HEADS, head_size)
    key_heads = key_normed.astype(jnp.float32).reshape(text_rows, HEADS, head_size)
    value_heads = value_rows.astype(jnp.float32).reshape(text_rows, HEADS, head_size)
    scores = jnp.einsum('thd,lhd->htl', query_heads, key_heads) / math.sqrt(head_size)
    visible = jnp.arange(text_rows, dtype=jnp.int32) < length
    masked = jnp.where(visible, scores, -1e+30)
    row_max = lax.optimization_barrier(jnp.max(masked, axis=-1, keepdims=True))
    exp_terms = jnp.where(visible, jnp.exp(masked - row_max), 0.0)
    attn_weights = exp_terms / lax.optimization_barrier(jnp.sum(exp_terms, axis=-1, keepdims=True))
    weights_half = attn_weights.astype(jnp.bfloat16).astype(jnp.float32)
    attended = jnp.einsum('htl,lhd->thd', weights_half, value_heads)
    return (attn_weights, attended.reshape(row_count, HEADS * head_size).astype(jnp.bfloat16))

def branch_forward(latent_rows, context, length, mod_shift, mod_scale, cross_gain, cross_bias, q_gain, k_gain, w_query, w_key, w_value, w_out, w_head, head_bias):
    key_raw = jnp.dot(context, w_key, preferred_element_type=jnp.float32).astype(jnp.bfloat16)
    value_rows = jnp.dot(context, w_value, preferred_element_type=jnp.float32).astype(jnp.bfloat16)
    key_float = key_raw.astype(jnp.float32)
    key_inverse = rms_scale(key_float)
    key_unit = key_float * key_inverse
    key_normed = (key_unit * k_gain).astype(jnp.bfloat16)
    normed_unit, ignored = layer_norm(latent_rows.astype(jnp.float32))
    cross_in = (normed_unit * cross_gain + cross_bias).astype(jnp.bfloat16)
    query_raw = jnp.dot(cross_in, w_query, preferred_element_type=jnp.float32)
    query_normed = (query_raw * rms_scale(query_raw) * q_gain).astype(jnp.bfloat16)
    attn_weights, attended = attend(query_normed, key_normed, value_rows, length)
    after = latent_rows.astype(jnp.float32) + jnp.dot(attended, w_out, preferred_element_type=jnp.float32)
    head_unit, head_inverse = layer_norm(after)
    head_in = (head_unit * (1.0 + mod_scale) + mod_shift).astype(jnp.bfloat16)
    noise_pred = jnp.dot(head_in, w_head, preferred_element_type=jnp.float32) + head_bias
    saved = (query_normed, key_inverse, key_unit, value_rows, attn_weights, head_unit, head_inverse)
    return (noise_pred, saved)

def branch_backward(d_noise, saved, mod_scale, k_gain, w_key, w_value, w_out, w_head):
    query_normed, key_inverse, key_unit, value_rows, attn_weights, head_unit, head_inverse = saved
    row_count = query_normed.shape[0]
    text_rows = value_rows.shape[0]
    head_size = query_normed.shape[1] // HEADS
    d_head = jnp.dot(d_noise, w_head.T, preferred_element_type=jnp.float32)
    d_unit = d_head * (1.0 + mod_scale)
    d_after = head_inverse * (d_unit - lax.optimization_barrier(jnp.mean(d_unit, axis=-1, keepdims=True)) - head_unit * lax.optimization_barrier(jnp.mean(d_unit * head_unit, axis=-1, keepdims=True)))
    d_after = d_after.astype(jnp.bfloat16)
    d_attended = jnp.dot(d_after, w_out.T, preferred_element_type=jnp.float32).astype(jnp.bfloat16)
    d_heads = d_attended.astype(jnp.float32).reshape(row_count, HEADS, head_size)
    value_heads = value_rows.astype(jnp.float32).reshape(text_rows, HEADS, head_size)
    query_heads = query_normed.astype(jnp.float32).reshape(row_count, HEADS, head_size)
    d_weights = jnp.einsum('thd,lhd->htl', d_heads, value_heads)
    d_scores = attn_weights * (d_weights - lax.optimization_barrier(jnp.sum(d_weights * attn_weights, axis=-1, keepdims=True)))
    d_scores = (d_scores / math.sqrt(head_size)).astype(jnp.bfloat16).astype(jnp.float32)
    weights_half = attn_weights.astype(jnp.bfloat16).astype(jnp.float32)
    d_keys = jnp.einsum('htl,thd->lhd', d_scores, query_heads).reshape(text_rows, HEADS * head_size)
    d_values = jnp.einsum('htl,thd->lhd', weights_half, d_heads).reshape(text_rows, HEADS * head_size)
    gained = d_keys * k_gain
    statistic = lax.optimization_barrier(jnp.mean(gained * key_unit, axis=-1, keepdims=True))
    d_key_raw = key_inverse * (gained - key_unit * statistic)
    return jnp.dot(d_key_raw, w_key.astype(jnp.float32).T, precision=lax.Precision.HIGHEST) + jnp.dot(d_values, w_value.astype(jnp.float32).T, precision=lax.Precision.HIGHEST)

def reference(latents, prompt, null_embed, text_lengths, timesteps, head_mod, cross_gain, cross_bias, q_gain, k_gain, w_query, w_key, w_value, w_out, w_head, head_bias, target):

    def one_clip(inputs):
        latent_pair, prompt_clip, length, step_index, target_clip = inputs
        mod_shift = head_mod[step_index, 0]
        mod_scale = head_mod[step_index, 1]
        contexts = (prompt_clip, null_embed)
        lengths = (length, jnp.int32(TEXT_LEN))
        noises = []
        saveds = []
        for branch in range(2):
            noise_pred, saved = branch_forward(latent_pair[branch], contexts[branch], lengths[branch], mod_shift, mod_scale, cross_gain, cross_bias, q_gain, k_gain, w_query, w_key, w_value, w_out, w_head, head_bias)
            noises.append(noise_pred)
            saveds.append(saved)
        guided = noises[1] + GUIDE_SCALE * (noises[0] - noises[1])
        resid = guided - target_clip.astype(jnp.float32)
        grads = []
        for branch, factor in ((0, GUIDE_SCALE), (1, 1.0 - GUIDE_SCALE)):
            d_noise = (factor * resid).astype(jnp.bfloat16)
            grads.append(branch_backward(d_noise, saveds[branch], mod_scale, k_gain, w_key, w_value, w_out, w_head))
        return (guided, grads[0], grads[1])
    guided, cond_grads, null_grads = lax.map(one_clip, (latents, prompt, text_lengths, timesteps, target))
    null_mean = lax.optimization_barrier(jnp.sum(null_grads, axis=0)) / CLIPS
    embed_grad = jnp.stack([cond_grads, jnp.broadcast_to(null_mean, cond_grads.shape)], axis=1)
    return (guided, embed_grad)
```

```python
import functools
import math

import jax
import jax.numpy as jnp
from jax import lax
from jax.experimental import pallas as pl
from jax.experimental.pallas import tpu as pltpu
from jax.sharding import PartitionSpec as P

LANES = 128
GUIDE_SCALE = 5.0
NORM_EPS = 1e-06
GROUP = 4
MESH = pl.DeviceIdType.MESH
F32 = jnp.float32
BF16 = jnp.bfloat16
QUERY, OUT, KEY, VALUE = range(4)


class Place:
    def __init__(self):
        seq = lax.axis_index("seq")
        self.nz = lax.axis_size("clip")
        self.ny = lax.axis_size("seq") // 4
        self.z = lax.axis_index("clip")
        self.xl = lax.axis_index("guide")
        self.y = lax.div(seq, 4)
        self.xh = lax.rem(lax.div(seq, 2), 2)
        self.c = lax.rem(seq, 2)
        self.x = self.xh * 2 + self.xl

    def device(self, z=None, y=None, xh=None, xl=None, c=None):
        z = self.z if z is None else z
        y = self.y if y is None else y
        xh = self.xh if xh is None else xh
        xl = self.xl if xl is None else xl
        c = self.c if c is None else c
        return {"clip": z, "guide": xl, "seq": y * 4 + xh * 2 + c}

    def up_y(self, by):
        return lax.rem(self.y + (by + self.ny), self.ny)

    def up_z(self, by):
        return lax.rem(self.z + (by + self.nz), self.nz)

    def up_x(self, by):
        return lax.rem(self.x + (by + 4), 4)

    def at_y(self, by):
        return self.device(y=self.up_y(by))

    def at_z(self, by):
        return self.device(z=self.up_z(by))

    def at_x(self, by):
        x = self.up_x(by)
        return self.device(xh=lax.div(x, 2), xl=lax.rem(x, 2))

    def sibling(self):
        return self.device(c=1 - self.c)

    def other_columns(self):
        return self.device(xh=1 - self.xh, xl=1 - self.xl)

    def other_tokens(self):
        return self.device(xh=1 - self.xh)

    def other_branch(self):
        return self.device(xl=1 - self.xl)


def remote(src, dst, send_sem, recv_sem, device):
    return pltpu.make_async_remote_copy(
        src_ref=src,
        dst_ref=dst,
        send_sem=send_sem,
        recv_sem=recv_sem,
        device_id=device,
        device_id_type=MESH,
    )


def reach(count):
    return {1: count // 2, -1: count - 1 - count // 2}


class RingY:
    def __init__(self, here, base, partner, recv, send):
        self.here, self.base, self.partner, self.recv, self.send = here, base, partner, recv, send
        hops = reach(here.ny)
        self.hops = {(d, o): hops[d if o == 0 else -d] for d in (1, -1) for o in (0, 1)}
        self.rounds = here.ny // 2

    def chunk(self, y, xh, c):
        return self.base.at[y, xh, c]

    def copy(self, y, xh, c, lane, device):
        ref = self.chunk(y, xh, c)
        return remote(ref, ref, self.send.at[lane], self.recv.at[y * 4 + xh * 2 + c], device)

    def pass_on(self, y, other, step):
        here = self.here
        xh = here.xh if other == 0 else 1 - here.xh
        for d in (1, -1):
            if step == 0 and self.hops[d, other] > 0:
                self.copy(y, xh, here.c, 0, here.at_y(d)).start()
        self.copy(y, xh, here.c, 1, here.sibling()).start()

    def start(self):
        here = self.here
        self.copy(here.y, here.xh, here.c, 2, self.partner).start()
        self.pass_on(here.y, 0, 0)

    def over_x(self):
        here = self.here
        self.copy(here.y, 1 - here.xh, here.c, 2, self.partner).wait_recv()
        self.pass_on(here.y, 1, 0)

    def round(self, k):
        here = self.here
        for other in (0, 1):
            xh = here.xh if other == 0 else 1 - here.xh
            for d in (1, -1):
                if k <= self.hops[d, other]:
                    y = here.up_y(-d * k)
                    self.copy(y, xh, here.c, 0, here.at_y(d)).wait_recv()
                    if k < self.hops[d, other]:
                        self.copy(y, xh, here.c, 0, here.at_y(d)).start()
                    self.copy(y, xh, here.c, 1, here.sibling()).start()

    def from_sibling(self, y):
        here = self.here
        for xh in (0, 1):
            self.copy(y, xh, 1 - here.c, 1, here.sibling()).wait_recv()

    def finish(self):
        here = self.here
        for lane, ref in (
            (0, self.base.at[pl.ds(0, here.ny - 1), :, here.c]),
            (1, self.base.at[:, :, here.c]),
            (2, self.chunk(here.y, here.xh, here.c)),
        ):
            remote(ref, ref, self.send.at[lane], self.recv.at[0], here.sibling()).wait_send()


class RingZ:
    def __init__(self, here, base, first, recv, send):
        self.here, self.base, self.first, self.recv, self.send = here, base, first, recv, send
        self.hops = reach(here.ny)
        hops = reach(here.nz)
        self.z_hops = {(d, h): hops[d if h == 0 else -d] for d in (1, -1) for h in (0, 1)}
        self.rounds = here.ny // 2
        self.z_rounds = here.nz // 2

    def tile(self, z):
        return pl.ds(pl.multiple_of(self.first + z * LANES, LANES), LANES)

    def over(self, xh):
        here = self.here
        ref = self.base.at[here.y, xh, here.c, :, self.tile(here.z)]
        return remote(ref, ref, self.send.at[0], self.recv.at[0], here.other_columns())

    def along(self, y, d):
        here = self.here
        ref = self.base.at[y, :, here.c, :, self.tile(here.z)]
        return remote(ref, ref, self.send.at[1], self.recv.at[1 + y], here.at_y(d))

    def half(self, z, h, c, lane, device):
        size = self.here.ny // 2
        ref = self.base.at[pl.ds(h * size, size), :, c, :, self.tile(z)]
        start = 1 + self.here.ny + (lane - 2) * 2 * self.here.nz
        return remote(ref, ref, self.send.at[lane], self.recv.at[start + z * 2 + h], device)

    def start(self):
        self.over(self.here.xh).start()

    def over_x(self):
        self.over(1 - self.here.xh).wait_recv()
        for d in (1, -1):
            if self.hops[d] > 0:
                self.along(self.here.y, d).start()

    def round(self, k):
        for d in (1, -1):
            if k <= self.hops[d]:
                y = self.here.up_y(-d * k)
                self.along(y, d).wait_recv()
                if k < self.hops[d]:
                    self.along(y, d).start()

    def start_z(self):
        here = self.here
        for h in (0, 1):
            for d in (1, -1):
                if self.z_hops[d, h] > 0:
                    self.half(here.z, h, here.c, 2, here.at_z(d)).start()
        for h in (0, 1):
            self.half(here.z, h, here.c, 3, here.sibling()).start()

    def z_round(self, k):
        here = self.here
        for h in (0, 1):
            for d in (1, -1):
                if k <= self.z_hops[d, h]:
                    z = here.up_z(-d * k)
                    self.half(z, h, here.c, 2, here.at_z(d)).wait_recv()
                    if k < self.z_hops[d, h]:
                        self.half(z, h, here.c, 2, here.at_z(d)).start()
                    self.half(z, h, here.c, 3, here.sibling()).start()

    def from_sibling(self):
        here = self.here
        for z in range(here.nz):
            for h in (0, 1):
                self.half(z, h, 1 - here.c, 3, here.sibling()).wait_recv()

    def finish(self):
        here = self.here
        tiles = here.nz * LANES
        for lane, ref in (
            (0, self.base.at[here.y, here.xh, here.c, :, self.tile(here.z)]),
            (1, self.base.at[pl.ds(0, here.ny - 1), :, here.c, :, self.tile(here.z)]),
            (2, self.base.at[:, :, here.c, :, pl.ds(0, tiles - LANES)]),
            (3, self.base.at[:, :, here.c, :, pl.ds(0, tiles)]),
        ):
            remote(ref, ref, self.send.at[lane], self.recv.at[0], here.sibling()).wait_send()


class RingX:
    def __init__(self, here, base, first, width, recv, send):
        self.here, self.base, self.first, self.width = here, base, first, width
        self.recv, self.send = recv, send
        self.hops = reach(here.ny)
        self.rounds = here.ny // 2

    def part(self, xl):
        return pl.ds(pl.multiple_of(self.first + xl * self.width, LANES), self.width)

    def along(self, y, d):
        here = self.here
        ref = self.base.at[y, here.xh, here.c, :, self.part(here.xl)]
        return remote(ref, ref, self.send.at[0], self.recv.at[y], here.at_y(d))

    def half(self, x, h, c, lane, device):
        size = self.here.ny // 2
        ref = self.base.at[pl.ds(h * size, size), lax.div(x, 2), c, :, self.part(lax.rem(x, 2))]
        start = self.here.ny + (lane - 1) * 8
        return remote(ref, ref, self.send.at[lane], self.recv.at[start + x * 2 + h], device)

    def start(self):
        for d in (1, -1):
            if self.hops[d] > 0:
                self.along(self.here.y, d).start()

    def round(self, k):
        for d in (1, -1):
            if k <= self.hops[d]:
                y = self.here.up_y(-d * k)
                self.along(y, d).wait_recv()
                if k < self.hops[d]:
                    self.along(y, d).start()

    def start_x(self):
        here = self.here
        for h, d in ((0, 1), (1, -1), (1, 1), (0, -1)):
            self.half(here.x, h, here.c, 1, here.at_x(d)).start()
        for h in (0, 1):
            self.half(here.x, h, here.c, 2, here.sibling()).start()

    def x_round(self, k):
        here = self.here
        if k == 1:
            came = ((0, 1, True), (1, -1, True), (1, 1, False), (0, -1, False))
        else:
            came = ((0, 2, False), (1, -2, False))
        for h, d, further in came:
            x = here.up_x(-d)
            toward = here.at_x(1 if d > 0 else -1)
            self.half(x, h, here.c, 1, toward).wait_recv()
            if further:
                self.half(x, h, here.c, 1, toward).start()
            self.half(x, h, here.c, 2, here.sibling()).start()

    def from_sibling(self):
        here = self.here
        for x in range(4):
            for h in (0, 1):
                self.half(jnp.int32(x), h, 1 - here.c, 2, here.sibling()).wait_recv()

    def finish(self):
        here = self.here
        for lane, ref in (
            (0, self.base.at[pl.ds(0, here.ny - 1), 0, here.c, :, pl.ds(0, self.width)]),
            (1, self.base.at[:, 0, here.c, :, pl.ds(0, 3 * self.width)]),
            (2, self.base.at[:, 0, here.c, :, pl.ds(0, 4 * self.width)]),
        ):
            remote(ref, ref, self.send.at[lane], self.recv.at[0], here.sibling()).wait_send()


def down(values):
    return jnp.sum(values, axis=0, keepdims=True)


def dot(left, right):
    return jnp.dot(left, right, preferred_element_type=F32)


def dot_lanes(left, right):
    return lax.dot_general(left, right, (((1,), (1,)), ((), ())), preferred_element_type=F32)


def rows_of(index, size):
    return pl.ds(pl.multiple_of(index * size, size), size)


def kernel(
    length_ref,
    step_ref,
    latents,
    prompt,
    null_embed,
    head_mod,
    cross_gain,
    cross_bias,
    q_gain,
    k_gain,
    w_query,
    w_key,
    w_value,
    w_out,
    w_head,
    head_bias,
    target,
    guided_ref,
    grad_ref,
    weights,
    text,
    context,
    columns,
    w_head_rows,
    tokens,
    cross_in,
    query_raw,
    query,
    key_normed,
    value_rows,
    key_raw,
    attn,
    attended,
    after,
    head_in,
    d_unit,
    d_after,
    d_attended,
    noise,
    d_text,
    d_sibling,
    y_send,
    y_recv,
    x_send,
    x_recv,
    pick,
    core_send,
    core_recv,
    z_send,
    z_recv,
    text_recv,
    text_send,
    query_recv,
    query_send,
    out_z_recv,
    out_z_send,
    out_x_recv,
    out_x_send,
    key_recv,
    key_send,
    value_z_recv,
    value_z_send,
    value_x_recv,
    value_x_send,
    swap_sem,
    sibling_sem,
    y_sem,
    tail_sem,
):
    here = Place()
    ny, nz = here.ny, here.nz
    rows, width = w_query.shape
    token_count = latents.shape[0]
    text_rows = prompt.shape[0]
    heads = width // LANES
    blocks = width // LANES
    token_blocks = token_count // LANES
    band = 4 * rows
    root = 1.0 / math.sqrt(LANES)

    partners = [here.sibling(), here.other_columns(), here.other_tokens(), here.other_branch()]
    partners += [here.at_y(d) for d in range(1, ny)] + [here.at_z(d) for d in range(1, nz)]
    barrier = pltpu.get_barrier_semaphore()
    for device in partners:
        pl.semaphore_signal(barrier, inc=1, device_id=device, device_id_type=MESH)
    z_lanes = nz * LANES
    part = (width - z_lanes) // 2
    for index, own in ((QUERY, w_query), (KEY, w_key)):
        weights[index, here.y, here.xh, here.c] = own[...]
    for index, own in ((OUT, w_out), (VALUE, w_value)):
        for lanes in (
            rows_of(here.z, LANES),
            pl.ds(pl.multiple_of(z_lanes + here.xl * part, LANES), part),
        ):
            weights[index, here.y, here.xh, here.c, :, lanes] = own[:, lanes]
    pl.semaphore_wait(barrier, len(partners))

    text_ring = RingY(here, text, here.other_tokens(), text_recv, text_send)
    query_ring = RingY(here, weights.at[QUERY], here.other_columns(), query_recv, query_send)
    out_z = RingZ(here, weights.at[OUT], 0, out_z_recv, out_z_send)
    out_x = RingX(here, weights.at[OUT], z_lanes, part, out_x_recv, out_x_send)
    key_ring = RingY(here, weights.at[KEY], here.other_columns(), key_recv, key_send)
    value_z = RingZ(here, weights.at[VALUE], 0, value_z_recv, value_z_send)
    value_x = RingX(here, weights.at[VALUE], z_lanes, part, value_x_recv, value_x_send)
    half_y = ny // 2

    out_z.start()
    out_x.start()
    query_ring.start()

    @pl.when(here.xl == 0)
    def _():
        context[...] = prompt[...]

    @pl.when(here.xl == 1)
    def _():
        context[...] = null_embed[...]

    text[here.y, here.xh, here.c, :rows] = dot_lanes(w_key[...], context[...]).astype(BF16)
    text[here.y, here.xh, here.c, rows:] = dot_lanes(w_value[...], context[...]).astype(BF16)
    text_ring.start()
    out_z.over_x()

    modulation = head_mod[step_ref[0]]
    stack = jnp.concatenate(
        [
            cross_gain[...],
            cross_bias[...],
            q_gain[...],
            k_gain[...],
            1.0 + modulation[1:2],
            modulation[0:1],
            jnp.zeros((LANES - 6, width), F32),
        ],
        axis=0,
    )
    for block in range(blocks):
        lanes = slice(block * LANES, (block + 1) * LANES)
        columns[lanes, :] = stack[:, lanes].T
        w_head_rows[lanes, :] = w_head[:, lanes].T

    def turn(block, total):
        at = rows_of(block, LANES)
        for t in range(token_blocks):
            lanes = slice(t * LANES, (t + 1) * LANES)
            tokens[at, lanes] = latents[lanes, at].T
        return total + down(tokens[at, :].astype(F32))

    zero_row = jnp.zeros((1, token_count), F32)
    mean = lax.fori_loop(0, blocks, turn, zero_row) / width

    text_ring.over_x()
    query_ring.over_x()
    out_x.round(1)
    out_z.round(1)

    def spread(block, total):
        centred = tokens[rows_of(block, LANES), :].astype(F32) - mean
        return total + down(centred * centred)

    inverse = lax.rsqrt(lax.fori_loop(0, blocks, spread, zero_row) / width + NORM_EPS)

    def normalise(block, carry):
        at = rows_of(block, LANES)
        unit = (tokens[at, :].astype(F32) - mean) * inverse
        cross_in[at, :] = (unit * columns[at, 0:1] + columns[at, 1:2]).astype(BF16)
        return carry

    lax.fori_loop(0, blocks, normalise, 0)

    def project(y, total):
        raw = dot(weights[QUERY, y].reshape(band, width), cross_in[...])
        query_raw[pl.ds(pl.multiple_of(y * band, 64 if band % 64 == 0 else 16), band), :] = raw
        return total + down(raw * raw)

    def project_round(k, total):
        for d in (1, -1) if 2 * k < ny else (1,):
            query_ring.from_sibling(here.up_y(-d * k))
            total = project(here.up_y(-d * k), total)
        return total

    square = zero_row
    for k in range(1, half_y + 1):
        text_ring.round(k)
        if k > 1:
            out_x.round(k)
            out_z.round(k)
        if k == half_y:
            out_x.start_x()
            out_z.start_z()
        if k == 1:
            query_ring.from_sibling(here.y)
            square = project(here.y, square)
        else:
            square = project_round(k - 1, square)
        query_ring.round(k)
    for y in range(ny):
        text_ring.from_sibling(y)

    def text_block(block):
        per = []
        for start in (0, rows):
            per.append(text[:, :, :, start : start + rows, :].reshape(width, text_rows))
        return per

    keys, values = text_block(0)
    keys = keys.astype(F32)
    key_inverse = lax.rsqrt(down(keys * keys) / width + NORM_EPS)
    for h in range(heads):
        lanes = slice(h * LANES, (h + 1) * LANES)
        one = keys[lanes]
        key_raw[:, lanes] = one.T.astype(BF16)
        key_normed[h] = (one * key_inverse * columns[lanes, 3:4]).T.astype(BF16)
        value_rows[h] = values[lanes].astype(F32).T.astype(BF16)
    value_columns = values

    out_x.x_round(1)
    square = project_round(half_y, square)
    key_ring.start()
    value_z.start()
    value_x.start()
    query_inverse = lax.rsqrt(square / width + NORM_EPS)

    length = here.xl * text_rows + (1 - here.xl) * length_ref[0]
    visible = lax.broadcasted_iota(jnp.int32, (text_rows, token_count), 0) < length

    def attend(h, carry):
        at = rows_of(h, LANES)
        query[at, :] = (query_raw[at, :] * query_inverse * columns[at, 2:3]).astype(BF16)
        scores = dot(key_normed[h], query[at, :]) * root
        masked = jnp.where(visible, scores, -1e30)
        terms = jnp.where(visible, jnp.exp(masked - jnp.max(masked, axis=0, keepdims=True)), 0.0)
        shares = terms / down(terms)
        attn[h] = shares
        attended[at, :] = lax.dot_general(
            value_rows[h],
            shares.astype(BF16),
            (((0,), (0,)), ((), ())),
            preferred_element_type=F32,
        ).astype(BF16)
        return carry

    z_done, x_done = 0, 1
    step = GROUP
    for first in range(0, heads, step):
        lax.fori_loop(first, first + step, attend, 0)
        if z_done < out_z.z_rounds:
            z_done += 1
            out_z.z_round(z_done)
        if x_done < 2:
            x_done += 1
            out_x.x_round(x_done)
        if first == 0:
            key_ring.over_x()
            value_z.over_x()
    while z_done < out_z.z_rounds:
        z_done += 1
        out_z.z_round(z_done)
    value_x.round(1)
    value_z.round(1)
    out_x.from_sibling()
    out_z.from_sibling()

    def project_out(y, total):
        at = pl.ds(pl.multiple_of(y * band, 64 if band % 64 == 0 else 16), band)
        rows_after = dot(weights[OUT, y].reshape(band, width), attended[...]) + tokens[at, :].astype(F32)
        after[at, :] = rows_after
        return total + down(rows_after)

    total = lax.fori_loop(0, half_y, project_out, zero_row)
    key_ring.round(1)
    if half_y > 1:
        value_x.round(2)
        value_z.round(2)
    total = lax.fori_loop(half_y, ny, project_out, total)
    head_mean = total / width

    def head_spread(block, total):
        centred = after[rows_of(block, LANES), :] - head_mean
        return total + down(centred * centred)

    head_inverse = lax.rsqrt(lax.fori_loop(0, blocks, head_spread, zero_row) / width + NORM_EPS)

    def modulate(block, carry):
        at = rows_of(block, LANES)
        unit = (after[at, :] - head_mean) * head_inverse
        head_in[at, :] = (unit * columns[at, 4:5] + columns[at, 5:6]).astype(BF16)
        return carry

    lax.fori_loop(0, blocks, modulate, 0)
    noise[here.xl] = dot(w_head[...], head_in[...]) + head_bias[...]
    swap = remote(
        noise.at[here.xl], noise.at[here.xl], swap_sem.at[0], swap_sem.at[1], here.other_branch()
    )
    swap.start()
    for k in range(3, half_y + 1):
        value_x.round(k)
        value_z.round(k)
    value_x.start_x()
    value_z.start_z()
    if half_y > 1:
        key_ring.round(2)
    swap_back = remote(
        noise.at[1 - here.xl],
        noise.at[1 - here.xl],
        swap_sem.at[0],
        swap_sem.at[1],
        here.other_branch(),
    )
    swap_back.wait_recv()
    swap.wait_send()
    guided = noise[1] + GUIDE_SCALE * (noise[0] - noise[1])
    guided_ref[...] = guided
    factor = GUIDE_SCALE - (2.0 * GUIDE_SCALE - 1.0) * here.xl.astype(F32)
    d_noise = (factor * (guided - target[...].astype(F32))).astype(BF16)

    def head_back(block, sums):
        at = rows_of(block, LANES)
        unit = (after[at, :] - head_mean) * head_inverse
        part_unit = dot(w_head_rows[at, :], d_noise) * columns[at, 4:5]
        d_unit[at, :] = part_unit
        return (sums[0] + down(part_unit), sums[1] + down(part_unit * unit))

    first_sum, second_sum = lax.fori_loop(0, blocks, head_back, (zero_row, zero_row))
    first_mean, second_mean = first_sum / width, second_sum / width

    def norm_back(block, carry):
        at = rows_of(block, LANES)
        unit = (after[at, :] - head_mean) * head_inverse
        grads = (head_inverse * (d_unit[at, :] - first_mean - unit * second_mean)).astype(BF16)
        for t in range(token_blocks):
            lanes = slice(t * LANES, (t + 1) * LANES)
            d_after[lanes, at] = grads[:, lanes].T
        return carry

    lax.fori_loop(0, blocks, norm_back, 0)

    def out_back(block, carry):
        at = rows_of(block, 2 * LANES)
        matrix = weights[OUT, :, :, :, :, at].reshape(width, 2 * LANES)
        d_attended[:, at] = dot(d_after[...], matrix).astype(BF16)
        return carry

    lax.fori_loop(0, blocks // 2, out_back, 0)
    value_x.x_round(1)
    value_z.z_round(1)
    if half_y > 2:
        key_ring.round(3)

    def attend_back(h, carry):
        at = rows_of(h, LANES)
        grads = d_attended[:, at]
        shares = attn[h]
        d_shares = dot_lanes(value_rows[h], grads)
        d_scores = shares * (d_shares - down(d_shares * shares))
        d_text[0, :, at] = dot_lanes((d_scores * root).astype(BF16), query[at, :])
        d_text[1, :, at] = dot(shares.astype(BF16), grads)
        return carry

    groups = heads // GROUP
    wide = GROUP * LANES

    def to_sibling(g):
        lanes = slice(g * wide, (g + 1) * wide)
        return remote(
            d_text.at[1 - here.c, :, lanes],
            d_sibling.at[:, lanes],
            sibling_sem.at[0, g],
            sibling_sem.at[1, g],
            here.sibling(),
        )

    def to_row(g, d):
        lanes = slice(g * wide, (g + 1) * wide)
        return remote(
            y_send.at[here.up_y(d), :, lanes],
            y_recv.at[here.y, :, lanes],
            y_sem.at[0, g],
            y_sem.at[1, g],
            here.at_y(d),
        )

    def sum_cores(g):
        lanes = slice(g * wide, (g + 1) * wide)
        to_sibling(g).wait_recv()
        both = d_text[here.c, :, lanes] + d_sibling[:, lanes]
        d_text[here.c, :, lanes] = both
        y_send[:, :, lanes] = both.astype(BF16).reshape(ny, text_rows // ny, wide)
        for d in range(1, ny):
            to_row(g, d).start()

    for g in range(groups):
        lax.fori_loop(g * GROUP, (g + 1) * GROUP, attend_back, 0)
        to_sibling(g).start()
        if g > 0:
            sum_cores(g - 1)
        if g + 2 <= value_z.z_rounds:
            value_z.z_round(g + 2)
        if g == 0:
            value_x.x_round(2)
    sum_cores(groups - 1)
    for k in range(groups + 2, value_z.z_rounds + 1):
        value_z.z_round(k)
    if half_y > 3:
        key_ring.round(4)

    for g in range(groups):
        lanes = slice(g * wide, (g + 1) * wide)
        ref = y_recv.at[pl.ds(0, ny - 1), :, lanes]
        remote(ref, ref, y_sem.at[0, g], y_sem.at[1, g], here.sibling()).wait_recv()
    share = text_rows // ny
    summed = d_text[here.c, pl.ds(pl.multiple_of(here.y * share, share), share), :]
    for d in range(1, ny):
        summed = summed + y_recv[here.up_y(d)].astype(F32)
    x_send[0] = summed[: share // 2]
    x_send[1] = summed[share // 2 :]
    cross = remote(
        x_send.at[1 - here.xh], x_recv, tail_sem.at[0], tail_sem.at[1], here.other_tokens()
    )
    cross.start()
    for y in range(ny):
        key_ring.from_sibling(y)
    value_x.from_sibling()
    value_z.from_sibling()

    near = key_raw[pl.ds(pl.multiple_of(here.y * share, share), share), :].astype(F32)
    pick[0] = near[: share // 2]
    pick[1] = near[share // 2 :]
    own_keys = pick[here.xh]
    own_inverse = lax.rsqrt(jnp.mean(own_keys * own_keys, axis=-1, keepdims=True) + NORM_EPS)
    own_unit = own_keys * own_inverse
    cross.wait_recv()
    own_sum = x_send[here.xh] + x_recv[...]
    gained = own_sum * k_gain[...]
    statistic = jnp.mean(gained * own_unit, axis=-1, keepdims=True)
    pick[0] = own_inverse * (gained - own_unit * statistic)
    pick[1] = own_sum
    left = pick[here.c]
    high = left.astype(BF16)
    low = (left - high.astype(F32)).astype(BF16)
    both = jnp.concatenate([high, low], axis=0)
    few = share // 2

    def text_back(block, carry):
        at = rows_of(block, 2 * LANES)
        matrix = weights[KEY + here.c, :, :, :, :, at].reshape(width, 2 * LANES)
        product = dot(both, matrix)
        pick[0, :, at] = product[:few] + product[few:]
        return carry

    lax.fori_loop(0, blocks // 2, text_back, 0)
    own_rows = few // 2
    middle = width // 2

    def fold(values):
        return jnp.concatenate([values[:, :middle], values[:, middle:]], axis=0)

    product = pick[0]
    core_send[0] = fold(product[:own_rows])
    core_send[1] = fold(product[own_rows:])
    cores = remote(
        core_send.at[1 - here.c], core_recv, tail_sem.at[2], tail_sem.at[3], here.sibling()
    )
    cores.start()
    cores.wait_recv()
    z_send[...] = core_send[here.c] + core_recv[...]

    def unfold(values):
        grad_ref[:, :middle] = values[:own_rows]
        grad_ref[:, middle:] = values[own_rows:]

    @pl.when(here.xl == 0)
    def _():
        unfold(z_send[...])

    @pl.when(here.xl == 1)
    def _():
        for d in range(1, nz):
            remote(
                z_send, z_recv.at[here.z], tail_sem.at[4], tail_sem.at[5], here.at_z(d)
            ).start()
        ref = z_recv.at[pl.ds(0, nz - 1)]
        gathered = remote(ref, ref, tail_sem.at[4], tail_sem.at[5], here.sibling())
        gathered.wait_recv()
        clips = z_send[...]
        for d in range(1, nz):
            clips = clips + z_recv[here.up_z(d)]
        unfold(clips / nz)
        gathered.wait_send()

    cores.wait_send()
    cross.wait_send()
    for g in range(groups):
        to_sibling(g).wait_send()
        lanes = slice(g * wide, (g + 1) * wide)
        ref = y_send.at[pl.ds(0, ny - 1), :, lanes]
        remote(ref, ref, y_sem.at[0, g], y_sem.at[1, g], here.sibling()).wait_send()
    for ring in (text_ring, query_ring, out_z, out_x, key_ring, value_z, value_x):
        ring.finish()


def on_device(
    latents,
    prompt,
    null_embed,
    text_lengths,
    timesteps,
    head_mod,
    cross_gain,
    cross_bias,
    q_gain,
    k_gain,
    w_query,
    w_key,
    w_value,
    w_out,
    w_head,
    head_bias,
    target,
):
    nz = lax.axis_size("clip")
    ny = lax.axis_size("seq") // 4
    tokens = latents[0, 0]
    count, width = tokens.shape
    text_rows = null_embed.shape[0]
    rows = w_query.shape[1]
    patch = w_head.shape[1]
    heads = width // LANES
    share = text_rows // ny
    own_rows = share // 4
    dma = pltpu.SemaphoreType.DMA
    vmem = pl.BlockSpec(memory_space=pltpu.VMEM)
    smem = pl.BlockSpec(memory_space=pltpu.SMEM)
    z_recvs = 1 + ny + 4 * nz
    x_recvs = ny + 16
    guided, grad = pl.pallas_call(
        kernel,
        out_shape=(
            jax.ShapeDtypeStruct((patch, count), F32),
            jax.ShapeDtypeStruct((own_rows, width), F32),
        ),
        in_specs=[smem, smem] + [vmem] * 15,
        out_specs=(vmem, vmem),
        scratch_shapes=[
            pltpu.VMEM((4, ny, 2, 2, rows, width), BF16),
            pltpu.VMEM((ny, 2, 2, 2 * rows, text_rows), BF16),
            pltpu.VMEM((text_rows, width), BF16),
            pltpu.VMEM((width, LANES), F32),
            pltpu.VMEM((width, patch), BF16),
            pltpu.VMEM((width, count), BF16),
            pltpu.VMEM((width, count), BF16),
            pltpu.VMEM((width, count), F32),
            pltpu.VMEM((width, count), BF16),
            pltpu.VMEM((heads, text_rows, LANES), BF16),
            pltpu.VMEM((heads, text_rows, LANES), BF16),
            pltpu.VMEM((text_rows, width), BF16),
            pltpu.VMEM((heads, text_rows, count), F32),
            pltpu.VMEM((width, count), BF16),
            pltpu.VMEM((width, count), F32),
            pltpu.VMEM((width, count), BF16),
            pltpu.VMEM((width, count), F32),
            pltpu.VMEM((count, width), BF16),
            pltpu.VMEM((count, width), BF16),
            pltpu.VMEM((2, patch, count), F32),
            pltpu.VMEM((2, text_rows, width), F32),
            pltpu.VMEM((text_rows, width), F32),
            pltpu.VMEM((ny, share, width), BF16),
            pltpu.VMEM((ny, share, width), BF16),
            pltpu.VMEM((2, share // 2, width), F32),
            pltpu.VMEM((share // 2, width), F32),
            pltpu.VMEM((2, share // 2, width), F32),
            pltpu.VMEM((2, 2 * own_rows, width // 2), F32),
            pltpu.VMEM((2 * own_rows, width // 2), F32),
            pltpu.VMEM((2 * own_rows, width // 2), F32),
            pltpu.VMEM((nz, 2 * own_rows, width // 2), F32),
            dma((4 * ny,)),
            dma((3,)),
            dma((4 * ny,)),
            dma((3,)),
            dma((z_recvs,)),
            dma((4,)),
            dma((x_recvs,)),
            dma((3,)),
            dma((4 * ny,)),
            dma((3,)),
            dma((z_recvs,)),
            dma((4,)),
            dma((x_recvs,)),
            dma((3,)),
            dma((2,)),
            dma((2, heads // GROUP)),
            dma((2, heads // GROUP)),
            dma((6,)),
        ],
        compiler_params=pltpu.CompilerParams(
            collective_id=0, has_side_effects=True, vmem_limit_bytes=60 * 1024 * 1024
        ),
        cost_estimate=pl.CostEstimate(
            flops=8 * count * width * width, bytes_accessed=8 * count * width, transcendentals=0
        ),
    )(
        text_lengths,
        timesteps,
        tokens,
        prompt[0],
        null_embed,
        head_mod,
        cross_gain.reshape(1, width),
        cross_bias.reshape(1, width),
        q_gain.reshape(1, width),
        k_gain.reshape(1, width),
        w_query.T,
        w_key.T,
        w_value.T,
        w_out.T,
        w_head.T,
        head_bias.reshape(patch, 1),
        target[0].T,
    )
    return (guided.T[None], grad.reshape(1, 1, own_rows, width))


def solution(mesh):
    return jax.shard_map(
        on_device,
        mesh=mesh,
        in_specs=(
            P("clip", "guide", "seq", None),
            P("clip", None, None),
            P(),
            P("clip"),
            P("clip"),
            P(),
            P(),
            P(),
            P(),
            P(),
            P(None, "seq"),
            P(None, "seq"),
            P(None, "seq"),
            P(None, "seq"),
            P(),
            P(),
            P("clip", "seq", None),
        ),
        out_specs=(P("clip", "seq", None), P("clip", "guide", "seq", None)),
        check_vma=False,
    )
```

```python
import functools
import math

import jax
import jax.numpy as jnp
from jax import lax
from jax.experimental import pallas as pl
from jax.experimental.pallas import tpu as pltpu
from jax.sharding import PartitionSpec as P

LANES = 128
GUIDE_SCALE = 5.0
NORM_EPS = 1e-06
COLOURS = 4
MESH = pl.DeviceIdType.MESH
F32 = jnp.float32
BF16 = jnp.bfloat16
QUERY, OUT = range(2)


class Place:
    def __init__(self):
        seq = lax.axis_index("seq")
        self.nz = lax.axis_size("clip")
        self.ny = lax.axis_size("seq") // 4
        self.z = lax.axis_index("clip")
        self.xl = lax.axis_index("guide")
        self.y = lax.div(seq, 4)
        self.xh = lax.rem(lax.div(seq, 2), 2)
        self.c = lax.rem(seq, 2)
        self.x = self.xh * 2 + self.xl

    def device(self, z=None, y=None, xh=None, xl=None, c=None):
        z = self.z if z is None else z
        y = self.y if y is None else y
        xh = self.xh if xh is None else xh
        xl = self.xl if xl is None else xl
        c = self.c if c is None else c
        return {"clip": z, "guide": xl, "seq": y * 4 + xh * 2 + c}

    def up_y(self, by):
        return lax.rem(self.y + (by + self.ny), self.ny)

    def up_z(self, by):
        return lax.rem(self.z + (by + self.nz), self.nz)

    def up_x(self, by):
        return lax.rem(self.x + (by + 4), 4)

    def at_y(self, by):
        return self.device(y=self.up_y(by))

    def at_z(self, by):
        return self.device(z=self.up_z(by))

    def at_x(self, by):
        x = self.up_x(by)
        return self.device(xh=lax.div(x, 2), xl=lax.rem(x, 2))

    def sibling(self):
        return self.device(c=1 - self.c)

    def other_columns(self):
        return self.device(xh=1 - self.xh, xl=1 - self.xl)

    def other_tokens(self):
        return self.device(xh=1 - self.xh)

    def other_branch(self):
        return self.device(xl=1 - self.xl)


def remote(src, dst, send_sem, recv_sem, device):
    return pltpu.make_async_remote_copy(
        src_ref=src,
        dst_ref=dst,
        send_sem=send_sem,
        recv_sem=recv_sem,
        device_id=device,
        device_id_type=MESH,
    )


def reach(count):
    return {1: count // 2, -1: count - 1 - count // 2}


class RingY:
    def __init__(self, here, base, lanes, partner, recv, send):
        self.here, self.base, self.lanes, self.partner = here, base, lanes, partner
        self.recv, self.send = recv, send
        hops = reach(here.ny)
        self.hops = {(d, o): hops[d if o == 0 else -d] for d in (1, -1) for o in (0, 1)}
        self.rounds = here.ny // 2

    def chunk(self, y, xh, c):
        return self.base.at[y, xh, c, :, self.lanes]

    def copy(self, y, xh, c, lane, device):
        ref = self.chunk(y, xh, c)
        return remote(ref, ref, self.send.at[lane], self.recv.at[y * 4 + xh * 2 + c], device)

    def pass_on(self, y, other, step):
        here = self.here
        xh = here.xh if other == 0 else 1 - here.xh
        for d in (1, -1):
            if step == 0 and self.hops[d, other] > 0:
                self.copy(y, xh, here.c, 0, here.at_y(d)).start()
        self.copy(y, xh, here.c, 1, here.sibling()).start()

    def start(self):
        here = self.here
        self.copy(here.y, here.xh, here.c, 2, self.partner).start()
        self.pass_on(here.y, 0, 0)

    def over_x(self):
        here = self.here
        self.copy(here.y, 1 - here.xh, here.c, 2, self.partner).wait_recv()
        self.pass_on(here.y, 1, 0)

    def round(self, k):
        here = self.here
        for other in (0, 1):
            xh = here.xh if other == 0 else 1 - here.xh
            for d in (1, -1):
                if k <= self.hops[d, other]:
                    y = here.up_y(-d * k)
                    self.copy(y, xh, here.c, 0, here.at_y(d)).wait_recv()
                    if k < self.hops[d, other]:
                        self.copy(y, xh, here.c, 0, here.at_y(d)).start()
                    self.copy(y, xh, here.c, 1, here.sibling()).start()

    def from_sibling(self, y):
        here = self.here
        for xh in (0, 1):
            self.copy(y, xh, 1 - here.c, 1, here.sibling()).wait_recv()

    def finish(self):
        here = self.here
        for lane, ref in (
            (0, self.base.at[pl.ds(0, here.ny - 1), :, here.c, :, self.lanes]),
            (1, self.base.at[:, :, here.c, :, self.lanes]),
            (2, self.chunk(here.y, here.xh, here.c)),
        ):
            remote(ref, ref, self.send.at[lane], self.recv.at[0], here.sibling()).wait_send()


class RingFour:
    def __init__(self, here, base, first, width, axis, recv, send):
        self.here, self.base, self.first, self.width, self.axis = here, base, first, width, axis
        self.recv, self.send = recv, send
        self.hops = reach(here.ny)
        self.colour = here.x if axis == "x" else lax.rem(here.z, COLOURS)

    def part(self, index):
        return pl.ds(pl.multiple_of(self.first + index * self.width, LANES), self.width)

    def toward(self, d):
        return self.here.at_x(d) if self.axis == "x" else self.here.at_z(d)

    def along(self, y, d):
        here = self.here
        if self.axis == "x":
            ref = self.base.at[y, here.xh, here.c, :, self.part(here.xl)]
        else:
            ref = self.base.at[y, :, here.c, :, self.part(self.colour)]
        return remote(ref, ref, self.send.at[0], self.recv.at[y], here.at_y(d))

    def over(self, xh):
        here = self.here
        ref = self.base.at[here.y, xh, here.c, :, self.part(self.colour)]
        return remote(ref, ref, self.send.at[3], self.recv.at[here.ny + 16], here.other_columns())

    def half(self, colour, h, c, lane, device):
        size = self.here.ny // 2
        span = pl.ds(h * size, size)
        if self.axis == "x":
            ref = self.base.at[span, lax.div(colour, 2), c, :, self.part(lax.rem(colour, 2))]
        else:
            ref = self.base.at[span, :, c, :, self.part(colour)]
        slot = self.here.ny + (lane - 1) * 8 + colour * 2 + h
        return remote(ref, ref, self.send.at[lane], self.recv.at[slot], device)

    def begin_y(self):
        for d in (1, -1):
            if self.hops[d] > 0:
                self.along(self.here.y, d).start()

    def start(self):
        if self.axis == "x":
            self.begin_y()
        else:
            self.over(self.here.xh).start()

    def over_x(self):
        if self.axis == "z":
            self.over(1 - self.here.xh).wait_recv()
            self.begin_y()

    def round(self, k):
        for d in (1, -1):
            if k <= self.hops[d]:
                y = self.here.up_y(-d * k)
                self.along(y, d).wait_recv()
                if k < self.hops[d]:
                    self.along(y, d).start()

    def begin_four(self):
        here = self.here
        for h, d in ((0, 1), (1, -1), (1, 1), (0, -1)):
            self.half(self.colour, h, here.c, 1, self.toward(d)).start()
        for h in (0, 1):
            self.half(self.colour, h, here.c, 2, here.sibling()).start()

    def four(self, k):
        here = self.here
        if k == 1:
            came = ((0, 1, True), (1, -1, True), (1, 1, False), (0, -1, False))
        else:
            came = ((0, 2, False), (1, -2, False))
        for h, d, further in came:
            colour = lax.rem(self.colour + (COLOURS - d), COLOURS)
            toward = self.toward(1 if d > 0 else -1)
            self.half(colour, h, here.c, 1, toward).wait_recv()
            if further:
                self.half(colour, h, here.c, 1, toward).start()
            self.half(colour, h, here.c, 2, here.sibling()).start()

    def from_sibling(self):
        here = self.here
        for colour in range(COLOURS):
            for h in (0, 1):
                self.half(jnp.int32(colour), h, 1 - here.c, 2, here.sibling()).wait_recv()

    def finish(self):
        here = self.here
        xh = 0 if self.axis == "x" else slice(None)
        ends = [
            (0, self.base.at[pl.ds(0, here.ny - 1), xh, here.c, :, pl.ds(0, self.width)]),
            (1, self.base.at[:, xh, here.c, :, pl.ds(0, 3 * self.width)]),
            (2, self.base.at[:, xh, here.c, :, pl.ds(0, 4 * self.width)]),
        ]
        if self.axis == "z":
            ends.append((3, self.base.at[0, 0, here.c, :, pl.ds(0, self.width)]))
        for lane, ref in ends:
            remote(ref, ref, self.send.at[lane], self.recv.at[0], here.sibling()).wait_send()


class Pair:
    def __init__(self, here, base, recv, send):
        self.here, self.base, self.recv, self.send = here, base, recv, send
        self.parity = lax.rem(here.y, 2)
        self.other_y = here.device(y=here.y + 1 - 2 * self.parity)

    def copy(self, parity, xh, c, lane, device):
        ref = self.base.at[:, parity, xh, c]
        slot = parity * 4 + xh * 2 + c
        return remote(ref, ref, self.send.at[lane], self.recv.at[slot], device)

    def start(self):
        here = self.here
        self.copy(self.parity, here.xh, here.c, 2, here.other_columns()).start()
        self.copy(self.parity, here.xh, here.c, 0, self.other_y).start()
        self.copy(self.parity, here.xh, here.c, 1, here.sibling()).start()

    def over_x(self):
        here = self.here
        self.copy(self.parity, 1 - here.xh, here.c, 2, here.other_columns()).wait_recv()
        self.copy(self.parity, 1 - here.xh, here.c, 0, self.other_y).start()
        self.copy(self.parity, 1 - here.xh, here.c, 1, here.sibling()).start()

    def over_y(self):
        here = self.here
        for xh in (here.xh, 1 - here.xh):
            self.copy(1 - self.parity, xh, here.c, 0, self.other_y).wait_recv()
            self.copy(1 - self.parity, xh, here.c, 1, here.sibling()).start()

    def from_sibling(self):
        here = self.here
        for parity in (0, 1):
            for xh in (0, 1):
                self.copy(parity, xh, 1 - here.c, 1, here.sibling()).wait_recv()

    def finish(self):
        here = self.here
        for lane, ref in (
            (0, self.base.at[:, 0, :, here.c]),
            (1, self.base.at[:, :, :, here.c]),
            (2, self.base.at[:, 0, 0, here.c]),
        ):
            remote(ref, ref, self.send.at[lane], self.recv.at[0], here.sibling()).wait_send()


def down(values):
    return jnp.sum(values, axis=0, keepdims=True)


def dot(left, right):
    return jnp.dot(left, right, preferred_element_type=F32)


def dot_lanes(left, right):
    return lax.dot_general(left, right, (((1,), (1,)), ((), ())), preferred_element_type=F32)


def rows_of(index, size):
    return pl.ds(pl.multiple_of(index * size, size), size)


def log2(count):
    return count.bit_length() - 1


def kernel(
    length_ref,
    step_ref,
    latents,
    prompt,
    null_embed,
    head_mod,
    vectors,
    w_query,
    w_key,
    w_value,
    w_out,
    w_head,
    target,
    guided_ref,
    grad_ref,
    weights,
    pair_weights,
    text,
    context,
    columns,
    w_head_rows,
    tokens,
    cross_in,
    query_raw,
    query,
    key_normed,
    value_rows,
    key_raw,
    attn,
    attended,
    after,
    head_in,
    d_unit,
    d_after,
    d_attended,
    noise,
    d_text,
    d_sibling,
    y_send,
    y_recv,
    x_send,
    x_recv,
    product,
    unit_send,
    unit_recv,
    grad_send,
    grad_recv,
    z_send,
    z_recv,
    text_recv,
    text_send,
    recv_y,
    send_y,
    recv_z,
    send_z,
    recv_x,
    send_x,
    pair_recv,
    pair_send,
    swap_sem,
    sibling_sem,
    y_recv_sem,
    y_send_sem,
    tail_sem,
):
    here = Place()
    ny, nz = here.ny, here.nz
    rows, width = w_query.shape
    token_count = latents.shape[0]
    text_rows = prompt.shape[0]
    patch = w_head.shape[0]
    heads = width // LANES
    blocks = width // LANES
    token_blocks = token_count // LANES
    band = 4 * rows
    root = 1.0 / math.sqrt(LANES)
    pairs = ny // 2
    share = text_rows // ny
    own_rows = share // 4
    half, quarter, eighth = text_rows // 2, text_rows // 4, text_rows // 8
    wide = width // pairs
    middle = width // 2
    parity = lax.rem(here.y, 2)
    pair = lax.div(here.y, 2)

    partners = [here.sibling(), here.other_columns(), here.other_tokens(), here.other_branch()]
    partners += [here.at_y(d) for d in range(1, ny)] + [here.at_z(d) for d in range(1, nz)]
    barrier = pltpu.get_barrier_semaphore()
    for device in partners:
        pl.semaphore_signal(barrier, inc=1, device_id=device, device_id_type=MESH)

    x_part = LANES * (2 if blocks >= 12 else 1)
    x_first = width - 2 * x_part
    z_first = x_first - COLOURS * LANES
    y_lanes = pl.ds(0, z_first)
    for index, own in ((QUERY, w_query), (OUT, w_out)):
        for lanes in (
            y_lanes,
            pl.ds(pl.multiple_of(z_first + lax.rem(here.z, COLOURS) * LANES, LANES), LANES),
            pl.ds(pl.multiple_of(x_first + here.xl * x_part, LANES), x_part),
        ):
            weights[index, here.y, here.xh, here.c, :, lanes] = own[:, lanes]
    for index, own in enumerate((w_key, w_value)):
        pair_weights[index, parity, here.xh, here.c] = own[...]
    pl.semaphore_wait(barrier, len(partners))

    text_ring = RingY(here, text, slice(None), here.other_tokens(), text_recv, text_send)
    rings = []
    for index in (QUERY, OUT):
        base = weights.at[index]
        rings.append(
            (
                RingFour(here, base, x_first, x_part, "x", recv_x.at[index], send_x.at[index]),
                RingFour(here, base, z_first, LANES, "z", recv_z.at[index], send_z.at[index]),
                RingY(
                    here, base, y_lanes, here.other_columns(), recv_y.at[index], send_y.at[index]
                ),
            )
        )
    key_value = Pair(here, pair_weights, pair_recv, pair_send)

    def begin(index):
        for ring in rings[index]:
            ring.start()

    def over_x(index):
        for ring in rings[index][1:]:
            ring.over_x()

    def go_round(index, k):
        for ring in rings[index][:2]:
            ring.round(k)
            if k == pairs:
                ring.begin_four()
        rings[index][2].round(k)

    def go_four(index, k):
        for ring in rings[index][:2]:
            ring.four(k)

    def all_here(index):
        for ring in rings[index][:2]:
            ring.from_sibling()
        for y in range(ny):
            rings[index][2].from_sibling(y)

    begin(QUERY)

    def text_row(index):
        place = lax.shift_right_logical(index, log2(own_rows)) & (pairs - 1)
        place = place * 2 + (lax.shift_right_logical(index, log2(quarter)) & 1)
        place = place * 2 + (lax.shift_right_logical(index, log2(eighth)) & 1)
        place = place * 2 + (lax.shift_right_logical(index, log2(half)) & 1)
        return place * own_rows + (index & (own_rows - 1))

    square_iota = functools.partial(lax.broadcasted_iota, jnp.int32, (text_rows, text_rows))
    order = jnp.where(text_row(square_iota(0)) == square_iota(1), 1.0, 0.0).astype(BF16)

    @pl.when(here.xl == 0)
    def _():
        context[...] = dot(order, prompt[...]).astype(BF16)

    @pl.when(here.xl == 1)
    def _():
        context[...] = dot(order, null_embed[...]).astype(BF16)

    text[here.y, here.xh, here.c, :rows] = dot_lanes(w_key[...], context[...]).astype(BF16)
    text[here.y, here.xh, here.c, rows:] = dot_lanes(w_value[...], context[...]).astype(BF16)
    text_ring.start()
    over_x(QUERY)

    modulation = head_mod[step_ref[0]]
    stack = jnp.concatenate(
        [
            vectors[...],
            1.0 + modulation[1:2],
            modulation[0:1],
            jnp.zeros((LANES - 10, width), F32),
        ],
        axis=0,
    )
    for block in range(blocks):
        lanes = slice(block * LANES, (block + 1) * LANES)
        columns[lanes, :] = stack[:, lanes].T
        w_head_rows[lanes, :] = w_head[:, lanes].T

    def turn(block, total):
        at = rows_of(block, LANES)
        for t in range(token_blocks):
            lanes = slice(t * LANES, (t + 1) * LANES)
            tokens[at, lanes] = latents[lanes, at].T
        return total + down(tokens[at, :].astype(F32))

    zero_row = jnp.zeros((1, token_count), F32)
    mean = lax.fori_loop(0, blocks, turn, zero_row) / width

    go_round(QUERY, 1)
    text_ring.over_x()
    begin(OUT)

    def spread(block, total):
        centred = tokens[rows_of(block, LANES), :].astype(F32) - mean
        return total + down(centred * centred)

    inverse = lax.rsqrt(lax.fori_loop(0, blocks, spread, zero_row) / width + NORM_EPS)

    def normalise(block, carry):
        at = rows_of(block, LANES)
        unit = (tokens[at, :].astype(F32) - mean) * inverse
        cross_in[at, :] = (unit * columns[at, 0:1] + columns[at, 1:2]).astype(BF16)
        return carry

    lax.fori_loop(0, blocks, normalise, 0)

    if pairs > 1:
        go_round(QUERY, 2)
    text_ring.round(1)
    over_x(OUT)
    for k in range(3, pairs + 1):
        go_round(QUERY, k)
        text_ring.round(k - 1)
        go_round(OUT, k - 2)
    go_four(QUERY, 1)
    if pairs > 1:
        text_ring.round(pairs)
    for k in range(max(1, pairs - 1), pairs):
        go_round(OUT, k)
    go_four(QUERY, 2)
    go_round(OUT, pairs)
    for y in range(ny):
        text_ring.from_sibling(y)

    keys = text[:, :, :, :rows, :].reshape(width, text_rows).astype(F32)
    values = text[:, :, :, rows:, :].reshape(width, text_rows).astype(F32)
    key_inverse = lax.rsqrt(down(keys * keys) / width + NORM_EPS)
    for h in range(heads):
        lanes = slice(h * LANES, (h + 1) * LANES)
        one = keys[lanes]
        key_raw[:, lanes] = one.T.astype(BF16)
        key_normed[h] = (one * key_inverse * columns[lanes, 3:4]).T.astype(BF16)
        value_rows[h] = values[lanes].T.astype(BF16)

    all_here(QUERY)

    def project(y, total):
        raw = dot(weights[QUERY, y].reshape(band, width), cross_in[...])
        query_raw[rows_of(y, band), :] = raw
        return total + down(raw * raw)

    square = lax.fori_loop(0, ny, project, zero_row)
    go_four(OUT, 1)
    query_inverse = lax.rsqrt(square / width + NORM_EPS)

    length = here.xl * text_rows + (1 - here.xl) * length_ref[0]
    visible = text_row(lax.broadcasted_iota(jnp.int32, (text_rows, token_count), 0)) < length

    def attend(h, carry):
        at = rows_of(h, LANES)
        query[at, :] = (query_raw[at, :] * query_inverse * columns[at, 2:3]).astype(BF16)
        scores = dot(key_normed[h], query[at, :]) * root
        masked = jnp.where(visible, scores, -1e30)
        terms = jnp.where(visible, jnp.exp(masked - jnp.max(masked, axis=0, keepdims=True)), 0.0)
        shares = terms / down(terms)
        attn[h] = shares
        attended[at, :] = lax.dot_general(
            value_rows[h],
            shares.astype(BF16),
            (((0,), (0,)), ((), ())),
            preferred_element_type=F32,
        ).astype(BF16)
        return carry

    lax.fori_loop(0, heads // 2, attend, 0)
    go_four(OUT, 2)
    key_value.start()
    lax.fori_loop(heads // 2, heads, attend, 0)
    all_here(OUT)

    def project_out(y, total):
        at = rows_of(y, band)
        rows_after = dot(weights[OUT, y].reshape(band, width), attended[...]) + tokens[at, :].astype(F32)
        after[at, :] = rows_after
        return total + down(rows_after)

    head_mean = lax.fori_loop(0, ny, project_out, zero_row) / width

    def head_spread(block, total):
        centred = after[rows_of(block, LANES), :] - head_mean
        return total + down(centred * centred)

    head_inverse = lax.rsqrt(lax.fori_loop(0, blocks, head_spread, zero_row) / width + NORM_EPS)

    def modulate(block, carry):
        at = rows_of(block, LANES)
        unit = (after[at, :] - head_mean) * head_inverse
        head_in[at, :] = (unit * columns[at, 8:9] + columns[at, 9:10]).astype(BF16)
        return carry

    lax.fori_loop(0, blocks, modulate, 0)
    noise[here.xl] = dot(w_head[...], head_in[...]) + columns[:patch, 4:5]

    def swap(branch):
        ref = noise.at[branch]
        return remote(ref, ref, swap_sem.at[0], swap_sem.at[1], here.other_branch())

    swap(here.xl).start()
    key_value.over_x()

    def fold(values):
        return jnp.concatenate([values[:, :middle], values[:, middle:]], axis=0)

    def split(values):
        high = values.astype(BF16)
        low = (values - high.astype(F32)).astype(BF16)
        return jnp.concatenate([high, low], axis=0)

    first_row = here.c * half + parity * quarter + here.xh * eighth
    own_span = pl.ds(pl.multiple_of(first_row, eighth), eighth)
    own_lanes = rows_of(pair, wide)
    near = key_raw[own_span, :].astype(F32)
    near_inverse = lax.rsqrt(jnp.mean(near * near, axis=-1, keepdims=True) + NORM_EPS)
    near_unit = key_raw[own_span, own_lanes].astype(F32) * near_inverse

    def multiply(left, lead):
        both = split(left)

        def columns_of(block, carry):
            at = rows_of(block, 2 * LANES)
            if lead:
                matrix = pair_weights[:, :, :, :, :, at].reshape(2 * wide, 2 * LANES)
            else:
                matrix = pair_weights[0, :, :, :, :, at].reshape(wide, 2 * LANES)
            result = dot(both, matrix)
            product[:, at] = result[:eighth] + result[eighth:]
            return carry

        lax.fori_loop(0, blocks // 2, columns_of, 0)

    def exchange(send, recv, lane):
        for d in range(1, pairs):
            q = lax.rem(pair + d, pairs)
            remote(
                send.at[q],
                recv.at[pair],
                tail_sem.at[lane],
                tail_sem.at[lane + 1],
                here.device(y=q * 2 + parity),
            ).start()
        ref = recv.at[pl.ds(0, max(1, pairs - 1))]
        return remote(ref, ref, tail_sem.at[lane], tail_sem.at[lane + 1], here.sibling())

    def collect(send, recv):
        total = send[pair]
        for d in range(1, pairs):
            total = total + recv[lax.rem(pair + d, pairs)]
        return total

    swap(1 - here.xl).wait_recv()
    swap(here.xl).wait_send()
    guided = noise[1] + GUIDE_SCALE * (noise[0] - noise[1])
    guided_ref[...] = guided
    factor = GUIDE_SCALE - (2.0 * GUIDE_SCALE - 1.0) * here.xl.astype(F32)
    d_noise = (factor * (guided - target[...].astype(F32))).astype(BF16)

    def head_back(block, sums):
        at = rows_of(block, LANES)
        unit = (after[at, :] - head_mean) * head_inverse
        part_unit = dot(w_head_rows[at, :], d_noise) * columns[at, 8:9]
        d_unit[at, :] = part_unit
        return (sums[0] + down(part_unit), sums[1] + down(part_unit * unit))

    first_sum, second_sum = lax.fori_loop(0, blocks, head_back, (zero_row, zero_row))
    first_mean, second_mean = first_sum / width, second_sum / width

    def norm_back(block, carry):
        at = rows_of(block, LANES)
        unit = (after[at, :] - head_mean) * head_inverse
        grads = (head_inverse * (d_unit[at, :] - first_mean - unit * second_mean)).astype(BF16)
        for t in range(token_blocks):
            lanes = slice(t * LANES, (t + 1) * LANES)
            d_after[lanes, at] = grads[:, lanes].T
        return carry

    lax.fori_loop(0, blocks, norm_back, 0)

    def out_back(block, carry):
        at = rows_of(block, 2 * LANES)
        matrix = weights[OUT, :, :, :, :, at].reshape(width, 2 * LANES)
        d_attended[:, at] = dot(d_after[...], matrix).astype(BF16)
        return carry

    lax.fori_loop(0, blocks // 2, out_back, 0)
    key_value.over_y()

    def attend_back(h, carry):
        at = rows_of(h, LANES)
        grads = d_attended[:, at]
        shares = attn[h]
        d_shares = dot_lanes(value_rows[h], grads)
        d_scores = shares * (d_shares - down(d_shares * shares))
        d_text[0, :, at] = dot_lanes((d_scores * root).astype(BF16), query[at, :])
        d_text[1, :, at] = dot(shares.astype(BF16), grads)
        return carry

    def group(i):
        return lax.rem(pair + (i + 1), pairs)

    def core_span(c):
        return pl.ds(pl.multiple_of(c * half, half), half)

    def to_sibling(i):
        lanes = rows_of(group(i), wide)
        return remote(
            d_text.at[:, core_span(1 - here.c), lanes],
            d_sibling.at[:, :, lanes],
            sibling_sem.at[0, i],
            sibling_sem.at[1, i],
            here.sibling(),
        )

    def to_row(i, odd):
        lanes = rows_of(group(i), wide)
        span = pl.ds(pl.multiple_of(odd * quarter, quarter), quarter)
        return remote(
            y_send.at[:, span, lanes],
            y_recv.at[here.y],
            y_send_sem.at[i],
            y_recv_sem.at[here.y],
            here.device(y=group(i) * 2 + odd),
        )

    def sum_cores(i):
        lanes = rows_of(group(i), wide)
        to_sibling(i).wait_recv()
        both = d_text[:, core_span(here.c), lanes] + d_sibling[:, :, lanes]
        y_send[:, :, lanes] = both.astype(BF16)
        if i < pairs - 1:
            for odd in (0, 1):
                to_row(i, jnp.int32(odd)).start()
        else:
            to_row(i, 1 - parity).start()
            d_sibling[:, :, lanes] = both

    for i in range(pairs):
        first = group(i) * (heads // pairs)
        lax.fori_loop(first, first + heads // pairs, attend_back, 0)
        to_sibling(i).start()
        if i > 0:
            sum_cores(i - 1)
        if i == pairs - 2 or pairs == 1:
            key_value.from_sibling()
            multiply(near_unit * near_inverse, False)
            for q in range(pairs):
                unit_send[q] = fold(product[q * own_rows : (q + 1) * own_rows, :])
            units = exchange(unit_send, unit_recv, 2)
    sum_cores(pairs - 1)

    quarter_span = pl.ds(pl.multiple_of(parity * quarter, quarter), quarter)
    summed = d_sibling[:, quarter_span, own_lanes]
    for d in list(range(2, ny)) + [0]:
        y = lax.rem(pair * 2 + d, ny) if d else here.y + 1 - 2 * parity
        ref = y_recv.at[y]
        remote(ref, ref, y_send_sem.at[0], y_recv_sem.at[y], here.sibling()).wait_recv()
        summed = summed + y_recv[y].astype(F32)
    x_send[0] = summed[:, :eighth]
    x_send[1] = summed[:, eighth:]
    cross = remote(
        x_send.at[1 - here.xh], x_recv, tail_sem.at[0], tail_sem.at[1], here.other_tokens()
    )
    cross.start()
    if pairs > 1:
        units.wait_recv()
    unit_total = collect(unit_send, unit_recv)
    own_gain = vectors[3:4, own_lanes]
    cross.wait_recv()
    own_sum = x_send[here.xh] + x_recv[...]
    gained = own_sum[0] * own_gain
    statistic = jnp.sum(gained * near_unit, axis=-1, keepdims=True) / width
    multiply(jnp.concatenate([near_inverse * gained, own_sum[1]], axis=1), True)
    for q in range(pairs):
        span = slice(q * own_rows, (q + 1) * own_rows)
        grad_send[q, :, :middle] = fold(product[span, :])
        both = jnp.broadcast_to(statistic[span], (own_rows, LANES))
        grad_send[q, :, middle:] = jnp.concatenate([both, both], axis=0)
    grads = exchange(grad_send, grad_recv, 4)
    if pairs > 1:
        grads.wait_recv()
    total = collect(grad_send, grad_recv)
    z_send[...] = total[:, :middle] - total[:, middle : middle + 1] * unit_total

    def unfold(values):
        grad_ref[:, :middle] = values[:own_rows]
        grad_ref[:, middle:] = values[own_rows:]

    @pl.when(here.xl == 0)
    def _():
        unfold(z_send[...])

    @pl.when(here.xl == 1)
    def _():
        for d in range(1, nz):
            remote(
                z_send, z_recv.at[here.z], tail_sem.at[6], tail_sem.at[7], here.at_z(d)
            ).start()
        ref = z_recv.at[pl.ds(0, nz - 1)]
        gathered = remote(ref, ref, tail_sem.at[6], tail_sem.at[7], here.sibling())
        gathered.wait_recv()
        clips = z_send[...]
        for d in range(1, nz):
            clips = clips + z_recv[here.up_z(d)]
        unfold(clips / nz)
        gathered.wait_send()

    cross.wait_send()
    if pairs > 1:
        units.wait_send()
        grads.wait_send()
    for i in range(pairs):
        to_sibling(i).wait_send()
        ref = y_send.at[:, :, rows_of(group(i), wide)]
        if i == pairs - 1:
            ref = y_send.at[:, pl.ds(0, quarter), rows_of(group(i), wide)]
        remote(ref, ref, y_send_sem.at[i], y_recv_sem.at[0], here.sibling()).wait_send()
    text_ring.finish()
    key_value.finish()
    for three in rings:
        for ring in three:
            ring.finish()


def on_device(
    latents,
    prompt,
    null_embed,
    text_lengths,
    timesteps,
    head_mod,
    cross_gain,
    cross_bias,
    q_gain,
    k_gain,
    w_query,
    w_key,
    w_value,
    w_out,
    w_head,
    head_bias,
    target,
):
    nz = lax.axis_size("clip")
    ny = lax.axis_size("seq") // 4
    tokens = latents[0, 0]
    count, width = tokens.shape
    text_rows = null_embed.shape[0]
    rows = w_query.shape[1]
    patch = w_head.shape[1]
    heads = width // LANES
    pairs = ny // 2
    wide = width // pairs
    middle = width // 2
    half, quarter, eighth = text_rows // 2, text_rows // 4, text_rows // 8
    own_rows = text_rows // ny // 4
    dma = pltpu.SemaphoreType.DMA
    vmem = pl.BlockSpec(memory_space=pltpu.VMEM)
    smem = pl.BlockSpec(memory_space=pltpu.SMEM)
    vectors = jnp.stack(
        [cross_gain, cross_bias, q_gain, k_gain, jnp.pad(head_bias, (0, width - patch))]
        + [jnp.zeros_like(k_gain)] * 3
    )
    guided, grad = pl.pallas_call(
        kernel,
        out_shape=(
            jax.ShapeDtypeStruct((patch, count), F32),
            jax.ShapeDtypeStruct((own_rows, width), F32),
        ),
        in_specs=[smem, smem] + [vmem] * 11,
        out_specs=(vmem, vmem),
        scratch_shapes=[
            pltpu.VMEM((2, ny, 2, 2, rows, width), BF16),
            pltpu.VMEM((2, 2, 2, 2, rows, width), BF16),
            pltpu.VMEM((ny, 2, 2, 2 * rows, text_rows), BF16),
            pltpu.VMEM((text_rows, width), BF16),
            pltpu.VMEM((width, LANES), F32),
            pltpu.VMEM((width, patch), BF16),
            pltpu.VMEM((width, count), BF16),
            pltpu.VMEM((width, count), BF16),
            pltpu.VMEM((width, count), F32),
            pltpu.VMEM((width, count), BF16),
            pltpu.VMEM((heads, text_rows, LANES), BF16),
            pltpu.VMEM((heads, text_rows, LANES), BF16),
            pltpu.VMEM((text_rows, width), BF16),
            pltpu.VMEM((heads, text_rows, count), F32),
            pltpu.VMEM((width, count), BF16),
            pltpu.VMEM((width, count), F32),
            pltpu.VMEM((width, count), BF16),
            pltpu.VMEM((width, count), F32),
            pltpu.VMEM((count, width), BF16),
            pltpu.VMEM((count, width), BF16),
            pltpu.VMEM((2, patch, count), F32),
            pltpu.VMEM((2, text_rows, width), F32),
            pltpu.VMEM((2, half, width), F32),
            pltpu.VMEM((2, half, width), BF16),
            pltpu.VMEM((ny, 2, quarter, wide), BF16),
            pltpu.VMEM((2, 2, eighth, wide), F32),
            pltpu.VMEM((2, eighth, wide), F32),
            pltpu.VMEM((eighth, width), F32),
            pltpu.VMEM((pairs, 2 * own_rows, middle), F32),
            pltpu.VMEM((pairs, 2 * own_rows, middle), F32),
            pltpu.VMEM((pairs, 2 * own_rows, middle + LANES), F32),
            pltpu.VMEM((pairs, 2 * own_rows, middle + LANES), F32),
            pltpu.VMEM((2 * own_rows, middle), F32),
            pltpu.VMEM((nz, 2 * own_rows, middle), F32),
            dma((4 * ny,)),
            dma((3,)),
            dma((2, 4 * ny)),
            dma((2, 3)),
            dma((2, ny + 17)),
            dma((2, 4)),
            dma((2, ny + 16)),
            dma((2, 3)),
            dma((8,)),
            dma((3,)),
            dma((2,)),
            dma((2, pairs)),
            dma((ny,)),
            dma((pairs,)),
            dma((8,)),
        ],
        compiler_params=pltpu.CompilerParams(
            collective_id=0, has_side_effects=True, vmem_limit_bytes=60 * 1024 * 1024
        ),
        cost_estimate=pl.CostEstimate(
            flops=8 * count * width * width, bytes_accessed=8 * count * width, transcendentals=0
        ),
    )(
        text_lengths,
        timesteps,
        tokens,
        prompt[0],
        null_embed,
        head_mod,
        vectors,
        w_query.T,
        w_key.T,
        w_value.T,
        w_out.T,
        w_head.T,
        target[0].T,
    )
    return (guided.T[None], grad.reshape(1, 1, own_rows, width))


def solution(mesh):
    return jax.shard_map(
        on_device,
        mesh=mesh,
        in_specs=(
            P("clip", "guide", "seq", None),
            P("clip", None, None),
            P(),
            P("clip"),
            P("clip"),
            P(),
            P(),
            P(),
            P(),
            P(),
            P(None, "seq"),
            P(None, "seq"),
            P(None, "seq"),
            P(None, "seq"),
            P(),
            P(),
            P("clip", "seq", None),
        ),
        out_specs=(P("clip", "seq", None), P("clip", "guide", "seq", None)),
        check_vma=False,
    )
```

```python
import functools
import math

import jax
import jax.numpy as jnp
from jax import lax
from jax.experimental import pallas as pl
from jax.experimental.pallas import tpu as pltpu
from jax.sharding import PartitionSpec as P

LANES = 128
GUIDE_SCALE = 5.0
NORM_EPS = 1e-06
COLOURS = 4
MESH = pl.DeviceIdType.MESH
F32 = jnp.float32
BF16 = jnp.bfloat16
QUERY, OUT = range(2)


class Place:
    def __init__(self):
        seq = lax.axis_index("seq")
        self.nz = lax.axis_size("clip")
        self.ny = lax.axis_size("seq") // 4
        self.z = lax.axis_index("clip")
        self.xl = lax.axis_index("guide")
        self.y = lax.div(seq, 4)
        self.xh = lax.rem(lax.div(seq, 2), 2)
        self.c = lax.rem(seq, 2)
        self.x = self.xh * 2 + self.xl

    def device(self, z=None, y=None, xh=None, xl=None, c=None):
        z = self.z if z is None else z
        y = self.y if y is None else y
        xh = self.xh if xh is None else xh
        xl = self.xl if xl is None else xl
        c = self.c if c is None else c
        return {"clip": z, "guide": xl, "seq": y * 4 + xh * 2 + c}

    def up_y(self, by):
        return lax.rem(self.y + (by + self.ny), self.ny)

    def up_z(self, by):
        return lax.rem(self.z + (by + self.nz), self.nz)

    def up_x(self, by):
        return lax.rem(self.x + (by + 4), 4)

    def at_y(self, by):
        return self.device(y=self.up_y(by))

    def at_z(self, by):
        return self.device(z=self.up_z(by))

    def at_x(self, by):
        x = self.up_x(by)
        return self.device(xh=lax.div(x, 2), xl=lax.rem(x, 2))

    def sibling(self):
        return self.device(c=1 - self.c)

    def other_columns(self):
        return self.device(xh=1 - self.xh, xl=1 - self.xl)

    def other_tokens(self):
        return self.device(xh=1 - self.xh)

    def other_branch(self):
        return self.device(xl=1 - self.xl)


def remote(src, dst, send_sem, recv_sem, device):
    return pltpu.make_async_remote_copy(
        src_ref=src,
        dst_ref=dst,
        send_sem=send_sem,
        recv_sem=recv_sem,
        device_id=device,
        device_id_type=MESH,
    )


def reach(count):
    return {1: count // 2, -1: count - 1 - count // 2}


class RingY:
    def __init__(self, here, base, lanes, partner, recv, send):
        self.here, self.base, self.lanes, self.partner = here, base, lanes, partner
        self.recv, self.send = recv, send
        hops = reach(here.ny)
        self.hops = {(d, o): hops[d if o == 0 else -d] for d in (1, -1) for o in (0, 1)}
        self.rounds = here.ny // 2

    def chunk(self, y, xh, c):
        return self.base.at[y, xh, c, :, self.lanes]

    def copy(self, y, xh, c, lane, device):
        ref = self.chunk(y, xh, c)
        return remote(ref, ref, self.send.at[lane], self.recv.at[y * 4 + xh * 2 + c], device)

    def pass_on(self, y, other, step):
        here = self.here
        xh = here.xh if other == 0 else 1 - here.xh
        for d in (1, -1):
            if step == 0 and self.hops[d, other] > 0:
                self.copy(y, xh, here.c, 0, here.at_y(d)).start()
        self.copy(y, xh, here.c, 1, here.sibling()).start()

    def start(self):
        here = self.here
        self.copy(here.y, here.xh, here.c, 2, self.partner).start()
        self.pass_on(here.y, 0, 0)

    def over_x(self):
        here = self.here
        self.copy(here.y, 1 - here.xh, here.c, 2, self.partner).wait_recv()
        self.pass_on(here.y, 1, 0)

    def round(self, k):
        here = self.here
        for other in (0, 1):
            xh = here.xh if other == 0 else 1 - here.xh
            for d in (1, -1):
                if k <= self.hops[d, other]:
                    y = here.up_y(-d * k)
                    self.copy(y, xh, here.c, 0, here.at_y(d)).wait_recv()
                    if k < self.hops[d, other]:
                        self.copy(y, xh, here.c, 0, here.at_y(d)).start()
                    self.copy(y, xh, here.c, 1, here.sibling()).start()

    def from_sibling(self, y):
        here = self.here
        for xh in (0, 1):
            self.copy(y, xh, 1 - here.c, 1, here.sibling()).wait_recv()

    def finish(self):
        here = self.here
        for lane, ref in (
            (0, self.base.at[pl.ds(0, here.ny - 1), :, here.c, :, self.lanes]),
            (1, self.base.at[:, :, here.c, :, self.lanes]),
            (2, self.chunk(here.y, here.xh, here.c)),
        ):
            remote(ref, ref, self.send.at[lane], self.recv.at[0], here.sibling()).wait_send()


class RingFour:
    def __init__(self, here, base, first, width, axis, recv, send):
        self.here, self.base, self.first, self.width, self.axis = here, base, first, width, axis
        self.recv, self.send = recv, send
        self.hops = reach(here.ny)
        self.colour = here.x if axis == "x" else lax.rem(here.z, COLOURS)

    def part(self, index):
        return pl.ds(pl.multiple_of(self.first + index * self.width, LANES), self.width)

    def toward(self, d):
        return self.here.at_x(d) if self.axis == "x" else self.here.at_z(d)

    def along(self, y, d):
        here = self.here
        if self.axis == "x":
            ref = self.base.at[y, here.xh, here.c, :, self.part(here.xl)]
        else:
            ref = self.base.at[y, :, here.c, :, self.part(self.colour)]
        return remote(ref, ref, self.send.at[0], self.recv.at[y], here.at_y(d))

    def over(self, xh):
        here = self.here
        ref = self.base.at[here.y, xh, here.c, :, self.part(self.colour)]
        return remote(ref, ref, self.send.at[3], self.recv.at[here.ny + 16], here.other_columns())

    def half(self, colour, h, c, lane, device):
        size = self.here.ny // 2
        span = pl.ds(h * size, size)
        if self.axis == "x":
            ref = self.base.at[span, lax.div(colour, 2), c, :, self.part(lax.rem(colour, 2))]
        else:
            ref = self.base.at[span, :, c, :, self.part(colour)]
        slot = self.here.ny + (lane - 1) * 8 + colour * 2 + h
        return remote(ref, ref, self.send.at[lane], self.recv.at[slot], device)

    def begin_y(self):
        for d in (1, -1):
            if self.hops[d] > 0:
                self.along(self.here.y, d).start()

    def start(self):
        if self.axis == "x":
            self.begin_y()
        else:
            self.over(self.here.xh).start()

    def over_x(self):
        if self.axis == "z":
            self.over(1 - self.here.xh).wait_recv()
            self.begin_y()

    def round(self, k):
        for d in (1, -1):
            if k <= self.hops[d]:
                y = self.here.up_y(-d * k)
                self.along(y, d).wait_recv()
                if k < self.hops[d]:
                    self.along(y, d).start()

    def begin_four(self):
        here = self.here
        for h, d in ((0, 1), (1, -1), (1, 1), (0, -1)):
            self.half(self.colour, h, here.c, 1, self.toward(d)).start()
        for h in (0, 1):
            self.half(self.colour, h, here.c, 2, here.sibling()).start()

    def four(self, k):
        here = self.here
        if k == 1:
            came = ((0, 1, True), (1, -1, True), (1, 1, False), (0, -1, False))
        else:
            came = ((0, 2, False), (1, -2, False))
        for h, d, further in came:
            colour = lax.rem(self.colour + (COLOURS - d), COLOURS)
            toward = self.toward(1 if d > 0 else -1)
            self.half(colour, h, here.c, 1, toward).wait_recv()
            if further:
                self.half(colour, h, here.c, 1, toward).start()
            self.half(colour, h, here.c, 2, here.sibling()).start()

    def from_sibling(self):
        here = self.here
        for colour in range(COLOURS):
            for h in (0, 1):
                self.half(jnp.int32(colour), h, 1 - here.c, 2, here.sibling()).wait_recv()

    def finish(self):
        here = self.here
        xh = 0 if self.axis == "x" else slice(None)
        ends = [
            (0, self.base.at[pl.ds(0, here.ny - 1), xh, here.c, :, pl.ds(0, self.width)]),
            (1, self.base.at[:, xh, here.c, :, pl.ds(0, 3 * self.width)]),
            (2, self.base.at[:, xh, here.c, :, pl.ds(0, 4 * self.width)]),
        ]
        if self.axis == "z":
            ends.append((3, self.base.at[0, 0, here.c, :, pl.ds(0, self.width)]))
        for lane, ref in ends:
            remote(ref, ref, self.send.at[lane], self.recv.at[0], here.sibling()).wait_send()


class Pair:
    def __init__(self, here, base, recv, send):
        self.here, self.base, self.recv, self.send = here, base, recv, send
        self.parity = lax.rem(here.y, 2)
        self.other_y = here.device(y=here.y + 1 - 2 * self.parity)

    def copy(self, parity, xh, c, lane, device):
        ref = self.base.at[:, parity, xh, c]
        slot = parity * 4 + xh * 2 + c
        return remote(ref, ref, self.send.at[lane], self.recv.at[slot], device)

    def start(self):
        here = self.here
        self.copy(self.parity, here.xh, here.c, 2, here.other_columns()).start()
        self.copy(self.parity, here.xh, here.c, 0, self.other_y).start()
        self.copy(self.parity, here.xh, here.c, 1, here.sibling()).start()

    def over_x(self):
        here = self.here
        self.copy(self.parity, 1 - here.xh, here.c, 2, here.other_columns()).wait_recv()
        self.copy(self.parity, 1 - here.xh, here.c, 0, self.other_y).start()
        self.copy(self.parity, 1 - here.xh, here.c, 1, here.sibling()).start()

    def over_y(self):
        here = self.here
        for xh in (here.xh, 1 - here.xh):
            self.copy(1 - self.parity, xh, here.c, 0, self.other_y).wait_recv()
            self.copy(1 - self.parity, xh, here.c, 1, here.sibling()).start()

    def from_sibling(self):
        here = self.here
        for parity in (0, 1):
            for xh in (0, 1):
                self.copy(parity, xh, 1 - here.c, 1, here.sibling()).wait_recv()

    def finish(self):
        here = self.here
        for lane, ref in (
            (0, self.base.at[:, 0, :, here.c]),
            (1, self.base.at[:, :, :, here.c]),
            (2, self.base.at[:, 0, 0, here.c]),
        ):
            remote(ref, ref, self.send.at[lane], self.recv.at[0], here.sibling()).wait_send()


def down(values):
    return jnp.sum(values, axis=0, keepdims=True)


def dot(left, right):
    return jnp.dot(left, right, preferred_element_type=F32)


def dot_lanes(left, right):
    return lax.dot_general(left, right, (((1,), (1,)), ((), ())), preferred_element_type=F32)


def row(ref):
    return ref[...].reshape(1, ref.shape[0])


def rows_of(index, size):
    return pl.ds(pl.multiple_of(index * size, size), size)


def log2(count):
    return count.bit_length() - 1


def kernel(
    length_ref,
    step_ref,
    latents_in,
    prompt_in,
    null_in,
    head_mod_in,
    cross_gain,
    cross_bias,
    q_gain,
    k_gain,
    w_query,
    w_key,
    w_value,
    w_out,
    w_head_in,
    head_bias,
    target_in,
    guided_ref,
    grad_ref,
    latents,
    either,
    head_mod,
    w_head,
    target,
    weights,
    pair_weights,
    text,
    context,
    columns,
    w_head_rows,
    tokens,
    cross_in,
    query_raw,
    query,
    key_normed,
    value_rows,
    key_raw,
    attn,
    attended,
    after,
    head_in,
    d_unit,
    d_after,
    d_attended,
    noise,
    d_text,
    d_sibling,
    y_send,
    y_recv,
    x_send,
    x_recv,
    product,
    lane_gain,
    unit_send,
    unit_recv,
    grad_send,
    grad_recv,
    z_send,
    z_recv,
    text_recv,
    text_send,
    recv_y,
    send_y,
    recv_z,
    send_z,
    recv_x,
    send_x,
    pair_recv,
    pair_send,
    swap_sem,
    sibling_sem,
    y_recv_sem,
    y_send_sem,
    tail_sem,
    load_sem,
):
    here = Place()
    ny, nz = here.ny, here.nz
    rows, width = w_query.shape
    token_count = latents_in.shape[0]
    text_rows = prompt_in.shape[0]
    patch = w_head_in.shape[0]
    heads = width // LANES
    blocks = width // LANES
    token_blocks = token_count // LANES
    band = 4 * rows
    root = 1.0 / math.sqrt(LANES)
    pairs = ny // 2
    share = text_rows // ny
    own_rows = share // 4
    half, quarter, eighth = text_rows // 2, text_rows // 4, text_rows // 8
    wide = width // pairs
    middle = width // 2
    parity = lax.rem(here.y, 2)
    pair = lax.div(here.y, 2)

    partners = [here.sibling(), here.other_columns(), here.other_tokens(), here.other_branch()]
    partners += [here.at_y(d) for d in range(1, ny)] + [here.at_z(d) for d in range(1, nz)]
    barrier = pltpu.get_barrier_semaphore()
    for device in partners:
        pl.semaphore_signal(barrier, inc=1, device_id=device, device_id_type=MESH)

    x_part = LANES * (2 if blocks >= 12 else 1)
    x_first = width - 2 * x_part
    z_first = x_first - COLOURS * LANES
    y_lanes = pl.ds(0, z_first)
    loads = []

    def load(src, dst):
        loads.append(pltpu.make_async_copy(src, dst, load_sem.at[len(loads)]))
        loads[-1].start()

    for index, own in ((QUERY, w_query), (OUT, w_out)):
        for lanes in (
            y_lanes,
            pl.ds(pl.multiple_of(z_first + lax.rem(here.z, COLOURS) * LANES, LANES), LANES),
            pl.ds(pl.multiple_of(x_first + here.xl * x_part, LANES), x_part),
        ):
            load(own.at[:, lanes], weights.at[index, here.y, here.xh, here.c, :, lanes])
    for index, own in enumerate((w_key, w_value)):
        load(own, pair_weights.at[index, parity, here.xh, here.c])
    for src, dst in (
        (head_mod_in, head_mod),
        (w_head_in, w_head),
        (latents_in, latents),
        (target_in, target),
    ):
        load(src, dst)
    text_load = load_sem.at[len(loads)]

    @pl.when(here.xl == 0)
    def _():
        pltpu.make_async_copy(prompt_in, either, text_load).start()

    @pl.when(here.xl == 1)
    def _():
        pltpu.make_async_copy(null_in, either, text_load).start()

    for copy in loads[:6]:
        copy.wait()
    pl.semaphore_wait(barrier, len(partners))

    text_ring = RingY(here, text, slice(None), here.other_tokens(), text_recv, text_send)
    rings = []
    for index in (QUERY, OUT):
        base = weights.at[index]
        rings.append(
            (
                RingFour(here, base, x_first, x_part, "x", recv_x.at[index], send_x.at[index]),
                RingFour(here, base, z_first, LANES, "z", recv_z.at[index], send_z.at[index]),
                RingY(
                    here, base, y_lanes, here.other_columns(), recv_y.at[index], send_y.at[index]
                ),
            )
        )
    key_value = Pair(here, pair_weights, pair_recv, pair_send)

    x_query, z_query, y_query = rings[QUERY]
    x_out, z_out, y_out = rings[OUT]

    def small_round(index, k):
        for ring in rings[index][:2]:
            ring.round(k)
            if k == pairs:
                ring.begin_four()

    def go_four(index, k):
        for ring in rings[index][:2]:
            ring.four(k)

    def all_here(index):
        for ring in rings[index][:2]:
            ring.from_sibling()
        for y in range(ny):
            rings[index][2].from_sibling(y)

    for ring in rings[QUERY]:
        ring.start()

    def text_row(index):
        place = lax.shift_right_logical(index, log2(own_rows)) & (pairs - 1)
        place = place * 2 + (lax.shift_right_logical(index, log2(quarter)) & 1)
        place = place * 2 + (lax.shift_right_logical(index, log2(eighth)) & 1)
        place = place * 2 + (lax.shift_right_logical(index, log2(half)) & 1)
        return place * own_rows + (index & (own_rows - 1))

    square_iota = functools.partial(lax.broadcasted_iota, jnp.int32, (text_rows, text_rows))
    order = jnp.where(text_row(square_iota(0)) == square_iota(1), 1.0, 0.0).astype(BF16)

    pltpu.make_async_copy(prompt_in, either, text_load).wait()
    context[...] = dot(order, either[...]).astype(BF16)
    for copy in loads[6:8]:
        copy.wait()
    own_key = pair_weights[0, parity, here.xh, here.c]
    own_value = pair_weights[1, parity, here.xh, here.c]
    text[here.y, here.xh, here.c, :rows] = dot_lanes(own_key, context[...]).astype(BF16)
    text[here.y, here.xh, here.c, rows:] = dot_lanes(own_value, context[...]).astype(BF16)
    text_ring.start()
    z_query.over_x()
    y_query.over_x()

    for copy in loads[8:]:
        copy.wait()
    modulation = head_mod[step_ref[0]]
    stack = jnp.concatenate(
        [
            row(cross_gain),
            row(cross_bias),
            row(q_gain),
            row(k_gain),
            1.0 + modulation[1:2],
            modulation[0:1],
            jnp.concatenate([row(head_bias), jnp.zeros((1, width - patch), F32)], axis=1),
            jnp.zeros((LANES - 7, width), F32),
        ],
        axis=0,
    )
    for block in range(blocks):
        lanes = slice(block * LANES, (block + 1) * LANES)
        columns[lanes, :] = stack[:, lanes].T
        w_head_rows[lanes, :] = w_head[:, lanes].T

    def turn(block, total):
        at = rows_of(block, LANES)
        for t in range(token_blocks):
            lanes = slice(t * LANES, (t + 1) * LANES)
            tokens[at, lanes] = latents[lanes, at].T
        return total + down(tokens[at, :].astype(F32))

    zero_row = jnp.zeros((1, token_count), F32)
    mean = lax.fori_loop(0, blocks, turn, zero_row) / width

    small_round(QUERY, 1)
    text_ring.over_x()
    x_out.start()
    z_out.start()

    def spread(block, total):
        centred = tokens[rows_of(block, LANES), :].astype(F32) - mean
        return total + down(centred * centred)

    inverse = lax.rsqrt(lax.fori_loop(0, blocks, spread, zero_row) / width + NORM_EPS)

    def normalise(block, carry):
        at = rows_of(block, LANES)
        unit = (tokens[at, :].astype(F32) - mean) * inverse
        cross_in[at, :] = (unit * columns[at, 0:1] + columns[at, 1:2]).astype(BF16)
        return carry

    y_query.round(1)
    z_out.over_x()
    if pairs > 1:
        small_round(QUERY, 2)
    text_ring.round(1)
    lax.fori_loop(0, blocks, normalise, 0)

    y_out.start()
    for k in range(3, pairs + 1):
        small_round(QUERY, k)
        small_round(OUT, k - 2)
        if k == 3:
            y_out.over_x()
            y_query.round(2)
            text_ring.round(2)
    if pairs < 3:
        y_out.over_x()
        if pairs > 1:
            y_query.round(2)
            text_ring.round(2)
    if pairs > 2:
        y_query.round(3)
        text_ring.round(3)
    if pairs > 1:
        small_round(OUT, pairs - 1)
        y_out.round(1)
    go_four(QUERY, 1)
    small_round(OUT, pairs)
    if pairs > 3:
        text_ring.round(4)
        y_query.round(4)
    if pairs > 1:
        y_out.round(2)
    else:
        y_out.round(1)
    go_four(QUERY, 2)
    for y in range(ny):
        text_ring.from_sibling(y)

    keys = text[:, :, :, :rows, :].reshape(width, text_rows).astype(F32)
    values = text[:, :, :, rows:, :].reshape(width, text_rows).astype(F32)
    key_inverse = lax.rsqrt(down(keys * keys) / width + NORM_EPS)
    for h in range(heads):
        lanes = slice(h * LANES, (h + 1) * LANES)
        one = keys[lanes]
        key_raw[:, lanes] = one.T.astype(BF16)
        key_normed[h] = (one * key_inverse * columns[lanes, 3:4]).T.astype(BF16)
        value_rows[h] = values[lanes].T.astype(BF16)

    all_here(QUERY)

    def project(y, total):
        raw = dot(weights[QUERY, y].reshape(band, width), cross_in[...])
        query_raw[rows_of(y, band), :] = raw
        return total + down(raw * raw)

    square = lax.fori_loop(0, ny // 2, project, zero_row)
    go_four(OUT, 1)
    if pairs > 2:
        y_out.round(3)
    square = lax.fori_loop(ny // 2, ny, project, square)
    query_inverse = lax.rsqrt(square / width + NORM_EPS)

    length = here.xl * text_rows + (1 - here.xl) * length_ref[0]
    visible = text_row(lax.broadcasted_iota(jnp.int32, (text_rows, token_count), 0)) < length

    def attend(h, carry):
        at = rows_of(h, LANES)
        query[at, :] = (query_raw[at, :] * query_inverse * columns[at, 2:3]).astype(BF16)
        scores = dot(key_normed[h], query[at, :]) * root
        masked = jnp.where(visible, scores, -1e30)
        terms = jnp.where(visible, jnp.exp(masked - jnp.max(masked, axis=0, keepdims=True)), 0.0)
        shares = terms / down(terms)
        attn[h] = shares
        attended[at, :] = lax.dot_general(
            value_rows[h],
            shares.astype(BF16),
            (((0,), (0,)), ((), ())),
            preferred_element_type=F32,
        ).astype(BF16)
        return carry

    lax.fori_loop(0, heads // 4, attend, 0, unroll=True)
    go_four(OUT, 2)
    lax.fori_loop(heads // 4, heads // 2, attend, 0, unroll=True)
    if pairs > 3:
        y_out.round(4)
    key_value.start()
    lax.fori_loop(heads // 2, heads, attend, 0, unroll=True)
    all_here(OUT)

    def project_out(y, total):
        at = rows_of(y, band)
        rows_after = dot(weights[OUT, y].reshape(band, width), attended[...]) + tokens[at, :].astype(F32)
        after[at, :] = rows_after
        return total + down(rows_after)

    head_mean = lax.fori_loop(0, ny, project_out, zero_row) / width

    def head_spread(block, total):
        centred = after[rows_of(block, LANES), :] - head_mean
        return total + down(centred * centred)

    head_inverse = lax.rsqrt(lax.fori_loop(0, blocks, head_spread, zero_row) / width + NORM_EPS)

    def modulate(block, carry):
        at = rows_of(block, LANES)
        unit = (after[at, :] - head_mean) * head_inverse
        head_in[at, :] = (unit * columns[at, 4:5] + columns[at, 5:6]).astype(BF16)
        return carry

    lax.fori_loop(0, blocks, modulate, 0)
    noise[here.xl] = dot(w_head[...], head_in[...]) + columns[:patch, 6:7]

    def swap(branch):
        ref = noise.at[branch]
        return remote(ref, ref, swap_sem.at[0], swap_sem.at[1], here.other_branch())

    swap(here.xl).start()
    key_value.over_x()

    def fold(values):
        return jnp.concatenate([values[:, :middle], values[:, middle:]], axis=0)

    def split(values):
        high = values.astype(BF16)
        low = (values - high.astype(F32)).astype(BF16)
        return jnp.concatenate([high, low], axis=0)

    first_row = here.c * half + parity * quarter + here.xh * eighth
    own_span = pl.ds(pl.multiple_of(first_row, eighth), eighth)
    own_lanes = rows_of(pair, wide)
    near = key_raw[own_span, :].astype(F32)
    near_inverse = lax.rsqrt(jnp.mean(near * near, axis=-1, keepdims=True) + NORM_EPS)
    near_unit = key_raw[own_span, own_lanes].astype(F32) * near_inverse

    def multiply(left, lead):
        both = split(left)

        def columns_of(block, carry):
            at = rows_of(block, 2 * LANES)
            if lead:
                matrix = pair_weights[:, :, :, :, :, at].reshape(2 * wide, 2 * LANES)
            else:
                matrix = pair_weights[0, :, :, :, :, at].reshape(wide, 2 * LANES)
            result = dot(both, matrix)
            product[:, at] = result[:eighth] + result[eighth:]
            return carry

        lax.fori_loop(0, blocks // 2, columns_of, 0)

    def exchange(send, recv, lane):
        for d in range(1, pairs):
            q = lax.rem(pair + d, pairs)
            remote(
                send.at[q],
                recv.at[pair],
                tail_sem.at[lane],
                tail_sem.at[lane + 1],
                here.device(y=q * 2 + parity),
            ).start()
        ref = recv.at[pl.ds(0, max(1, pairs - 1))]
        return remote(ref, ref, tail_sem.at[lane], tail_sem.at[lane + 1], here.sibling())

    def collect(send, recv):
        total = send[pair]
        for d in range(1, pairs):
            total = total + recv[lax.rem(pair + d, pairs)]
        return total

    swap(1 - here.xl).wait_recv()
    swap(here.xl).wait_send()
    guided = noise[1] + GUIDE_SCALE * (noise[0] - noise[1])
    guided_ref[...] = guided
    factor = GUIDE_SCALE - (2.0 * GUIDE_SCALE - 1.0) * here.xl.astype(F32)
    d_noise = (factor * (guided - target[...].astype(F32))).astype(BF16)

    def head_back(block, sums):
        at = rows_of(block, LANES)
        unit = (after[at, :] - head_mean) * head_inverse
        part_unit = dot(w_head_rows[at, :], d_noise) * columns[at, 4:5]
        d_unit[at, :] = part_unit
        return (sums[0] + down(part_unit), sums[1] + down(part_unit * unit))

    first_sum, second_sum = lax.fori_loop(0, blocks, head_back, (zero_row, zero_row))
    first_mean, second_mean = first_sum / width, second_sum / width

    def norm_back(block, carry):
        at = rows_of(block, LANES)
        unit = (after[at, :] - head_mean) * head_inverse
        grads = (head_inverse * (d_unit[at, :] - first_mean - unit * second_mean)).astype(BF16)
        for t in range(token_blocks):
            lanes = slice(t * LANES, (t + 1) * LANES)
            d_after[lanes, at] = grads[:, lanes].T
        return carry

    lax.fori_loop(0, blocks, norm_back, 0)

    def out_back(block, carry):
        at = rows_of(block, 2 * LANES)
        matrix = weights[OUT, :, :, :, :, at].reshape(width, 2 * LANES)
        d_attended[:, at] = dot(d_after[...], matrix).astype(BF16)
        return carry

    lax.fori_loop(0, blocks // 2, out_back, 0)
    key_value.over_y()

    def attend_back(h, carry):
        at = rows_of(h, LANES)
        grads = d_attended[:, at]
        shares = attn[h]
        d_shares = dot_lanes(value_rows[h], grads)
        d_scores = shares * (d_shares - down(d_shares * shares))
        d_text[0, :, at] = dot_lanes((d_scores * root).astype(BF16), query[at, :])
        d_text[1, :, at] = dot(shares.astype(BF16), grads)
        return carry

    def group(i):
        return lax.rem(pair + (i + 1), pairs)

    def core_span(c):
        return pl.ds(pl.multiple_of(c * half, half), half)

    def to_sibling(i):
        lanes = rows_of(group(i), wide)
        return remote(
            d_text.at[:, core_span(1 - here.c), lanes],
            d_sibling.at[:, :, lanes],
            sibling_sem.at[0, i],
            sibling_sem.at[1, i],
            here.sibling(),
        )

    def to_row(i, odd):
        lanes = rows_of(group(i), wide)
        span = pl.ds(pl.multiple_of(odd * quarter, quarter), quarter)
        return remote(
            y_send.at[:, span, lanes],
            y_recv.at[here.y],
            y_send_sem.at[i],
            y_recv_sem.at[here.y],
            here.device(y=group(i) * 2 + odd),
        )

    def sum_cores(i):
        lanes = rows_of(group(i), wide)
        to_sibling(i).wait_recv()
        both = d_text[:, core_span(here.c), lanes] + d_sibling[:, :, lanes]
        y_send[:, :, lanes] = both.astype(BF16)
        if i < pairs - 1:
            for odd in (0, 1):
                to_row(i, jnp.int32(odd)).start()
        else:
            to_row(i, 1 - parity).start()
            d_sibling[:, :, lanes] = both

    for i in range(pairs):
        for j in range(heads // pairs):
            attend_back(group(i) * (heads // pairs) + j, 0)
        to_sibling(i).start()
        if i > 0:
            sum_cores(i - 1)
        if i == pairs - 2 or pairs == 1:
            key_value.from_sibling()
            multiply(near_unit * near_inverse, False)
            for q in range(pairs):
                unit_send[q] = fold(product[q * own_rows : (q + 1) * own_rows, :])
            units = exchange(unit_send, unit_recv, 2)
    sum_cores(pairs - 1)

    quarter_span = pl.ds(pl.multiple_of(parity * quarter, quarter), quarter)
    summed = d_sibling[:, quarter_span, own_lanes]
    for d in list(range(2, ny)) + [0]:
        y = lax.rem(pair * 2 + d, ny) if d else here.y + 1 - 2 * parity
        ref = y_recv.at[y]
        remote(ref, ref, y_send_sem.at[0], y_recv_sem.at[y], here.sibling()).wait_recv()
        summed = summed + y_recv[y].astype(F32)
    x_send[0] = summed[:, :eighth]
    x_send[1] = summed[:, eighth:]
    cross = remote(
        x_send.at[1 - here.xh], x_recv, tail_sem.at[0], tail_sem.at[1], here.other_tokens()
    )
    cross.start()
    if pairs > 1:
        units.wait_recv()
    unit_total = collect(unit_send, unit_recv)
    lane_gain[...] = row(k_gain)
    own_gain = lane_gain[:, own_lanes]
    cross.wait_recv()
    own_sum = x_send[here.xh] + x_recv[...]
    gained = own_sum[0] * own_gain
    statistic = jnp.sum(gained * near_unit, axis=-1, keepdims=True) / width
    multiply(jnp.concatenate([near_inverse * gained, own_sum[1]], axis=1), True)
    for q in range(pairs):
        span = slice(q * own_rows, (q + 1) * own_rows)
        grad_send[q, :, :middle] = fold(product[span, :])
        both = jnp.broadcast_to(statistic[span], (own_rows, LANES))
        grad_send[q, :, middle:] = jnp.concatenate([both, both], axis=0)
    grads = exchange(grad_send, grad_recv, 4)
    if pairs > 1:
        grads.wait_recv()
    total = collect(grad_send, grad_recv)
    own_grad = total[:, :middle] - total[:, middle : middle + 1] * unit_total

    def unfold(values):
        grad_ref[:, :middle] = values[:own_rows]
        grad_ref[:, middle:] = values[own_rows:]

    @pl.when(here.xl == 0)
    def _():
        unfold(own_grad)

    @pl.when(here.xl == 1)
    def _():
        z_send[...] = jnp.concatenate(
            [own_grad[:, : middle // 2], own_grad[:, middle // 2 :]], axis=0
        ).astype(BF16)
        for d in range(1, nz):
            remote(
                z_send, z_recv.at[here.z], tail_sem.at[6], tail_sem.at[7], here.at_z(d)
            ).start()
        ref = z_recv.at[pl.ds(0, nz - 1)]
        gathered = remote(ref, ref, tail_sem.at[6], tail_sem.at[7], here.sibling())
        gathered.wait_recv()
        others = z_recv[here.up_z(1)].astype(F32)
        for d in range(2, nz):
            others = others + z_recv[here.up_z(d)].astype(F32)
        few = 2 * own_rows
        unfold((own_grad + jnp.concatenate([others[:few], others[few:]], axis=1)) / nz)
        gathered.wait_send()

    cross.wait_send()
    if pairs > 1:
        units.wait_send()
        grads.wait_send()
    for i in range(pairs):
        to_sibling(i).wait_send()
        ref = y_send.at[:, :, rows_of(group(i), wide)]
        if i == pairs - 1:
            ref = y_send.at[:, pl.ds(0, quarter), rows_of(group(i), wide)]
        remote(ref, ref, y_send_sem.at[i], y_recv_sem.at[0], here.sibling()).wait_send()
    text_ring.finish()
    key_value.finish()
    for three in rings:
        for ring in three:
            ring.finish()


def hand_over(guided_in, grad_in, guided_ref, grad_ref):
    guided_ref[...] = guided_in[...]
    grad_ref[...] = grad_in[...]


def on_device(
    latents,
    prompt,
    null_embed,
    text_lengths,
    timesteps,
    head_mod,
    cross_gain,
    cross_bias,
    q_gain,
    k_gain,
    w_query,
    w_key,
    w_value,
    w_out,
    w_head,
    head_bias,
    target,
):
    nz = lax.axis_size("clip")
    ny = lax.axis_size("seq") // 4
    tokens = latents[0, 0]
    count, width = tokens.shape
    text_rows = null_embed.shape[0]
    rows = w_query.shape[1]
    patch = w_head.shape[1]
    heads = width // LANES
    pairs = ny // 2
    wide = width // pairs
    middle = width // 2
    half, quarter, eighth = text_rows // 2, text_rows // 4, text_rows // 8
    own_rows = text_rows // ny // 4
    dma = pltpu.SemaphoreType.DMA
    vmem = pl.BlockSpec(memory_space=pltpu.VMEM)
    smem = pl.BlockSpec(memory_space=pltpu.SMEM)
    guided, grad = pl.pallas_call(
        kernel,
        out_shape=(
            jax.ShapeDtypeStruct((patch, count), F32),
            jax.ShapeDtypeStruct((own_rows, width), F32),
        ),
        in_specs=[smem, smem]
        + [pl.BlockSpec(memory_space=pl.ANY)] * 4
        + [vmem] * 4
        + [pl.BlockSpec(memory_space=pl.ANY)] * 5
        + [vmem]
        + [pl.BlockSpec(memory_space=pl.ANY)],
        out_specs=(vmem, vmem),
        scratch_shapes=[
            pltpu.VMEM((count, width), BF16),
            pltpu.VMEM((text_rows, width), BF16),
            pltpu.VMEM(head_mod.shape, F32),
            pltpu.VMEM((patch, width), BF16),
            pltpu.VMEM((patch, count), BF16),
            pltpu.VMEM((2, ny, 2, 2, rows, width), BF16),
            pltpu.VMEM((2, 2, 2, 2, rows, width), BF16),
            pltpu.VMEM((ny, 2, 2, 2 * rows, text_rows), BF16),
            pltpu.VMEM((text_rows, width), BF16),
            pltpu.VMEM((width, LANES), F32),
            pltpu.VMEM((width, patch), BF16),
            pltpu.VMEM((width, count), BF16),
            pltpu.VMEM((width, count), BF16),
            pltpu.VMEM((width, count), F32),
            pltpu.VMEM((width, count), BF16),
            pltpu.VMEM((heads, text_rows, LANES), BF16),
            pltpu.VMEM((heads, text_rows, LANES), BF16),
            pltpu.VMEM((text_rows, width), BF16),
            pltpu.VMEM((heads, text_rows, count), F32),
            pltpu.VMEM((width, count), BF16),
            pltpu.VMEM((width, count), F32),
            pltpu.VMEM((width, count), BF16),
            pltpu.VMEM((width, count), F32),
            pltpu.VMEM((count, width), BF16),
            pltpu.VMEM((count, width), BF16),
            pltpu.VMEM((2, patch, count), F32),
            pltpu.VMEM((2, text_rows, width), F32),
            pltpu.VMEM((2, half, width), F32),
            pltpu.VMEM((2, half, width), BF16),
            pltpu.VMEM((ny, 2, quarter, wide), BF16),
            pltpu.VMEM((2, 2, eighth, wide), F32),
            pltpu.VMEM((2, eighth, wide), F32),
            pltpu.VMEM((eighth, width), F32),
            pltpu.VMEM((1, width), F32),
            pltpu.VMEM((pairs, 2 * own_rows, middle), F32),
            pltpu.VMEM((pairs, 2 * own_rows, middle), F32),
            pltpu.VMEM((pairs, 2 * own_rows, middle + LANES), F32),
            pltpu.VMEM((pairs, 2 * own_rows, middle + LANES), F32),
            pltpu.VMEM((4 * own_rows, middle // 2), BF16),
            pltpu.VMEM((nz, 4 * own_rows, middle // 2), BF16),
            dma((4 * ny,)),
            dma((3,)),
            dma((2, 4 * ny)),
            dma((2, 3)),
            dma((2, ny + 17)),
            dma((2, 4)),
            dma((2, ny + 16)),
            dma((2, 3)),
            dma((8,)),
            dma((3,)),
            dma((2,)),
            dma((2, pairs)),
            dma((ny,)),
            dma((pairs,)),
            dma((8,)),
            dma((14,)),
        ],
        compiler_params=pltpu.CompilerParams(
            collective_id=0, has_side_effects=True, vmem_limit_bytes=60 * 1024 * 1024
        ),
        cost_estimate=pl.CostEstimate(
            flops=8 * count * width * width, bytes_accessed=8 * count * width, transcendentals=0
        ),
    )(
        text_lengths,
        timesteps,
        tokens,
        prompt[0],
        null_embed,
        head_mod,
        cross_gain,
        cross_bias,
        q_gain,
        k_gain,
        w_query.T,
        w_key.T,
        w_value.T,
        w_out.T,
        w_head.T,
        head_bias,
        target[0].T,
    )
    guided, grad = pl.pallas_call(
        hand_over,
        out_shape=(
            jax.ShapeDtypeStruct((patch, count), F32),
            jax.ShapeDtypeStruct((own_rows, width), F32),
        ),
        in_specs=[vmem, vmem],
        out_specs=(vmem, vmem),
    )(guided, grad)
    return (guided.T[None], grad.reshape(1, 1, own_rows, width))


def solution(mesh):
    return jax.shard_map(
        on_device,
        mesh=mesh,
        in_specs=(
            P("clip", "guide", "seq", None),
            P("clip", None, None),
            P(),
            P("clip"),
            P("clip"),
            P(),
            P(),
            P(),
            P(),
            P(),
            P(None, "seq"),
            P(None, "seq"),
            P(None, "seq"),
            P(None, "seq"),
            P(),
            P(),
            P("clip", "seq", None),
        ),
        out_specs=(P("clip", "seq", None), P("clip", "guide", "seq", None)),
        check_vma=False,
    )
```

```python
import functools
import math

import jax
import jax.numpy as jnp
from jax import lax
from jax.experimental import pallas as pl
from jax.experimental.pallas import tpu as pltpu
from jax.sharding import PartitionSpec as P

LANES = 128
GUIDE_SCALE = 5.0
NORM_EPS = 1e-06
COLOURS = 4
MESH = pl.DeviceIdType.MESH
F32 = jnp.float32
BF16 = jnp.bfloat16
QUERY, OUT = range(2)


class Place:
    def __init__(self):
        seq = lax.axis_index("seq")
        self.nz = lax.axis_size("clip")
        self.ny = lax.axis_size("seq") // 4
        self.z = lax.axis_index("clip")
        self.xl = lax.axis_index("guide")
        self.y = lax.div(seq, 4)
        self.xh = lax.rem(lax.div(seq, 2), 2)
        self.c = lax.rem(seq, 2)
        self.x = self.xh * 2 + self.xl

    def device(self, z=None, y=None, xh=None, xl=None, c=None):
        z = self.z if z is None else z
        y = self.y if y is None else y
        xh = self.xh if xh is None else xh
        xl = self.xl if xl is None else xl
        c = self.c if c is None else c
        return {"clip": z, "guide": xl, "seq": y * 4 + xh * 2 + c}

    def up_y(self, by):
        return lax.rem(self.y + (by + self.ny), self.ny)

    def up_z(self, by):
        return lax.rem(self.z + (by + self.nz), self.nz)

    def up_x(self, by):
        return lax.rem(self.x + (by + 4), 4)

    def at_y(self, by):
        return self.device(y=self.up_y(by))

    def at_z(self, by):
        return self.device(z=self.up_z(by))

    def at_x(self, by):
        x = self.up_x(by)
        return self.device(xh=lax.div(x, 2), xl=lax.rem(x, 2))

    def sibling(self):
        return self.device(c=1 - self.c)

    def other_columns(self):
        return self.device(xh=1 - self.xh, xl=1 - self.xl)

    def other_tokens(self):
        return self.device(xh=1 - self.xh)

    def other_branch(self):
        return self.device(xl=1 - self.xl)


def remote(src, dst, send_sem, recv_sem, device):
    return pltpu.make_async_remote_copy(
        src_ref=src,
        dst_ref=dst,
        send_sem=send_sem,
        recv_sem=recv_sem,
        device_id=device,
        device_id_type=MESH,
    )


def reach(count):
    return {1: count // 2, -1: count - 1 - count // 2}


class RingY:
    def __init__(self, here, base, lanes, partner, recv, send):
        self.here, self.base, self.lanes, self.partner = here, base, lanes, partner
        self.recv, self.send = recv, send
        hops = reach(here.ny)
        self.hops = {(d, o): hops[d if o == 0 else -d] for d in (1, -1) for o in (0, 1)}
        self.rounds = here.ny // 2

    def chunk(self, y, xh, c):
        return self.base.at[y, xh, c, :, self.lanes]

    def copy(self, y, xh, c, lane, device):
        ref = self.chunk(y, xh, c)
        return remote(ref, ref, self.send.at[lane], self.recv.at[y * 4 + xh * 2 + c], device)

    def pass_on(self, y, other, step):
        here = self.here
        xh = here.xh if other == 0 else 1 - here.xh
        for d in (1, -1):
            if step == 0 and self.hops[d, other] > 0:
                self.copy(y, xh, here.c, 0, here.at_y(d)).start()
        self.copy(y, xh, here.c, 1, here.sibling()).start()

    def start(self):
        here = self.here
        self.copy(here.y, here.xh, here.c, 2, self.partner).start()
        self.pass_on(here.y, 0, 0)

    def over_x(self):
        here = self.here
        self.copy(here.y, 1 - here.xh, here.c, 2, self.partner).wait_recv()
        self.pass_on(here.y, 1, 0)

    def round(self, k):
        here = self.here
        for other in (0, 1):
            xh = here.xh if other == 0 else 1 - here.xh
            for d in (1, -1):
                if k <= self.hops[d, other]:
                    y = here.up_y(-d * k)
                    self.copy(y, xh, here.c, 0, here.at_y(d)).wait_recv()
                    if k < self.hops[d, other]:
                        self.copy(y, xh, here.c, 0, here.at_y(d)).start()
                    self.copy(y, xh, here.c, 1, here.sibling()).start()

    def from_sibling(self, y):
        here = self.here
        for xh in (0, 1):
            self.copy(y, xh, 1 - here.c, 1, here.sibling()).wait_recv()

    def finish(self):
        here = self.here
        for lane, ref in (
            (0, self.base.at[pl.ds(0, here.ny - 1), :, here.c, :, self.lanes]),
            (1, self.base.at[:, :, here.c, :, self.lanes]),
            (2, self.chunk(here.y, here.xh, here.c)),
        ):
            remote(ref, ref, self.send.at[lane], self.recv.at[0], here.sibling()).wait_send()


class RingFour:
    def __init__(self, here, base, first, width, axis, recv, send):
        self.here, self.base, self.first, self.width, self.axis = here, base, first, width, axis
        self.recv, self.send = recv, send
        self.hops = reach(here.ny)
        self.colour = here.x if axis == "x" else lax.rem(here.z, COLOURS)

    def part(self, index):
        return pl.ds(pl.multiple_of(self.first + index * self.width, LANES), self.width)

    def toward(self, d):
        return self.here.at_x(d) if self.axis == "x" else self.here.at_z(d)

    def along(self, y, d):
        here = self.here
        if self.axis == "x":
            ref = self.base.at[y, here.xh, here.c, :, self.part(here.xl)]
        else:
            ref = self.base.at[y, :, here.c, :, self.part(self.colour)]
        return remote(ref, ref, self.send.at[0], self.recv.at[y], here.at_y(d))

    def over(self, xh):
        here = self.here
        ref = self.base.at[here.y, xh, here.c, :, self.part(self.colour)]
        return remote(ref, ref, self.send.at[3], self.recv.at[here.ny + 16], here.other_columns())

    def half(self, colour, h, c, lane, device):
        size = self.here.ny // 2
        span = pl.ds(h * size, size)
        if self.axis == "x":
            ref = self.base.at[span, lax.div(colour, 2), c, :, self.part(lax.rem(colour, 2))]
        else:
            ref = self.base.at[span, :, c, :, self.part(colour)]
        slot = self.here.ny + (lane - 1) * 8 + colour * 2 + h
        return remote(ref, ref, self.send.at[lane], self.recv.at[slot], device)

    def begin_y(self):
        for d in (1, -1):
            if self.hops[d] > 0:
                self.along(self.here.y, d).start()

    def start(self):
        if self.axis == "x":
            self.begin_y()
        else:
            self.over(self.here.xh).start()

    def over_x(self):
        if self.axis == "z":
            self.over(1 - self.here.xh).wait_recv()
            self.begin_y()

    def round(self, k):
        for d in (1, -1):
            if k <= self.hops[d]:
                y = self.here.up_y(-d * k)
                self.along(y, d).wait_recv()
                if k < self.hops[d]:
                    self.along(y, d).start()

    def begin_four(self):
        here = self.here
        for h, d in ((0, 1), (1, -1), (1, 1), (0, -1)):
            self.half(self.colour, h, here.c, 1, self.toward(d)).start()
        for h in (0, 1):
            self.half(self.colour, h, here.c, 2, here.sibling()).start()

    def four(self, k):
        here = self.here
        if k == 1:
            came = ((0, 1, True), (1, -1, True), (1, 1, False), (0, -1, False))
        else:
            came = ((0, 2, False), (1, -2, False))
        for h, d, further in came:
            colour = lax.rem(self.colour + (COLOURS - d), COLOURS)
            toward = self.toward(1 if d > 0 else -1)
            self.half(colour, h, here.c, 1, toward).wait_recv()
            if further:
                self.half(colour, h, here.c, 1, toward).start()
            self.half(colour, h, here.c, 2, here.sibling()).start()

    def from_sibling(self):
        here = self.here
        for colour in range(COLOURS):
            for h in (0, 1):
                self.half(jnp.int32(colour), h, 1 - here.c, 2, here.sibling()).wait_recv()

    def finish(self):
        here = self.here
        xh = 0 if self.axis == "x" else slice(None)
        ends = [
            (0, self.base.at[pl.ds(0, here.ny - 1), xh, here.c, :, pl.ds(0, self.width)]),
            (1, self.base.at[:, xh, here.c, :, pl.ds(0, 3 * self.width)]),
            (2, self.base.at[:, xh, here.c, :, pl.ds(0, 4 * self.width)]),
        ]
        if self.axis == "z":
            ends.append((3, self.base.at[0, 0, here.c, :, pl.ds(0, self.width)]))
        for lane, ref in ends:
            remote(ref, ref, self.send.at[lane], self.recv.at[0], here.sibling()).wait_send()


class Pair:
    def __init__(self, here, base, recv, send):
        self.here, self.base, self.recv, self.send = here, base, recv, send
        self.parity = lax.rem(here.y, 2)
        self.other_y = here.device(y=here.y + 1 - 2 * self.parity)

    def copy(self, parity, xh, c, lane, device):
        ref = self.base.at[:, parity, xh, c]
        slot = parity * 4 + xh * 2 + c
        return remote(ref, ref, self.send.at[lane], self.recv.at[slot], device)

    def start(self):
        here = self.here
        self.copy(self.parity, here.xh, here.c, 2, here.other_columns()).start()
        self.copy(self.parity, here.xh, here.c, 1, here.sibling()).start()

    def over_x(self):
        here = self.here
        self.copy(self.parity, 1 - here.xh, here.c, 2, here.other_columns()).wait_recv()
        self.copy(self.parity, 1 - here.xh, here.c, 1, here.sibling()).start()

    def begin_y(self):
        here = self.here
        for xh in (here.xh, 1 - here.xh):
            self.copy(self.parity, xh, here.c, 0, self.other_y).start()

    def over_y(self):
        here = self.here
        for xh in (here.xh, 1 - here.xh):
            self.copy(1 - self.parity, xh, here.c, 0, self.other_y).wait_recv()
            self.copy(1 - self.parity, xh, here.c, 1, here.sibling()).start()

    def from_sibling(self):
        here = self.here
        for parity in (0, 1):
            for xh in (0, 1):
                self.copy(parity, xh, 1 - here.c, 1, here.sibling()).wait_recv()

    def finish(self):
        here = self.here
        for lane, ref in (
            (0, self.base.at[:, 0, :, here.c]),
            (1, self.base.at[:, :, :, here.c]),
            (2, self.base.at[:, 0, 0, here.c]),
        ):
            remote(ref, ref, self.send.at[lane], self.recv.at[0], here.sibling()).wait_send()


def down(values):
    return jnp.sum(values, axis=0, keepdims=True)


def gather_down(values):
    return jnp.sum(values.reshape(values.shape[0] // 8, 8, values.shape[1]), axis=0)


def dot(left, right):
    return jnp.dot(left, right, preferred_element_type=F32)


def dot_lanes(left, right):
    return lax.dot_general(left, right, (((1,), (1,)), ((), ())), preferred_element_type=F32)


def row(ref):
    return ref[...].reshape(1, ref.shape[0])


def rows_of(index, size):
    return pl.ds(pl.multiple_of(index * size, size), size)


def log2(count):
    return count.bit_length() - 1


def kernel(
    length_ref,
    step_ref,
    latents_in,
    prompt_in,
    null_in,
    head_mod_in,
    cross_gain,
    cross_bias,
    q_gain,
    k_gain,
    w_query,
    w_key,
    w_value,
    w_out,
    w_head_in,
    head_bias,
    target_in,
    guided_ref,
    grad_ref,
    latents,
    either,
    head_mod,
    w_head,
    target,
    weights,
    pair_weights,
    text,
    context,
    columns,
    w_head_rows,
    tokens,
    cross_in,
    query_raw,
    query,
    key_normed,
    value_rows,
    key_raw,
    attn,
    attended,
    after,
    head_in,
    d_unit,
    d_after,
    d_attended,
    noise,
    d_text,
    d_sibling,
    y_send,
    y_recv,
    product,
    lane_gain,
    unit_send,
    unit_recv,
    grad_send,
    grad_recv,
    z_send,
    z_recv,
    text_recv,
    text_send,
    recv_y,
    send_y,
    recv_z,
    send_z,
    recv_x,
    send_x,
    pair_recv,
    pair_send,
    swap_sem,
    sibling_sem,
    y_recv_sem,
    y_send_sem,
    tail_sem,
    load_sem,
):
    here = Place()
    ny, nz = here.ny, here.nz
    rows, width = w_query.shape
    token_count = latents_in.shape[0]
    text_rows = prompt_in.shape[0]
    patch = w_head_in.shape[0]
    heads = width // LANES
    blocks = width // LANES
    token_blocks = token_count // LANES
    band = 4 * rows
    root = 1.0 / math.sqrt(LANES)
    pairs = ny // 2
    share = text_rows // ny
    own_rows = share // 4
    half, quarter, eighth = text_rows // 2, text_rows // 4, text_rows // 8
    wide = width // pairs
    middle = width // 2
    parity = lax.rem(here.y, 2)
    pair = lax.div(here.y, 2)

    partners = [here.sibling(), here.other_columns(), here.other_tokens(), here.other_branch()]
    partners += [here.at_y(d) for d in range(1, ny)] + [here.at_z(d) for d in range(1, nz)]
    partners += [here.device(y=here.up_y(d), xh=1 - here.xh) for d in range(1, ny)]
    barrier = pltpu.get_barrier_semaphore()
    for device in partners:
        pl.semaphore_signal(barrier, inc=1, device_id=device, device_id_type=MESH)

    x_part = LANES * (2 if blocks >= 12 else 1)
    x_first = width - 2 * x_part
    z_first = x_first - COLOURS * LANES
    y_lanes = pl.ds(0, z_first)
    loads = []

    def load(src, dst):
        loads.append(pltpu.make_async_copy(src, dst, load_sem.at[len(loads)]))
        loads[-1].start()

    for index, own in ((QUERY, w_query), (OUT, w_out)):
        for lanes in (
            y_lanes,
            pl.ds(pl.multiple_of(z_first + lax.rem(here.z, COLOURS) * LANES, LANES), LANES),
            pl.ds(pl.multiple_of(x_first + here.xl * x_part, LANES), x_part),
        ):
            load(own.at[:, lanes], weights.at[index, here.y, here.xh, here.c, :, lanes])
    for index, own in enumerate((w_key, w_value)):
        load(own, pair_weights.at[index, parity, here.xh, here.c])
    for src, dst in (
        (head_mod_in, head_mod),
        (w_head_in, w_head),
        (latents_in, latents),
        (target_in, target),
    ):
        load(src, dst)
    text_load = load_sem.at[len(loads)]

    @pl.when(here.xl == 0)
    def _():
        pltpu.make_async_copy(prompt_in, either, text_load).start()

    @pl.when(here.xl == 1)
    def _():
        pltpu.make_async_copy(null_in, either, text_load).start()

    for copy in loads[:6]:
        copy.wait()
    pl.semaphore_wait(barrier, len(partners))

    text_ring = RingY(here, text, slice(None), here.other_tokens(), text_recv, text_send)
    rings = []
    for index in (QUERY, OUT):
        base = weights.at[index]
        rings.append(
            (
                RingFour(here, base, x_first, x_part, "x", recv_x.at[index], send_x.at[index]),
                RingFour(here, base, z_first, LANES, "z", recv_z.at[index], send_z.at[index]),
                RingY(
                    here, base, y_lanes, here.other_columns(), recv_y.at[index], send_y.at[index]
                ),
            )
        )
    key_value = Pair(here, pair_weights, pair_recv, pair_send)

    x_query, z_query, y_query = rings[QUERY]
    x_out, z_out, y_out = rings[OUT]

    def small_round(index, k):
        for ring in rings[index][:2]:
            ring.round(k)
            if k == pairs:
                ring.begin_four()

    def go_four(index, k):
        for ring in rings[index][:2]:
            ring.four(k)

    def all_here(index):
        for ring in rings[index][:2]:
            ring.from_sibling()
        for y in range(ny):
            rings[index][2].from_sibling(y)

    for ring in rings[QUERY]:
        ring.start()

    def text_row(index):
        place = lax.shift_right_logical(index, log2(own_rows)) & (pairs - 1)
        place = place * 2 + (lax.shift_right_logical(index, log2(quarter)) & 1)
        place = place * 2 + (lax.shift_right_logical(index, log2(eighth)) & 1)
        place = place * 2 + (lax.shift_right_logical(index, log2(half)) & 1)
        return place * own_rows + (index & (own_rows - 1))

    square_iota = functools.partial(lax.broadcasted_iota, jnp.int32, (text_rows, text_rows))
    order = jnp.where(text_row(square_iota(0)) == square_iota(1), 1.0, 0.0).astype(BF16)

    pltpu.make_async_copy(prompt_in, either, text_load).wait()
    context[...] = dot(order, either[...]).astype(BF16)
    for copy in loads[6:8]:
        copy.wait()
    own_key = pair_weights[0, parity, here.xh, here.c]
    own_value = pair_weights[1, parity, here.xh, here.c]
    text[here.y, here.xh, here.c, :rows] = dot_lanes(own_key, context[...]).astype(BF16)
    text[here.y, here.xh, here.c, rows:] = dot_lanes(own_value, context[...]).astype(BF16)
    text_ring.start()
    z_query.over_x()
    y_query.over_x()

    for copy in loads[8:]:
        copy.wait()
    modulation = head_mod[step_ref[0]]
    stack = jnp.concatenate(
        [
            row(cross_gain),
            row(cross_bias),
            row(q_gain),
            row(k_gain),
            1.0 + modulation[1:2],
            modulation[0:1],
            jnp.concatenate([row(head_bias), jnp.zeros((1, width - patch), F32)], axis=1),
            jnp.zeros((LANES - 7, width), F32),
        ],
        axis=0,
    )
    for block in range(blocks):
        lanes = slice(block * LANES, (block + 1) * LANES)
        columns[lanes, :] = stack[:, lanes].T
        w_head_rows[lanes, :] = w_head[:, lanes].T

    def turn(block, total):
        at = rows_of(block, LANES)
        for t in range(token_blocks):
            lanes = slice(t * LANES, (t + 1) * LANES)
            tokens[at, lanes] = latents[lanes, at].T
        return total + gather_down(tokens[at, :].astype(F32))

    zero_row = jnp.zeros((8, token_count), F32)
    unroll = 4 if blocks % 4 == 0 else 1
    mean = down(lax.fori_loop(0, blocks, turn, zero_row, unroll=unroll)) / width

    small_round(QUERY, 1)
    text_ring.over_x()
    x_out.start()
    z_out.start()

    def spread(block, total):
        centred = tokens[rows_of(block, LANES), :].astype(F32) - mean
        return total + gather_down(centred * centred)

    variance = down(lax.fori_loop(0, blocks, spread, zero_row, unroll=unroll)) / width
    inverse = lax.rsqrt(variance + NORM_EPS)

    def normalise(block, carry):
        at = rows_of(block, LANES)
        unit = (tokens[at, :].astype(F32) - mean) * inverse
        cross_in[at, :] = (unit * columns[at, 0:1] + columns[at, 1:2]).astype(BF16)
        return carry

    y_query.round(1)
    z_out.over_x()
    if pairs > 1:
        small_round(QUERY, 2)
    text_ring.round(1)
    lax.fori_loop(0, blocks, normalise, 0, unroll=unroll)

    y_out.start()
    key_value.start()
    for k in range(3, pairs + 1):
        small_round(QUERY, k)
        small_round(OUT, k - 2)
        if k == 3:
            y_out.over_x()
            y_query.round(2)
            text_ring.round(2)
    if pairs < 3:
        y_out.over_x()
        if pairs > 1:
            y_query.round(2)
            text_ring.round(2)
    if pairs > 2:
        y_query.round(3)
        text_ring.round(3)
    if pairs > 1:
        small_round(OUT, pairs - 1)
        y_out.round(1)
    go_four(QUERY, 1)
    small_round(OUT, pairs)
    if pairs > 3:
        text_ring.round(4)
        y_query.round(4)
    if pairs > 1:
        y_out.round(2)
    else:
        y_out.round(1)
    go_four(QUERY, 2)
    key_value.over_x()
    for y in range(ny):
        text_ring.from_sibling(y)

    keys = text[:, :, :, :rows, :].reshape(width, text_rows).astype(F32)
    values = text[:, :, :, rows:, :].reshape(width, text_rows).astype(F32)
    key_inverse = lax.rsqrt(down(keys * keys) / width + NORM_EPS)
    for h in range(heads):
        lanes = slice(h * LANES, (h + 1) * LANES)
        one = keys[lanes]
        key_raw[:, lanes] = one.T.astype(BF16)
        key_normed[h] = (one * key_inverse * columns[lanes, 3:4]).T.astype(BF16)
        value_rows[h] = values[lanes].T.astype(BF16)

    go_four(OUT, 1)
    all_here(QUERY)

    def project(i, total):
        raw = dot(weights[QUERY, pl.ds(i * 2, 2)].reshape(2 * band, width), cross_in[...])
        query_raw[rows_of(i, 2 * band), :] = raw
        return total + gather_down(raw * raw)

    square = lax.fori_loop(0, pairs // 2, project, zero_row)
    if pairs > 2:
        y_out.round(3)
    key_value.begin_y()
    square = lax.fori_loop(pairs // 2, pairs, project, square)
    query_inverse = lax.rsqrt(down(square) / width + NORM_EPS)

    length = here.xl * text_rows + (1 - here.xl) * length_ref[0]
    visible = text_row(lax.broadcasted_iota(jnp.int32, (text_rows, token_count), 0)) < length

    def attend(h, carry):
        at = rows_of(h, LANES)
        query[at, :] = (query_raw[at, :] * query_inverse * columns[at, 2:3]).astype(BF16)
        scores = dot(key_normed[h], query[at, :]) * root
        masked = jnp.where(visible, scores, -1e30)
        terms = jnp.where(visible, jnp.exp(masked - jnp.max(masked, axis=0, keepdims=True)), 0.0)
        shares = terms / down(terms)
        attn[h] = shares
        attended[at, :] = lax.dot_general(
            value_rows[h],
            shares.astype(BF16),
            (((0,), (0,)), ((), ())),
            preferred_element_type=F32,
        ).astype(BF16)
        return carry

    lax.fori_loop(0, heads // 4, attend, 0, unroll=True)
    go_four(OUT, 2)
    lax.fori_loop(heads // 4, heads // 2, attend, 0, unroll=True)
    if pairs > 3:
        y_out.round(4)
    lax.fori_loop(heads // 2, heads, attend, 0, unroll=True)
    all_here(OUT)

    cutting = (token_blocks + 1) // 2 * LANES
    parts = [slice(0, cutting)] + ([slice(cutting, token_count)] if cutting < token_count else [])

    def swap(number, branch):
        ref = noise.at[branch, :, parts[number]]
        return remote(
            ref, ref, swap_sem.at[0, number], swap_sem.at[1, number], here.other_branch()
        )

    def head_forward(number):
        lanes = parts[number]
        start = jnp.zeros((8, lanes.stop - lanes.start), F32)

        def project_out(i, total):
            at = rows_of(i, 2 * band)
            matrix = weights[OUT, pl.ds(i * 2, 2)].reshape(2 * band, width)
            rows_after = dot(matrix, attended[:, lanes]) + tokens[at, lanes].astype(F32)
            after[at, lanes] = rows_after
            return total + gather_down(rows_after)

        head_mean = down(lax.fori_loop(0, pairs, project_out, start)) / width

        def head_spread(block, total):
            centred = after[rows_of(block, LANES), lanes] - head_mean
            return total + gather_down(centred * centred)

        variance = down(lax.fori_loop(0, blocks, head_spread, start, unroll=unroll)) / width
        head_inverse = lax.rsqrt(variance + NORM_EPS)

        def modulate(block, carry):
            at = rows_of(block, LANES)
            unit = (after[at, lanes] - head_mean) * head_inverse
            head_in[at, lanes] = (unit * columns[at, 4:5] + columns[at, 5:6]).astype(BF16)
            return carry

        lax.fori_loop(0, blocks, modulate, 0, unroll=unroll)
        noise[here.xl, :, lanes] = dot(w_head[...], head_in[:, lanes]) + columns[:patch, 6:7]
        swap(number, here.xl).start()
        return head_mean, head_inverse

    factor = GUIDE_SCALE - (2.0 * GUIDE_SCALE - 1.0) * here.xl.astype(F32)

    def head_backward(number, head_mean, head_inverse):
        lanes = parts[number]
        start = jnp.zeros((8, lanes.stop - lanes.start), F32)
        swap(number, 1 - here.xl).wait_recv()
        cond, null = noise[0, :, lanes], noise[1, :, lanes]
        guided = null + GUIDE_SCALE * (cond - null)
        guided_ref[:, lanes] = guided
        d_noise = (factor * (guided - target[:, lanes].astype(F32))).astype(BF16)

        def head_back(block, sums):
            at = rows_of(block, LANES)
            unit = (after[at, lanes] - head_mean) * head_inverse
            part_unit = dot(w_head_rows[at, :], d_noise) * columns[at, 4:5]
            d_unit[at, lanes] = part_unit
            return (sums[0] + gather_down(part_unit), sums[1] + gather_down(part_unit * unit))

        first_sum, second_sum = lax.fori_loop(
            0, blocks, head_back, (start, start), unroll=unroll
        )
        first_mean, second_mean = down(first_sum) / width, down(second_sum) / width

        def norm_back(block, carry):
            at = rows_of(block, LANES)
            unit = (after[at, lanes] - head_mean) * head_inverse
            grads = (head_inverse * (d_unit[at, lanes] - first_mean - unit * second_mean)).astype(
                BF16
            )
            for t in range(lanes.start, lanes.stop, LANES):
                d_after[t : t + LANES, at] = grads[:, t - lanes.start : t - lanes.start + LANES].T
            return carry

        lax.fori_loop(0, blocks, norm_back, 0, unroll=unroll)

    stats = [head_forward(number) for number in range(len(parts))]
    def fold(values):
        return jnp.concatenate([values[:, :middle], values[:, middle:]], axis=0)

    def split(values):
        high = values.astype(BF16)
        low = (values - high.astype(F32)).astype(BF16)
        return jnp.concatenate([high, low], axis=0)

    first_row = here.c * half + parity * quarter + here.xh * eighth
    own_span = pl.ds(pl.multiple_of(first_row, eighth), eighth)
    own_lanes = rows_of(pair, wide)
    near = key_raw[own_span, :].astype(F32)
    near_inverse = lax.rsqrt(jnp.mean(near * near, axis=-1, keepdims=True) + NORM_EPS)
    near_unit = key_raw[own_span, own_lanes].astype(F32) * near_inverse

    def multiply(left, lead):
        both = split(left)

        def columns_of(block, carry):
            at = rows_of(block, 2 * LANES)
            if lead:
                matrix = pair_weights[:, :, :, :, :, at].reshape(2 * wide, 2 * LANES)
            else:
                matrix = pair_weights[0, :, :, :, :, at].reshape(wide, 2 * LANES)
            result = dot(both, matrix)
            product[:, at] = result[:eighth] + result[eighth:]
            return carry

        lax.fori_loop(0, blocks // 2, columns_of, 0)

    def exchange(send, recv, lane):
        for d in range(1, pairs):
            q = lax.rem(pair + d, pairs)
            remote(
                send.at[q],
                recv.at[pair],
                tail_sem.at[lane],
                tail_sem.at[lane + 1],
                here.device(y=q * 2 + parity),
            ).start()
        ref = recv.at[pl.ds(0, max(1, pairs - 1))]
        return remote(ref, ref, tail_sem.at[lane], tail_sem.at[lane + 1], here.sibling())

    def collect(send, recv):
        total = send[pair]
        for d in range(1, pairs):
            total = total + recv[lax.rem(pair + d, pairs)]
        return total

    for number, (head_mean, head_inverse) in enumerate(stats):
        head_backward(number, head_mean, head_inverse)

    def out_back(block, carry):
        at = rows_of(block, 2 * LANES)
        matrix = weights[OUT, :, :, :, :, at].reshape(width, 2 * LANES)
        d_attended[:, at] = dot(d_after[...], matrix).astype(BF16)
        return carry

    lax.fori_loop(0, blocks // 2, out_back, 0, unroll=2)
    key_value.over_y()

    def attend_back(h, carry):
        at = rows_of(h, LANES)
        grads = d_attended[:, at]
        shares = attn[h]
        d_shares = dot_lanes(value_rows[h], grads)
        d_scores = shares * (d_shares - down(d_shares * shares))
        d_text[0, :, at] = dot_lanes((d_scores * root).astype(BF16), query[at, :])
        d_text[1, :, at] = dot(shares.astype(BF16), grads)
        return carry

    def group(i):
        return lax.rem(pair + (i + 1), pairs)

    def core_span(c):
        return pl.ds(pl.multiple_of(c * half, half), half)

    def to_sibling(i):
        lanes = rows_of(group(i), wide)
        return remote(
            d_text.at[:, core_span(1 - here.c), lanes],
            d_sibling.at[:, :, lanes],
            sibling_sem.at[0, i],
            sibling_sem.at[1, i],
            here.sibling(),
        )

    def to_row(i, odd, xh):
        lanes = rows_of(group(i), wide)
        span = pl.ds(pl.multiple_of(odd * quarter + xh * eighth, eighth), eighth)
        return remote(
            y_send.at[:, span, lanes],
            y_recv.at[here.y, here.xh],
            y_send_sem.at[i],
            y_recv_sem.at[here.y * 2 + here.xh],
            here.device(y=group(i) * 2 + odd, xh=xh),
        )

    def sum_cores(i):
        lanes = rows_of(group(i), wide)
        to_sibling(i).wait_recv()
        both = d_text[:, core_span(here.c), lanes] + d_sibling[:, :, lanes]
        y_send[:, :, lanes] = both.astype(BF16)
        if i < pairs - 1:
            for odd in (0, 1):
                for xh in (0, 1):
                    to_row(i, jnp.int32(odd), jnp.int32(xh)).start()
        else:
            to_row(i, 1 - parity, here.xh).start()
            to_row(i, 1 - parity, 1 - here.xh).start()
            to_row(i, parity, 1 - here.xh).start()
            d_sibling[:, :, lanes] = both

    for i in range(pairs):
        for j in range(heads // pairs):
            attend_back(group(i) * (heads // pairs) + j, 0)
        to_sibling(i).start()
        if i > 0:
            sum_cores(i - 1)
        if i == pairs - 2 or pairs == 1:
            key_value.from_sibling()
            multiply(near_unit * near_inverse, False)
            for q in range(pairs):
                unit_send[q] = fold(product[q * own_rows : (q + 1) * own_rows, :])
            units = exchange(unit_send, unit_recv, 2)
    sum_cores(pairs - 1)

    eighth_span = pl.ds(
        pl.multiple_of(parity * quarter + here.xh * eighth, eighth), eighth
    )
    own_sum = d_sibling[:, eighth_span, own_lanes]
    near_y = here.y + 1 - 2 * parity
    sources = [(lax.rem(pair * 2 + d, ny), xh) for d in range(2, ny) for xh in (0, 1)]
    sources += [(here.y, 1 - here.xh), (near_y, here.xh), (near_y, 1 - here.xh)]
    for y, xh in sources:
        ref = y_recv.at[y, xh]
        remote(
            ref, ref, y_send_sem.at[0], y_recv_sem.at[y * 2 + xh], here.sibling()
        ).wait_recv()
        own_sum = own_sum + y_recv[y, xh].astype(F32)
    if pairs > 1:
        units.wait_recv()
    unit_total = collect(unit_send, unit_recv)
    lane_gain[...] = row(k_gain)
    own_gain = lane_gain[:, own_lanes]
    gained = own_sum[0] * own_gain
    statistic = jnp.sum(gained * near_unit, axis=-1, keepdims=True) / width
    multiply(jnp.concatenate([near_inverse * gained, own_sum[1]], axis=1), True)
    for q in range(pairs):
        span = slice(q * own_rows, (q + 1) * own_rows)
        grad_send[q, :, :middle] = fold(product[span, :])
        both = jnp.broadcast_to(statistic[span], (own_rows, LANES))
        grad_send[q, :, middle:] = jnp.concatenate([both, both], axis=0)
    grads = exchange(grad_send, grad_recv, 4)
    if pairs > 1:
        grads.wait_recv()
    total = collect(grad_send, grad_recv)
    own_grad = total[:, :middle] - total[:, middle : middle + 1] * unit_total

    def unfold(values):
        grad_ref[:, :middle] = values[:own_rows]
        grad_ref[:, middle:] = values[own_rows:]

    @pl.when(here.xl == 0)
    def _():
        unfold(own_grad)

    @pl.when(here.xl == 1)
    def _():
        z_send[...] = jnp.concatenate(
            [own_grad[:, : middle // 2], own_grad[:, middle // 2 :]], axis=0
        ).astype(BF16)
        for d in range(1, nz):
            remote(
                z_send, z_recv.at[here.z], tail_sem.at[6], tail_sem.at[7], here.at_z(d)
            ).start()
        ref = z_recv.at[pl.ds(0, nz - 1)]
        gathered = remote(ref, ref, tail_sem.at[6], tail_sem.at[7], here.sibling())
        gathered.wait_recv()
        others = z_recv[here.up_z(1)].astype(F32)
        for d in range(2, nz):
            others = others + z_recv[here.up_z(d)].astype(F32)
        few = 2 * own_rows
        unfold((own_grad + jnp.concatenate([others[:few], others[few:]], axis=1)) / nz)
        gathered.wait_send()

    for number in range(len(parts)):
        swap(number, here.xl).wait_send()
    if pairs > 1:
        units.wait_send()
        grads.wait_send()
    for i in range(pairs):
        to_sibling(i).wait_send()
        ref = y_send.at[:, :, rows_of(group(i), wide)]
        if i == pairs - 1:
            ref = y_send.at[:, pl.ds(0, 3 * eighth), rows_of(group(i), wide)]
        remote(ref, ref, y_send_sem.at[i], y_recv_sem.at[0], here.sibling()).wait_send()
    text_ring.finish()
    key_value.finish()
    for three in rings:
        for ring in three:
            ring.finish()


def hand_over(guided_in, grad_in, guided_ref, grad_ref):
    guided_ref[...] = guided_in[...]
    grad_ref[...] = grad_in[...]


def on_device(
    latents,
    prompt,
    null_embed,
    text_lengths,
    timesteps,
    head_mod,
    cross_gain,
    cross_bias,
    q_gain,
    k_gain,
    w_query,
    w_key,
    w_value,
    w_out,
    w_head,
    head_bias,
    target,
):
    nz = lax.axis_size("clip")
    ny = lax.axis_size("seq") // 4
    tokens = latents[0, 0]
    count, width = tokens.shape
    text_rows = null_embed.shape[0]
    rows = w_query.shape[1]
    patch = w_head.shape[1]
    heads = width // LANES
    pairs = ny // 2
    wide = width // pairs
    middle = width // 2
    half, quarter, eighth = text_rows // 2, text_rows // 4, text_rows // 8
    own_rows = text_rows // ny // 4
    dma = pltpu.SemaphoreType.DMA
    vmem = pl.BlockSpec(memory_space=pltpu.VMEM)
    smem = pl.BlockSpec(memory_space=pltpu.SMEM)
    guided, grad = pl.pallas_call(
        kernel,
        out_shape=(
            jax.ShapeDtypeStruct((patch, count), F32),
            jax.ShapeDtypeStruct((own_rows, width), F32),
        ),
        in_specs=[smem, smem]
        + [pl.BlockSpec(memory_space=pl.ANY)] * 4
        + [vmem] * 4
        + [pl.BlockSpec(memory_space=pl.ANY)] * 5
        + [vmem]
        + [pl.BlockSpec(memory_space=pl.ANY)],
        out_specs=(vmem, vmem),
        scratch_shapes=[
            pltpu.VMEM((count, width), BF16),
            pltpu.VMEM((text_rows, width), BF16),
            pltpu.VMEM(head_mod.shape, F32),
            pltpu.VMEM((patch, width), BF16),
            pltpu.VMEM((patch, count), BF16),
            pltpu.VMEM((2, ny, 2, 2, rows, width), BF16),
            pltpu.VMEM((2, 2, 2, 2, rows, width), BF16),
            pltpu.VMEM((ny, 2, 2, 2 * rows, text_rows), BF16),
            pltpu.VMEM((text_rows, width), BF16),
            pltpu.VMEM((width, LANES), F32),
            pltpu.VMEM((width, patch), BF16),
            pltpu.VMEM((width, count), BF16),
            pltpu.VMEM((width, count), BF16),
            pltpu.VMEM((width, count), F32),
            pltpu.VMEM((width, count), BF16),
            pltpu.VMEM((heads, text_rows, LANES), BF16),
            pltpu.VMEM((heads, text_rows, LANES), BF16),
            pltpu.VMEM((text_rows, width), BF16),
            pltpu.VMEM((heads, text_rows, count), F32),
            pltpu.VMEM((width, count), BF16),
            pltpu.VMEM((width, count), F32),
            pltpu.VMEM((width, count), BF16),
            pltpu.VMEM((width, count), F32),
            pltpu.VMEM((count, width), BF16),
            pltpu.VMEM((count, width), BF16),
            pltpu.VMEM((2, patch, count), F32),
            pltpu.VMEM((2, text_rows, width), F32),
            pltpu.VMEM((2, half, width), F32),
            pltpu.VMEM((2, half, width), BF16),
            pltpu.VMEM((ny, 2, 2, eighth, wide), BF16),
            pltpu.VMEM((eighth, width), F32),
            pltpu.VMEM((1, width), F32),
            pltpu.VMEM((pairs, 2 * own_rows, middle), F32),
            pltpu.VMEM((pairs, 2 * own_rows, middle), F32),
            pltpu.VMEM((pairs, 2 * own_rows, middle + LANES), F32),
            pltpu.VMEM((pairs, 2 * own_rows, middle + LANES), F32),
            pltpu.VMEM((4 * own_rows, middle // 2), BF16),
            pltpu.VMEM((nz, 4 * own_rows, middle // 2), BF16),
            dma((4 * ny,)),
            dma((3,)),
            dma((2, 4 * ny)),
            dma((2, 3)),
            dma((2, ny + 17)),
            dma((2, 4)),
            dma((2, ny + 16)),
            dma((2, 3)),
            dma((8,)),
            dma((3,)),
            dma((2, 2)),
            dma((2, pairs)),
            dma((2 * ny,)),
            dma((pairs,)),
            dma((8,)),
            dma((14,)),
        ],
        compiler_params=pltpu.CompilerParams(
            collective_id=0, has_side_effects=True, vmem_limit_bytes=60 * 1024 * 1024
        ),
        cost_estimate=pl.CostEstimate(
            flops=8 * count * width * width, bytes_accessed=8 * count * width, transcendentals=0
        ),
    )(
        text_lengths,
        timesteps,
        tokens,
        prompt[0],
        null_embed,
        head_mod,
        cross_gain,
        cross_bias,
        q_gain,
        k_gain,
        w_query.T,
        w_key.T,
        w_value.T,
        w_out.T,
        w_head.T,
        head_bias,
        target[0].T,
    )
    guided, grad = pl.pallas_call(
        hand_over,
        out_shape=(
            jax.ShapeDtypeStruct((patch, count), F32),
            jax.ShapeDtypeStruct((own_rows, width), F32),
        ),
        in_specs=[vmem, vmem],
        out_specs=(vmem, vmem),
    )(guided, grad)
    return (guided.T[None], grad.reshape(1, 1, own_rows, width))


def solution(mesh):
    return jax.shard_map(
        on_device,
        mesh=mesh,
        in_specs=(
            P("clip", "guide", "seq", None),
            P("clip", None, None),
            P(),
            P("clip"),
            P("clip"),
            P(),
            P(),
            P(),
            P(),
            P(),
            P(None, "seq"),
            P(None, "seq"),
            P(None, "seq"),
            P(None, "seq"),
            P(),
            P(),
            P("clip", "seq", None),
        ),
        out_specs=(P("clip", "seq", None), P("clip", "guide", "seq", None)),
        check_vma=False,
    )
```

```python
import functools
import math

import jax
import jax.numpy as jnp
from jax import lax
from jax.experimental import pallas as pl
from jax.experimental.pallas import tpu as pltpu
from jax.sharding import PartitionSpec as P

LANES = 128
GUIDE_SCALE = 5.0
NORM_EPS = 1e-06
COLOURS = 4
MESH = pl.DeviceIdType.MESH
F32 = jnp.float32
BF16 = jnp.bfloat16
QUERY, OUT = range(2)


class Place:
    def __init__(self):
        seq = lax.axis_index("seq")
        self.nz = lax.axis_size("clip")
        self.ny = lax.axis_size("seq") // 4
        self.z = lax.axis_index("clip")
        self.xl = lax.axis_index("guide")
        self.y = lax.div(seq, 4)
        self.xh = lax.rem(lax.div(seq, 2), 2)
        self.c = lax.rem(seq, 2)
        self.x = self.xh * 2 + self.xl

    def device(self, z=None, y=None, xh=None, xl=None, c=None):
        z = self.z if z is None else z
        y = self.y if y is None else y
        xh = self.xh if xh is None else xh
        xl = self.xl if xl is None else xl
        c = self.c if c is None else c
        return {"clip": z, "guide": xl, "seq": y * 4 + xh * 2 + c}

    def up_y(self, by):
        return lax.rem(self.y + (by + self.ny), self.ny)

    def up_z(self, by):
        return lax.rem(self.z + (by + self.nz), self.nz)

    def up_x(self, by):
        return lax.rem(self.x + (by + 4), 4)

    def at_y(self, by):
        return self.device(y=self.up_y(by))

    def at_z(self, by):
        return self.device(z=self.up_z(by))

    def at_x(self, by):
        x = self.up_x(by)
        return self.device(xh=lax.div(x, 2), xl=lax.rem(x, 2))

    def sibling(self):
        return self.device(c=1 - self.c)

    def other_columns(self):
        return self.device(xh=1 - self.xh, xl=1 - self.xl)

    def other_tokens(self):
        return self.device(xh=1 - self.xh)

    def other_branch(self):
        return self.device(xl=1 - self.xl)


def remote(src, dst, send_sem, recv_sem, device):
    return pltpu.make_async_remote_copy(
        src_ref=src,
        dst_ref=dst,
        send_sem=send_sem,
        recv_sem=recv_sem,
        device_id=device,
        device_id_type=MESH,
    )


def reach(count):
    return {1: count // 2, -1: count - 1 - count // 2}


class RingY:
    def __init__(self, here, base, lanes, partner, recv, send):
        self.here, self.base, self.lanes, self.partner = here, base, lanes, partner
        self.recv, self.send = recv, send
        hops = reach(here.ny)
        self.hops = {(d, o): hops[d if o == 0 else -d] for d in (1, -1) for o in (0, 1)}
        self.rounds = here.ny // 2

    def chunk(self, y, xh, c):
        return self.base.at[y, xh, c, :, self.lanes]

    def copy(self, y, xh, c, lane, device):
        ref = self.chunk(y, xh, c)
        return remote(ref, ref, self.send.at[lane], self.recv.at[y * 4 + xh * 2 + c], device)

    def pass_on(self, y, other, step):
        here = self.here
        xh = here.xh if other == 0 else 1 - here.xh
        for d in (1, -1):
            if step == 0 and self.hops[d, other] > 0:
                self.copy(y, xh, here.c, 0, here.at_y(d)).start()
        self.copy(y, xh, here.c, 1, here.sibling()).start()

    def start(self):
        here = self.here
        self.copy(here.y, here.xh, here.c, 2, self.partner).start()
        self.pass_on(here.y, 0, 0)

    def over_x(self):
        here = self.here
        self.copy(here.y, 1 - here.xh, here.c, 2, self.partner).wait_recv()
        self.pass_on(here.y, 1, 0)

    def round(self, k):
        here = self.here
        for other in (0, 1):
            xh = here.xh if other == 0 else 1 - here.xh
            for d in (1, -1):
                if k <= self.hops[d, other]:
                    y = here.up_y(-d * k)
                    self.copy(y, xh, here.c, 0, here.at_y(d)).wait_recv()
                    if k < self.hops[d, other]:
                        self.copy(y, xh, here.c, 0, here.at_y(d)).start()
                    self.copy(y, xh, here.c, 1, here.sibling()).start()

    def from_sibling(self, y):
        here = self.here
        for xh in (0, 1):
            self.copy(y, xh, 1 - here.c, 1, here.sibling()).wait_recv()

    def finish(self):
        here = self.here
        for lane, ref in (
            (0, self.base.at[pl.ds(0, here.ny - 1), :, here.c, :, self.lanes]),
            (1, self.base.at[:, :, here.c, :, self.lanes]),
            (2, self.chunk(here.y, here.xh, here.c)),
        ):
            remote(ref, ref, self.send.at[lane], self.recv.at[0], here.sibling()).wait_send()


class RingFour:
    def __init__(self, here, base, first, width, axis, recv, send):
        self.here, self.base, self.first, self.width, self.axis = here, base, first, width, axis
        self.recv, self.send = recv, send
        self.hops = reach(here.ny)
        self.colour = here.x if axis == "x" else lax.rem(here.z, COLOURS)

    def part(self, index):
        return pl.ds(pl.multiple_of(self.first + index * self.width, LANES), self.width)

    def toward(self, d):
        return self.here.at_x(d) if self.axis == "x" else self.here.at_z(d)

    def along(self, y, d):
        here = self.here
        if self.axis == "x":
            ref = self.base.at[y, here.xh, here.c, :, self.part(here.xl)]
        else:
            ref = self.base.at[y, :, here.c, :, self.part(self.colour)]
        return remote(ref, ref, self.send.at[0], self.recv.at[y], here.at_y(d))

    def over(self, xh):
        here = self.here
        ref = self.base.at[here.y, xh, here.c, :, self.part(self.colour)]
        return remote(ref, ref, self.send.at[3], self.recv.at[here.ny + 16], here.other_columns())

    def half(self, colour, h, c, lane, device):
        size = self.here.ny // 2
        span = pl.ds(h * size, size)
        if self.axis == "x":
            ref = self.base.at[span, lax.div(colour, 2), c, :, self.part(lax.rem(colour, 2))]
        else:
            ref = self.base.at[span, :, c, :, self.part(colour)]
        slot = self.here.ny + (lane - 1) * 8 + colour * 2 + h
        return remote(ref, ref, self.send.at[lane], self.recv.at[slot], device)

    def begin_y(self):
        for d in (1, -1):
            if self.hops[d] > 0:
                self.along(self.here.y, d).start()

    def start(self):
        if self.axis == "x":
            self.begin_y()
        else:
            self.over(self.here.xh).start()

    def over_x(self):
        if self.axis == "z":
            self.over(1 - self.here.xh).wait_recv()
            self.begin_y()

    def round(self, k):
        for d in (1, -1):
            if k <= self.hops[d]:
                y = self.here.up_y(-d * k)
                self.along(y, d).wait_recv()
                if k < self.hops[d]:
                    self.along(y, d).start()

    def begin_four(self):
        here = self.here
        for h, d in ((0, 1), (1, -1), (1, 1), (0, -1)):
            self.half(self.colour, h, here.c, 1, self.toward(d)).start()
        for h in (0, 1):
            self.half(self.colour, h, here.c, 2, here.sibling()).start()

    def four(self, k):
        here = self.here
        if k == 1:
            came = ((0, 1, True), (1, -1, True), (1, 1, False), (0, -1, False))
        else:
            came = ((0, 2, False), (1, -2, False))
        for h, d, further in came:
            colour = lax.rem(self.colour + (COLOURS - d), COLOURS)
            toward = self.toward(1 if d > 0 else -1)
            self.half(colour, h, here.c, 1, toward).wait_recv()
            if further:
                self.half(colour, h, here.c, 1, toward).start()
            self.half(colour, h, here.c, 2, here.sibling()).start()

    def from_sibling(self):
        here = self.here
        for colour in range(COLOURS):
            for h in (0, 1):
                self.half(jnp.int32(colour), h, 1 - here.c, 2, here.sibling()).wait_recv()

    def finish(self):
        here = self.here
        xh = 0 if self.axis == "x" else slice(None)
        ends = [
            (0, self.base.at[pl.ds(0, here.ny - 1), xh, here.c, :, pl.ds(0, self.width)]),
            (1, self.base.at[:, xh, here.c, :, pl.ds(0, 3 * self.width)]),
            (2, self.base.at[:, xh, here.c, :, pl.ds(0, 4 * self.width)]),
        ]
        if self.axis == "z":
            ends.append((3, self.base.at[0, 0, here.c, :, pl.ds(0, self.width)]))
        for lane, ref in ends:
            remote(ref, ref, self.send.at[lane], self.recv.at[0], here.sibling()).wait_send()


class Pair:
    def __init__(self, here, base, recv, send):
        self.here, self.base, self.recv, self.send = here, base, recv, send
        self.parity = lax.rem(here.y, 2)
        self.other_y = here.device(y=here.y + 1 - 2 * self.parity)

    def copy(self, parity, xh, c, lane, device):
        ref = self.base.at[:, parity, xh, c]
        slot = parity * 4 + xh * 2 + c
        return remote(ref, ref, self.send.at[lane], self.recv.at[slot], device)

    def start(self):
        here = self.here
        self.copy(self.parity, here.xh, here.c, 2, here.other_columns()).start()
        self.copy(self.parity, here.xh, here.c, 1, here.sibling()).start()

    def over_x(self):
        here = self.here
        self.copy(self.parity, 1 - here.xh, here.c, 2, here.other_columns()).wait_recv()
        self.copy(self.parity, 1 - here.xh, here.c, 1, here.sibling()).start()

    def begin_y(self):
        here = self.here
        for xh in (here.xh, 1 - here.xh):
            self.copy(self.parity, xh, here.c, 0, self.other_y).start()

    def over_y(self):
        here = self.here
        for xh in (here.xh, 1 - here.xh):
            self.copy(1 - self.parity, xh, here.c, 0, self.other_y).wait_recv()
            self.copy(1 - self.parity, xh, here.c, 1, here.sibling()).start()

    def from_sibling(self):
        here = self.here
        for parity in (0, 1):
            for xh in (0, 1):
                self.copy(parity, xh, 1 - here.c, 1, here.sibling()).wait_recv()

    def finish(self):
        here = self.here
        for lane, ref in (
            (0, self.base.at[:, 0, :, here.c]),
            (1, self.base.at[:, :, :, here.c]),
            (2, self.base.at[:, 0, 0, here.c]),
        ):
            remote(ref, ref, self.send.at[lane], self.recv.at[0], here.sibling()).wait_send()


def down(values):
    return jnp.sum(values, axis=0, keepdims=True)


def gather_down(values):
    return jnp.sum(values.reshape(values.shape[0] // 8, 8, values.shape[1]), axis=0)


def dot(left, right):
    return jnp.dot(left, right, preferred_element_type=F32)


def dot_lanes(left, right):
    return lax.dot_general(left, right, (((1,), (1,)), ((), ())), preferred_element_type=F32)


def row(ref):
    return ref[...].reshape(1, ref.shape[0])


def rows_of(index, size):
    return pl.ds(pl.multiple_of(index * size, size), size)


def log2(count):
    return count.bit_length() - 1


def kernel(
    length_ref,
    step_ref,
    latents_in,
    prompt_in,
    null_in,
    head_mod_in,
    cross_gain,
    cross_bias,
    q_gain,
    k_gain,
    w_query,
    w_key,
    w_value,
    w_out,
    w_head_in,
    head_bias,
    target_in,
    guided_ref,
    grad_ref,
    latents,
    either,
    head_mod,
    w_head,
    target,
    weights,
    pair_weights,
    text,
    context,
    columns,
    w_head_rows,
    tokens,
    cross_in,
    query_raw,
    query,
    key_normed,
    value_rows,
    key_raw,
    attn,
    attended,
    after,
    head_in,
    d_unit,
    d_after,
    d_attended,
    noise,
    d_text,
    d_sibling,
    y_send,
    y_recv,
    product,
    lane_gain,
    unit_send,
    unit_recv,
    grad_send,
    grad_recv,
    z_send,
    z_recv,
    text_recv,
    text_send,
    recv_y,
    send_y,
    recv_z,
    send_z,
    recv_x,
    send_x,
    pair_recv,
    pair_send,
    swap_sem,
    sibling_sem,
    y_recv_sem,
    y_send_sem,
    tail_sem,
    load_sem,
):
    here = Place()
    ny, nz = here.ny, here.nz
    rows, width = w_query.shape
    token_count = latents_in.shape[0]
    text_rows = prompt_in.shape[0]
    patch = w_head_in.shape[0]
    heads = width // LANES
    blocks = width // LANES
    token_blocks = token_count // LANES
    band = 4 * rows
    root = 1.0 / math.sqrt(LANES)
    pairs = ny // 2
    share = text_rows // ny
    own_rows = share // 4
    half, quarter, eighth = text_rows // 2, text_rows // 4, text_rows // 8
    wide = width // pairs
    middle = width // 4
    parity = lax.rem(here.y, 2)
    pair = lax.div(here.y, 2)

    partners = [here.sibling(), here.other_columns(), here.other_tokens(), here.other_branch()]
    partners += [here.at_y(d) for d in range(1, ny)] + [here.at_z(d) for d in range(1, nz)]
    partners += [here.device(y=here.up_y(d), xh=1 - here.xh) for d in range(1, ny)]
    barrier = pltpu.get_barrier_semaphore()
    for device in partners:
        pl.semaphore_signal(barrier, inc=1, device_id=device, device_id_type=MESH)

    x_part = LANES * (2 if blocks >= 12 else 1)
    x_first = width - 2 * x_part
    z_first = x_first - COLOURS * LANES
    y_lanes = pl.ds(0, z_first)
    loads = []

    def load(src, dst):
        loads.append(pltpu.make_async_copy(src, dst, load_sem.at[len(loads)]))
        loads[-1].start()

    for index, own in ((QUERY, w_query), (OUT, w_out)):
        for lanes in (
            y_lanes,
            pl.ds(pl.multiple_of(z_first + lax.rem(here.z, COLOURS) * LANES, LANES), LANES),
            pl.ds(pl.multiple_of(x_first + here.xl * x_part, LANES), x_part),
        ):
            load(own.at[:, lanes], weights.at[index, here.y, here.xh, here.c, :, lanes])
    for index, own in enumerate((w_key, w_value)):
        load(own, pair_weights.at[index, parity, here.xh, here.c])
    for src, dst in (
        (head_mod_in, head_mod),
        (w_head_in, w_head),
        (latents_in, latents),
        (target_in, target),
    ):
        load(src, dst)
    text_load = load_sem.at[len(loads)]

    @pl.when(here.xl == 0)
    def _():
        pltpu.make_async_copy(prompt_in, either, text_load).start()

    @pl.when(here.xl == 1)
    def _():
        pltpu.make_async_copy(null_in, either, text_load).start()

    for copy in loads[:6]:
        copy.wait()
    pl.semaphore_wait(barrier, len(partners))

    text_ring = RingY(here, text, slice(None), here.other_tokens(), text_recv, text_send)
    rings = []
    for index in (QUERY, OUT):
        base = weights.at[index]
        rings.append(
            (
                RingFour(here, base, x_first, x_part, "x", recv_x.at[index], send_x.at[index]),
                RingFour(here, base, z_first, LANES, "z", recv_z.at[index], send_z.at[index]),
                RingY(
                    here, base, y_lanes, here.other_columns(), recv_y.at[index], send_y.at[index]
                ),
            )
        )
    key_value = Pair(here, pair_weights, pair_recv, pair_send)

    x_query, z_query, y_query = rings[QUERY]
    x_out, z_out, y_out = rings[OUT]

    def small_round(index, k):
        for ring in rings[index][:2]:
            ring.round(k)
            if k == pairs:
                ring.begin_four()

    def go_four(index, k):
        for ring in rings[index][:2]:
            ring.four(k)

    def all_here(index):
        for ring in rings[index][:2]:
            ring.from_sibling()
        for y in range(ny):
            rings[index][2].from_sibling(y)

    for ring in rings[QUERY]:
        ring.start()

    def text_row(index):
        place = lax.shift_right_logical(index, log2(own_rows)) & (pairs - 1)
        place = place * 2 + (lax.shift_right_logical(index, log2(quarter)) & 1)
        place = place * 2 + (lax.shift_right_logical(index, log2(eighth)) & 1)
        place = place * 2 + (lax.shift_right_logical(index, log2(half)) & 1)
        return place * own_rows + (index & (own_rows - 1))

    square_iota = functools.partial(lax.broadcasted_iota, jnp.int32, (text_rows, text_rows))
    order = jnp.where(text_row(square_iota(0)) == square_iota(1), 1.0, 0.0).astype(BF16)

    pltpu.make_async_copy(prompt_in, either, text_load).wait()
    context[...] = dot(order, either[...]).astype(BF16)
    for copy in loads[6:8]:
        copy.wait()
    own_key = pair_weights[0, parity, here.xh, here.c]
    own_value = pair_weights[1, parity, here.xh, here.c]
    text[here.y, here.xh, here.c, :rows] = dot_lanes(own_key, context[...]).astype(BF16)
    text[here.y, here.xh, here.c, rows:] = dot_lanes(own_value, context[...]).astype(BF16)
    text_ring.start()
    z_query.over_x()
    y_query.over_x()

    for copy in loads[8:]:
        copy.wait()
    modulation = head_mod[step_ref[0]]
    stack = jnp.concatenate(
        [
            row(cross_gain),
            row(cross_bias),
            row(q_gain),
            row(k_gain),
            1.0 + modulation[1:2],
            modulation[0:1],
            jnp.concatenate([row(head_bias), jnp.zeros((1, width - patch), F32)], axis=1),
            jnp.zeros((LANES - 7, width), F32),
        ],
        axis=0,
    )
    for block in range(blocks):
        lanes = slice(block * LANES, (block + 1) * LANES)
        columns[lanes, :] = stack[:, lanes].T
        w_head_rows[lanes, :] = w_head[:, lanes].T

    def turn(block, total):
        at = rows_of(block, LANES)
        for t in range(token_blocks):
            lanes = slice(t * LANES, (t + 1) * LANES)
            tokens[at, lanes] = latents[lanes, at].T
        return total + gather_down(tokens[at, :].astype(F32))

    zero_row = jnp.zeros((8, token_count), F32)
    unroll = 4 if blocks % 4 == 0 else 1
    mean = down(lax.fori_loop(0, blocks, turn, zero_row, unroll=unroll)) / width

    small_round(QUERY, 1)
    text_ring.over_x()
    x_out.start()
    z_out.start()

    def spread(block, total):
        centred = tokens[rows_of(block, LANES), :].astype(F32) - mean
        return total + gather_down(centred * centred)

    variance = down(lax.fori_loop(0, blocks, spread, zero_row, unroll=unroll)) / width
    inverse = lax.rsqrt(variance + NORM_EPS)

    def normalise(block, carry):
        at = rows_of(block, LANES)
        unit = (tokens[at, :].astype(F32) - mean) * inverse
        cross_in[at, :] = (unit * columns[at, 0:1] + columns[at, 1:2]).astype(BF16)
        return carry

    y_query.round(1)
    z_out.over_x()
    if pairs > 1:
        small_round(QUERY, 2)
    text_ring.round(1)
    lax.fori_loop(0, blocks, normalise, 0, unroll=unroll)

    y_out.start()
    key_value.start()
    for k in range(3, pairs + 1):
        small_round(QUERY, k)
        small_round(OUT, k - 2)
        if k == 3:
            y_out.over_x()
            y_query.round(2)
            text_ring.round(2)
    if pairs < 3:
        y_out.over_x()
        if pairs > 1:
            y_query.round(2)
            text_ring.round(2)
    if pairs > 2:
        y_query.round(3)
        text_ring.round(3)
    if pairs > 1:
        small_round(OUT, pairs - 1)
        y_out.round(1)
    go_four(QUERY, 1)
    small_round(OUT, pairs)
    if pairs > 3:
        text_ring.round(4)
        y_query.round(4)
    if pairs > 1:
        y_out.round(2)
    else:
        y_out.round(1)
    go_four(QUERY, 2)
    key_value.over_x()
    for y in range(ny):
        text_ring.from_sibling(y)

    keys = text[:, :, :, :rows, :].reshape(width, text_rows).astype(F32)
    values = text[:, :, :, rows:, :].reshape(width, text_rows).astype(F32)
    key_inverse = lax.rsqrt(down(keys * keys) / width + NORM_EPS)
    for h in range(heads):
        lanes = slice(h * LANES, (h + 1) * LANES)
        one = keys[lanes]
        key_raw[:, lanes] = one.T.astype(BF16)
        key_normed[h] = (one * key_inverse * columns[lanes, 3:4]).T.astype(BF16)
        value_rows[h] = values[lanes].T.astype(BF16)

    go_four(OUT, 1)
    all_here(QUERY)

    def project(i, total):
        raw = dot(weights[QUERY, pl.ds(i * 2, 2)].reshape(2 * band, width), cross_in[...])
        query_raw[rows_of(i, 2 * band), :] = raw
        return total + gather_down(raw * raw)

    square = lax.fori_loop(0, pairs // 2, project, zero_row)
    if pairs > 2:
        y_out.round(3)
    key_value.begin_y()
    square = lax.fori_loop(pairs // 2, pairs, project, square)
    query_inverse = lax.rsqrt(down(square) / width + NORM_EPS)

    length = here.xl * text_rows + (1 - here.xl) * length_ref[0]
    visible = text_row(lax.broadcasted_iota(jnp.int32, (text_rows, token_count), 0)) < length

    def attend(h, carry):
        at = rows_of(h, LANES)
        query[at, :] = (query_raw[at, :] * query_inverse * columns[at, 2:3]).astype(BF16)
        scores = dot(key_normed[h], query[at, :]) * root
        masked = jnp.where(visible, scores, -1e30)
        terms = jnp.where(visible, jnp.exp(masked - jnp.max(masked, axis=0, keepdims=True)), 0.0)
        shares = terms / down(terms)
        attn[h] = shares
        attended[at, :] = lax.dot_general(
            value_rows[h],
            shares.astype(BF16),
            (((0,), (0,)), ((), ())),
            preferred_element_type=F32,
        ).astype(BF16)
        return carry

    lax.fori_loop(0, heads // 4, attend, 0, unroll=True)
    go_four(OUT, 2)
    lax.fori_loop(heads // 4, heads // 2, attend, 0, unroll=True)
    if pairs > 3:
        y_out.round(4)
    lax.fori_loop(heads // 2, heads, attend, 0, unroll=True)
    all_here(OUT)

    cutting = (token_blocks + 1) // 2 * LANES
    parts = [slice(0, cutting)] + ([slice(cutting, token_count)] if cutting < token_count else [])

    def swap(number, branch):
        ref = noise.at[branch, :, parts[number]]
        return remote(
            ref, ref, swap_sem.at[0, number], swap_sem.at[1, number], here.other_branch()
        )

    def head_forward(number):
        lanes = parts[number]
        start = jnp.zeros((8, lanes.stop - lanes.start), F32)

        def project_out(i, total):
            at = rows_of(i, 2 * band)
            matrix = weights[OUT, pl.ds(i * 2, 2)].reshape(2 * band, width)
            rows_after = dot(matrix, attended[:, lanes]) + tokens[at, lanes].astype(F32)
            after[at, lanes] = rows_after
            return total + gather_down(rows_after)

        head_mean = down(lax.fori_loop(0, pairs, project_out, start)) / width

        def head_spread(block, total):
            centred = after[rows_of(block, LANES), lanes] - head_mean
            return total + gather_down(centred * centred)

        variance = down(lax.fori_loop(0, blocks, head_spread, start, unroll=unroll)) / width
        head_inverse = lax.rsqrt(variance + NORM_EPS)

        def modulate(block, carry):
            at = rows_of(block, LANES)
            unit = (after[at, lanes] - head_mean) * head_inverse
            head_in[at, lanes] = (unit * columns[at, 4:5] + columns[at, 5:6]).astype(BF16)
            return carry

        lax.fori_loop(0, blocks, modulate, 0, unroll=unroll)
        noise[here.xl, :, lanes] = dot(w_head[...], head_in[:, lanes]) + columns[:patch, 6:7]
        swap(number, here.xl).start()
        return head_mean, head_inverse

    factor = GUIDE_SCALE - (2.0 * GUIDE_SCALE - 1.0) * here.xl.astype(F32)

    def head_backward(number, head_mean, head_inverse):
        lanes = parts[number]
        start = jnp.zeros((8, lanes.stop - lanes.start), F32)
        swap(number, 1 - here.xl).wait_recv()
        cond, null = noise[0, :, lanes], noise[1, :, lanes]
        guided = null + GUIDE_SCALE * (cond - null)
        guided_ref[:, lanes] = guided
        d_noise = (factor * (guided - target[:, lanes].astype(F32))).astype(BF16)

        def head_back(block, sums):
            at = rows_of(block, LANES)
            unit = (after[at, lanes] - head_mean) * head_inverse
            part_unit = dot(w_head_rows[at, :], d_noise) * columns[at, 4:5]
            d_unit[at, lanes] = part_unit
            return (sums[0] + gather_down(part_unit), sums[1] + gather_down(part_unit * unit))

        first_sum, second_sum = lax.fori_loop(
            0, blocks, head_back, (start, start), unroll=unroll
        )
        first_mean, second_mean = down(first_sum) / width, down(second_sum) / width

        def norm_back(block, carry):
            at = rows_of(block, LANES)
            unit = (after[at, lanes] - head_mean) * head_inverse
            grads = (head_inverse * (d_unit[at, lanes] - first_mean - unit * second_mean)).astype(
                BF16
            )
            for t in range(lanes.start, lanes.stop, LANES):
                d_after[t : t + LANES, at] = grads[:, t - lanes.start : t - lanes.start + LANES].T
            return carry

        lax.fori_loop(0, blocks, norm_back, 0, unroll=unroll)

    stats = [head_forward(number) for number in range(len(parts))]
    def fold(values):
        return jnp.concatenate(
            [values[:, q * middle : (q + 1) * middle] for q in range(4)], axis=0
        )

    def split(values):
        high = values.astype(BF16)
        low = (values - high.astype(F32)).astype(BF16)
        return jnp.concatenate([high, low], axis=0)

    first_row = here.c * half + parity * quarter + here.xh * eighth
    own_span = pl.ds(pl.multiple_of(first_row, eighth), eighth)
    own_lanes = rows_of(pair, wide)
    near = key_raw[own_span, :].astype(F32)
    near_inverse = lax.rsqrt(jnp.mean(near * near, axis=-1, keepdims=True) + NORM_EPS)
    near_unit = key_raw[own_span, own_lanes].astype(F32) * near_inverse

    def multiply(left, lead):
        both = split(left)

        def columns_of(block, carry):
            at = rows_of(block, 2 * LANES)
            if lead:
                matrix = pair_weights[:, :, :, :, :, at].reshape(2 * wide, 2 * LANES)
            else:
                matrix = pair_weights[0, :, :, :, :, at].reshape(wide, 2 * LANES)
            result = dot(both, matrix)
            product[:, at] = result[:eighth] + result[eighth:]
            return carry

        lax.fori_loop(0, blocks // 2, columns_of, 0, unroll=2)

    def exchange(send, recv, lane):
        for d in range(1, pairs):
            q = lax.rem(pair + d, pairs)
            remote(
                send.at[q],
                recv.at[pair],
                tail_sem.at[lane],
                tail_sem.at[lane + 1],
                here.device(y=q * 2 + parity),
            ).start()
        ref = recv.at[pl.ds(0, max(1, pairs - 1))]
        return remote(ref, ref, tail_sem.at[lane], tail_sem.at[lane + 1], here.sibling())

    def collect(send, recv):
        total = send[pair].astype(F32)
        for d in range(1, pairs):
            total = total + recv[lax.rem(pair + d, pairs)].astype(F32)
        return total

    for number, (head_mean, head_inverse) in enumerate(stats):
        head_backward(number, head_mean, head_inverse)

    def out_back(block, carry):
        at = rows_of(block, 2 * LANES)
        matrix = weights[OUT, :, :, :, :, at].reshape(width, 2 * LANES)
        d_attended[:, at] = dot(d_after[...], matrix).astype(BF16)
        return carry

    lax.fori_loop(0, blocks // 2, out_back, 0, unroll=2)
    key_value.over_y()

    def attend_back(h, carry):
        at = rows_of(h, LANES)
        grads = d_attended[:, at]
        shares = attn[h]
        d_shares = dot_lanes(value_rows[h], grads)
        d_scores = shares * (d_shares - down(d_shares * shares))
        d_text[0, :, at] = dot_lanes((d_scores * root).astype(BF16), query[at, :])
        d_text[1, :, at] = dot(shares.astype(BF16), grads)
        return carry

    def group(i):
        return lax.rem(pair + (i + 1), pairs)

    def core_span(c):
        return pl.ds(pl.multiple_of(c * half, half), half)

    def to_sibling(i):
        lanes = rows_of(group(i), wide)
        return remote(
            d_text.at[:, core_span(1 - here.c), lanes],
            d_sibling.at[:, :, lanes],
            sibling_sem.at[0, i],
            sibling_sem.at[1, i],
            here.sibling(),
        )

    def to_row(i, odd, xh):
        lanes = rows_of(group(i), wide)
        span = pl.ds(pl.multiple_of(odd * quarter + xh * eighth, eighth), eighth)
        return remote(
            y_send.at[:, span, lanes],
            y_recv.at[here.y, here.xh],
            y_send_sem.at[i],
            y_recv_sem.at[here.y * 2 + here.xh],
            here.device(y=group(i) * 2 + odd, xh=xh),
        )

    def sum_cores(i):
        lanes = rows_of(group(i), wide)
        to_sibling(i).wait_recv()
        both = d_text[:, core_span(here.c), lanes] + d_sibling[:, :, lanes]
        y_send[:, :, lanes] = both.astype(BF16)
        if i < pairs - 1:
            for odd in (0, 1):
                for xh in (0, 1):
                    to_row(i, jnp.int32(odd), jnp.int32(xh)).start()
        else:
            to_row(i, 1 - parity, here.xh).start()
            to_row(i, 1 - parity, 1 - here.xh).start()
            to_row(i, parity, 1 - here.xh).start()
            d_sibling[:, :, lanes] = both

    for i in range(pairs):
        for j in range(heads // pairs):
            attend_back(group(i) * (heads // pairs) + j, 0)
        to_sibling(i).start()
        if i > 0:
            sum_cores(i - 1)
        if i == pairs - 2 or pairs == 1:
            key_value.from_sibling()
            multiply(near_unit * near_inverse, False)
            for q in range(pairs):
                unit_send[q] = fold(product[q * own_rows : (q + 1) * own_rows, :])
            units = exchange(unit_send, unit_recv, 2)
    sum_cores(pairs - 1)

    eighth_span = pl.ds(
        pl.multiple_of(parity * quarter + here.xh * eighth, eighth), eighth
    )
    own_sum = d_sibling[:, eighth_span, own_lanes]
    near_y = here.y + 1 - 2 * parity
    sources = [(lax.rem(pair * 2 + d, ny), xh) for d in range(2, ny) for xh in (0, 1)]
    sources += [(here.y, 1 - here.xh), (near_y, here.xh), (near_y, 1 - here.xh)]
    for y, xh in sources:
        ref = y_recv.at[y, xh]
        remote(
            ref, ref, y_send_sem.at[0], y_recv_sem.at[y * 2 + xh], here.sibling()
        ).wait_recv()
        own_sum = own_sum + y_recv[y, xh].astype(F32)
    if pairs > 1:
        units.wait_recv()
    unit_total = collect(unit_send, unit_recv)
    lane_gain[...] = row(k_gain)
    own_gain = lane_gain[:, own_lanes]
    gained = own_sum[0] * own_gain
    statistic = jnp.sum(gained * near_unit, axis=-1, keepdims=True) / width
    multiply(jnp.concatenate([near_inverse * gained, own_sum[1]], axis=1), True)
    for q in range(pairs):
        span = slice(q * own_rows, (q + 1) * own_rows)
        grad_send[q, :, :middle] = fold(product[span, :]).astype(BF16)
        both = jnp.broadcast_to(statistic[span], (own_rows, LANES))
        rounded = both.astype(BF16).astype(F32)
        low_half = lax.broadcasted_iota(jnp.int32, (own_rows, LANES), 1) < LANES // 2
        both = jnp.where(low_half, rounded, both - rounded)
        grad_send[q, :, middle:] = jnp.concatenate([both] * 4, axis=0).astype(BF16)
    grads = exchange(grad_send, grad_recv, 4)
    if pairs > 1:
        grads.wait_recv()
    total = collect(grad_send, grad_recv)
    both = total[:, middle : middle + 1] + total[:, middle + LANES // 2 : middle + LANES // 2 + 1]
    own_grad = total[:, :middle] - both * unit_total

    def unfold(values):
        for q in range(4):
            grad_ref[:, q * middle : (q + 1) * middle] = values[q * own_rows : (q + 1) * own_rows]

    @pl.when(here.xl == 0)
    def _():
        unfold(own_grad)

    @pl.when(here.xl == 1)
    def _():
        z_send[...] = own_grad.astype(BF16)
        for d in range(1, nz):
            remote(
                z_send, z_recv.at[here.z], tail_sem.at[6], tail_sem.at[7], here.at_z(d)
            ).start()
        ref = z_recv.at[pl.ds(0, nz - 1)]
        gathered = remote(ref, ref, tail_sem.at[6], tail_sem.at[7], here.sibling())
        gathered.wait_recv()
        others = z_recv[here.up_z(1)].astype(F32)
        for d in range(2, nz):
            others = others + z_recv[here.up_z(d)].astype(F32)
        unfold((own_grad + others) / nz)
        gathered.wait_send()

    for number in range(len(parts)):
        swap(number, here.xl).wait_send()
    if pairs > 1:
        units.wait_send()
        grads.wait_send()
    for i in range(pairs):
        to_sibling(i).wait_send()
        ref = y_send.at[:, :, rows_of(group(i), wide)]
        if i == pairs - 1:
            ref = y_send.at[:, pl.ds(0, 3 * eighth), rows_of(group(i), wide)]
        remote(ref, ref, y_send_sem.at[i], y_recv_sem.at[0], here.sibling()).wait_send()
    text_ring.finish()
    key_value.finish()
    for three in rings:
        for ring in three:
            ring.finish()


def hand_over(guided_in, grad_in, guided_ref, grad_ref, sem):
    copies = [
        pltpu.make_async_copy(guided_in, guided_ref, sem.at[0]),
        pltpu.make_async_copy(grad_in, grad_ref, sem.at[1]),
    ]
    for copy in copies:
        copy.start()
    for copy in copies:
        copy.wait()


def on_device(
    latents,
    prompt,
    null_embed,
    text_lengths,
    timesteps,
    head_mod,
    cross_gain,
    cross_bias,
    q_gain,
    k_gain,
    w_query,
    w_key,
    w_value,
    w_out,
    w_head,
    head_bias,
    target,
):
    nz = lax.axis_size("clip")
    ny = lax.axis_size("seq") // 4
    tokens = latents[0, 0]
    count, width = tokens.shape
    text_rows = null_embed.shape[0]
    rows = w_query.shape[1]
    patch = w_head.shape[1]
    heads = width // LANES
    pairs = ny // 2
    wide = width // pairs
    middle = width // 4
    half, quarter, eighth = text_rows // 2, text_rows // 4, text_rows // 8
    own_rows = text_rows // ny // 4
    dma = pltpu.SemaphoreType.DMA
    vmem = pl.BlockSpec(memory_space=pltpu.VMEM)
    smem = pl.BlockSpec(memory_space=pltpu.SMEM)
    guided, grad = pl.pallas_call(
        kernel,
        out_shape=(
            jax.ShapeDtypeStruct((patch, count), F32),
            jax.ShapeDtypeStruct((own_rows, width), F32),
        ),
        in_specs=[smem, smem]
        + [pl.BlockSpec(memory_space=pl.ANY)] * 4
        + [vmem] * 4
        + [pl.BlockSpec(memory_space=pl.ANY)] * 5
        + [vmem]
        + [pl.BlockSpec(memory_space=pl.ANY)],
        out_specs=(vmem, vmem),
        scratch_shapes=[
            pltpu.VMEM((count, width), BF16),
            pltpu.VMEM((text_rows, width), BF16),
            pltpu.VMEM(head_mod.shape, F32),
            pltpu.VMEM((patch, width), BF16),
            pltpu.VMEM((patch, count), BF16),
            pltpu.VMEM((2, ny, 2, 2, rows, width), BF16),
            pltpu.VMEM((2, 2, 2, 2, rows, width), BF16),
            pltpu.VMEM((ny, 2, 2, 2 * rows, text_rows), BF16),
            pltpu.VMEM((text_rows, width), BF16),
            pltpu.VMEM((width, LANES), F32),
            pltpu.VMEM((width, patch), BF16),
            pltpu.VMEM((width, count), BF16),
            pltpu.VMEM((width, count), BF16),
            pltpu.VMEM((width, count), F32),
            pltpu.VMEM((width, count), BF16),
            pltpu.VMEM((heads, text_rows, LANES), BF16),
            pltpu.VMEM((heads, text_rows, LANES), BF16),
            pltpu.VMEM((text_rows, width), BF16),
            pltpu.VMEM((heads, text_rows, count), F32),
            pltpu.VMEM((width, count), BF16),
            pltpu.VMEM((width, count), F32),
            pltpu.VMEM((width, count), BF16),
            pltpu.VMEM((width, count), F32),
            pltpu.VMEM((count, width), BF16),
            pltpu.VMEM((count, width), BF16),
            pltpu.VMEM((2, patch, count), F32),
            pltpu.VMEM((2, text_rows, width), F32),
            pltpu.VMEM((2, half, width), F32),
            pltpu.VMEM((2, half, width), BF16),
            pltpu.VMEM((ny, 2, 2, eighth, wide), BF16),
            pltpu.VMEM((eighth, width), F32),
            pltpu.VMEM((1, width), F32),
            pltpu.VMEM((pairs, 4 * own_rows, middle), F32),
            pltpu.VMEM((pairs, 4 * own_rows, middle), F32),
            pltpu.VMEM((pairs, 4 * own_rows, middle + LANES), BF16),
            pltpu.VMEM((pairs, 4 * own_rows, middle + LANES), BF16),
            pltpu.VMEM((4 * own_rows, middle), BF16),
            pltpu.VMEM((nz, 4 * own_rows, middle), BF16),
            dma((4 * ny,)),
            dma((3,)),
            dma((2, 4 * ny)),
            dma((2, 3)),
            dma((2, ny + 17)),
            dma((2, 4)),
            dma((2, ny + 16)),
            dma((2, 3)),
            dma((8,)),
            dma((3,)),
            dma((2, 2)),
            dma((2, pairs)),
            dma((2 * ny,)),
            dma((pairs,)),
            dma((8,)),
            dma((14,)),
        ],
        compiler_params=pltpu.CompilerParams(
            collective_id=0, has_side_effects=True, vmem_limit_bytes=60 * 1024 * 1024
        ),
        cost_estimate=pl.CostEstimate(
            flops=8 * count * width * width, bytes_accessed=8 * count * width, transcendentals=0
        ),
    )(
        text_lengths,
        timesteps,
        tokens,
        prompt[0],
        null_embed,
        head_mod,
        cross_gain,
        cross_bias,
        q_gain,
        k_gain,
        w_query.T,
        w_key.T,
        w_value.T,
        w_out.T,
        w_head.T,
        head_bias,
        target[0].T,
    )
    guided, grad = pl.pallas_call(
        hand_over,
        out_shape=(
            jax.ShapeDtypeStruct((patch, count), F32),
            jax.ShapeDtypeStruct((own_rows, width), F32),
        ),
        in_specs=[pl.BlockSpec(memory_space=pl.ANY)] * 2,
        out_specs=(pl.BlockSpec(memory_space=pl.ANY),) * 2,
        scratch_shapes=[dma((2,))],
    )(guided, grad)
    return (guided.T[None], grad.reshape(1, 1, own_rows, width))


def solution(mesh):
    return jax.shard_map(
        on_device,
        mesh=mesh,
        in_specs=(
            P("clip", "guide", "seq", None),
            P("clip", None, None),
            P(),
            P("clip"),
            P("clip"),
            P(),
            P(),
            P(),
            P(),
            P(),
            P(None, "seq"),
            P(None, "seq"),
            P(None, "seq"),
            P(None, "seq"),
            P(),
            P(),
            P("clip", "seq", None),
        ),
        out_specs=(P("clip", "seq", None), P("clip", "guide", "seq", None)),
        check_vma=False,
    )
```

```python
import functools
import math

import jax
import jax.numpy as jnp
from jax import lax
from jax.experimental import pallas as pl
from jax.experimental.pallas import tpu as pltpu
from jax.sharding import PartitionSpec as P

LANES = 128
GUIDE_SCALE = 5.0
NORM_EPS = 1e-06
COLOURS = 4
MESH = pl.DeviceIdType.MESH
F32 = jnp.float32
BF16 = jnp.bfloat16
QUERY, OUT = range(2)


class Place:
    def __init__(self):
        seq = lax.axis_index("seq")
        self.nz = lax.axis_size("clip")
        self.ny = lax.axis_size("seq") // 4
        self.z = lax.axis_index("clip")
        self.xl = lax.axis_index("guide")
        self.y = lax.div(seq, 4)
        self.xh = lax.rem(lax.div(seq, 2), 2)
        self.c = lax.rem(seq, 2)
        self.x = self.xh * 2 + self.xl

    def device(self, z=None, y=None, xh=None, xl=None, c=None):
        z = self.z if z is None else z
        y = self.y if y is None else y
        xh = self.xh if xh is None else xh
        xl = self.xl if xl is None else xl
        c = self.c if c is None else c
        return {"clip": z, "guide": xl, "seq": y * 4 + xh * 2 + c}

    def up_y(self, by):
        return lax.rem(self.y + (by + self.ny), self.ny)

    def up_z(self, by):
        return lax.rem(self.z + (by + self.nz), self.nz)

    def up_x(self, by):
        return lax.rem(self.x + (by + 4), 4)

    def at_y(self, by):
        return self.device(y=self.up_y(by))

    def at_z(self, by):
        return self.device(z=self.up_z(by))

    def at_x(self, by):
        x = self.up_x(by)
        return self.device(xh=lax.div(x, 2), xl=lax.rem(x, 2))

    def sibling(self):
        return self.device(c=1 - self.c)

    def other_columns(self):
        return self.device(xh=1 - self.xh, xl=1 - self.xl)

    def other_tokens(self):
        return self.device(xh=1 - self.xh)

    def other_branch(self):
        return self.device(xl=1 - self.xl)


def remote(src, dst, send_sem, recv_sem, device):
    return pltpu.make_async_remote_copy(
        src_ref=src,
        dst_ref=dst,
        send_sem=send_sem,
        recv_sem=recv_sem,
        device_id=device,
        device_id_type=MESH,
    )


def reach(count):
    return {1: count // 2, -1: count - 1 - count // 2}


class RingY:
    def __init__(self, here, base, lanes, partner, recv, send):
        self.here, self.base, self.lanes, self.partner = here, base, lanes, partner
        self.recv, self.send = recv, send
        hops = reach(here.ny)
        self.hops = {(d, o): hops[d if o == 0 else -d] for d in (1, -1) for o in (0, 1)}
        self.rounds = here.ny // 2

    def chunk(self, y, xh, c):
        return self.base.at[y, xh, c, :, self.lanes]

    def copy(self, y, xh, c, lane, device):
        ref = self.chunk(y, xh, c)
        return remote(ref, ref, self.send.at[lane], self.recv.at[y * 4 + xh * 2 + c], device)

    def pass_on(self, y, other, step):
        here = self.here
        xh = here.xh if other == 0 else 1 - here.xh
        for d in (1, -1):
            if step == 0 and self.hops[d, other] > 0:
                self.copy(y, xh, here.c, 0, here.at_y(d)).start()
        self.copy(y, xh, here.c, 1, here.sibling()).start()

    def start(self):
        here = self.here
        self.copy(here.y, here.xh, here.c, 2, self.partner).start()
        self.pass_on(here.y, 0, 0)

    def over_x(self):
        here = self.here
        self.copy(here.y, 1 - here.xh, here.c, 2, self.partner).wait_recv()
        self.pass_on(here.y, 1, 0)

    def round(self, k):
        here = self.here
        for other in (0, 1):
            xh = here.xh if other == 0 else 1 - here.xh
            for d in (1, -1):
                if k <= self.hops[d, other]:
                    y = here.up_y(-d * k)
                    self.copy(y, xh, here.c, 0, here.at_y(d)).wait_recv()
                    if k < self.hops[d, other]:
                        self.copy(y, xh, here.c, 0, here.at_y(d)).start()
                    self.copy(y, xh, here.c, 1, here.sibling()).start()

    def from_sibling(self, y):
        here = self.here
        for xh in (0, 1):
            self.copy(y, xh, 1 - here.c, 1, here.sibling()).wait_recv()

    def finish(self):
        here = self.here
        for lane, ref in (
            (0, self.base.at[pl.ds(0, here.ny - 1), :, here.c, :, self.lanes]),
            (1, self.base.at[:, :, here.c, :, self.lanes]),
            (2, self.chunk(here.y, here.xh, here.c)),
        ):
            remote(ref, ref, self.send.at[lane], self.recv.at[0], here.sibling()).wait_send()


class RingFour:
    def __init__(self, here, base, first, width, axis, recv, send):
        self.here, self.base, self.first, self.width, self.axis = here, base, first, width, axis
        self.recv, self.send = recv, send
        self.hops = reach(here.ny)
        self.colour = here.x if axis == "x" else lax.rem(here.z, COLOURS)

    def part(self, index):
        return pl.ds(pl.multiple_of(self.first + index * self.width, LANES), self.width)

    def toward(self, d):
        return self.here.at_x(d) if self.axis == "x" else self.here.at_z(d)

    def along(self, y, d):
        here = self.here
        if self.axis == "x":
            ref = self.base.at[y, here.xh, here.c, :, self.part(here.xl)]
        else:
            ref = self.base.at[y, :, here.c, :, self.part(self.colour)]
        return remote(ref, ref, self.send.at[0], self.recv.at[y], here.at_y(d))

    def over(self, xh):
        here = self.here
        ref = self.base.at[here.y, xh, here.c, :, self.part(self.colour)]
        return remote(ref, ref, self.send.at[3], self.recv.at[here.ny + 16], here.other_columns())

    def half(self, colour, h, c, lane, device):
        size = self.here.ny // 2
        span = pl.ds(h * size, size)
        if self.axis == "x":
            ref = self.base.at[span, lax.div(colour, 2), c, :, self.part(lax.rem(colour, 2))]
        else:
            ref = self.base.at[span, :, c, :, self.part(colour)]
        slot = self.here.ny + (lane - 1) * 8 + colour * 2 + h
        return remote(ref, ref, self.send.at[lane], self.recv.at[slot], device)

    def begin_y(self):
        for d in (1, -1):
            if self.hops[d] > 0:
                self.along(self.here.y, d).start()

    def start(self):
        if self.axis == "x":
            self.begin_y()
        else:
            self.over(self.here.xh).start()

    def over_x(self):
        if self.axis == "z":
            self.over(1 - self.here.xh).wait_recv()
            self.begin_y()

    def round(self, k):
        for d in (1, -1):
            if k <= self.hops[d]:
                y = self.here.up_y(-d * k)
                self.along(y, d).wait_recv()
                if k < self.hops[d]:
                    self.along(y, d).start()

    def begin_four(self):
        here = self.here
        for h, d in ((0, 1), (1, -1), (1, 1), (0, -1)):
            self.half(self.colour, h, here.c, 1, self.toward(d)).start()
        for h in (0, 1):
            self.half(self.colour, h, here.c, 2, here.sibling()).start()

    def four(self, k):
        here = self.here
        if k == 1:
            came = ((0, 1, True), (1, -1, True), (1, 1, False), (0, -1, False))
        else:
            came = ((0, 2, False), (1, -2, False))
        for h, d, further in came:
            colour = lax.rem(self.colour + (COLOURS - d), COLOURS)
            toward = self.toward(1 if d > 0 else -1)
            self.half(colour, h, here.c, 1, toward).wait_recv()
            if further:
                self.half(colour, h, here.c, 1, toward).start()
            self.half(colour, h, here.c, 2, here.sibling()).start()

    def from_sibling(self):
        here = self.here
        for colour in range(COLOURS):
            for h in (0, 1):
                self.half(jnp.int32(colour), h, 1 - here.c, 2, here.sibling()).wait_recv()

    def finish(self):
        here = self.here
        xh = 0 if self.axis == "x" else slice(None)
        ends = [
            (0, self.base.at[pl.ds(0, here.ny - 1), xh, here.c, :, pl.ds(0, self.width)]),
            (1, self.base.at[:, xh, here.c, :, pl.ds(0, 3 * self.width)]),
            (2, self.base.at[:, xh, here.c, :, pl.ds(0, 4 * self.width)]),
        ]
        if self.axis == "z":
            ends.append((3, self.base.at[0, 0, here.c, :, pl.ds(0, self.width)]))
        for lane, ref in ends:
            remote(ref, ref, self.send.at[lane], self.recv.at[0], here.sibling()).wait_send()


class Pair:
    def __init__(self, here, base, recv, send):
        self.here, self.base, self.recv, self.send = here, base, recv, send
        self.parity = lax.rem(here.y, 2)
        self.other_y = here.device(y=here.y + 1 - 2 * self.parity)

    def copy(self, parity, xh, c, lane, device):
        ref = self.base.at[:, parity, xh, c]
        slot = parity * 4 + xh * 2 + c
        return remote(ref, ref, self.send.at[lane], self.recv.at[slot], device)

    def start(self):
        here = self.here
        self.copy(self.parity, here.xh, here.c, 2, here.other_columns()).start()
        self.copy(self.parity, here.xh, here.c, 1, here.sibling()).start()

    def over_x(self):
        here = self.here
        self.copy(self.parity, 1 - here.xh, here.c, 2, here.other_columns()).wait_recv()
        self.copy(self.parity, 1 - here.xh, here.c, 1, here.sibling()).start()

    def begin_y(self):
        here = self.here
        for xh in (here.xh, 1 - here.xh):
            self.copy(self.parity, xh, here.c, 0, self.other_y).start()

    def over_y(self):
        here = self.here
        for xh in (here.xh, 1 - here.xh):
            self.copy(1 - self.parity, xh, here.c, 0, self.other_y).wait_recv()
            self.copy(1 - self.parity, xh, here.c, 1, here.sibling()).start()

    def from_sibling(self):
        here = self.here
        for parity in (0, 1):
            for xh in (0, 1):
                self.copy(parity, xh, 1 - here.c, 1, here.sibling()).wait_recv()

    def finish(self):
        here = self.here
        for lane, ref in (
            (0, self.base.at[:, 0, :, here.c]),
            (1, self.base.at[:, :, :, here.c]),
            (2, self.base.at[:, 0, 0, here.c]),
        ):
            remote(ref, ref, self.send.at[lane], self.recv.at[0], here.sibling()).wait_send()


def down(values):
    return jnp.sum(values, axis=0, keepdims=True)


def gather_down(values):
    return jnp.sum(values.reshape(values.shape[0] // 8, 8, values.shape[1]), axis=0)


def dot(left, right):
    return jnp.dot(left, right, preferred_element_type=F32)


def dot_lanes(left, right):
    return lax.dot_general(left, right, (((1,), (1,)), ((), ())), preferred_element_type=F32)


def row(ref):
    return ref[...].reshape(1, ref.shape[0])


def rows_of(index, size):
    return pl.ds(pl.multiple_of(index * size, size), size)


def log2(count):
    return count.bit_length() - 1


def kernel(
    length_ref,
    step_ref,
    latents_in,
    prompt_in,
    null_in,
    head_mod_in,
    cross_gain,
    cross_bias,
    q_gain,
    k_gain,
    w_query,
    w_key,
    w_value,
    w_out,
    w_head_in,
    head_bias,
    target_in,
    guided_ref,
    grad_ref,
    latents,
    either,
    head_mod,
    w_head,
    target,
    weights,
    pair_weights,
    text,
    context,
    columns,
    w_head_rows,
    tokens,
    cross_in,
    query_raw,
    query,
    key_normed,
    value_rows,
    key_raw,
    attn,
    attended,
    after,
    head_in,
    d_unit,
    d_after,
    d_attended,
    noise,
    d_text,
    d_sibling,
    y_send,
    y_recv,
    product,
    lane_gain,
    unit_send,
    unit_recv,
    grad_send,
    grad_recv,
    z_send,
    z_recv,
    text_recv,
    text_send,
    recv_y,
    send_y,
    recv_z,
    send_z,
    recv_x,
    send_x,
    pair_recv,
    pair_send,
    swap_sem,
    sibling_sem,
    y_recv_sem,
    y_send_sem,
    tail_sem,
    load_sem,
):
    here = Place()
    ny, nz = here.ny, here.nz
    rows, width = w_query.shape
    token_count = latents_in.shape[0]
    text_rows = prompt_in.shape[0]
    patch = w_head_in.shape[0]
    heads = width // LANES
    blocks = width // LANES
    token_blocks = token_count // LANES
    band = 4 * rows
    root = 1.0 / math.sqrt(LANES)
    pairs = ny // 2
    share = text_rows // ny
    own_rows = share // 4
    half, quarter, eighth = text_rows // 2, text_rows // 4, text_rows // 8
    wide = width // pairs
    middle = width // 4
    parity = lax.rem(here.y, 2)
    pair = lax.div(here.y, 2)

    partners = [here.sibling(), here.other_columns(), here.other_tokens(), here.other_branch()]
    partners += [here.at_y(d) for d in range(1, ny)] + [here.at_z(d) for d in range(1, nz)]
    partners += [here.device(y=here.up_y(d), xh=1 - here.xh) for d in range(1, ny)]
    barrier = pltpu.get_barrier_semaphore()
    for device in partners:
        pl.semaphore_signal(barrier, inc=1, device_id=device, device_id_type=MESH)

    x_part = LANES * (2 if blocks >= 12 else 1)
    x_first = width - 2 * x_part
    z_first = x_first - COLOURS * LANES
    y_lanes = pl.ds(0, z_first)
    loads = []

    def load(src, dst):
        loads.append(pltpu.make_async_copy(src, dst, load_sem.at[len(loads)]))
        loads[-1].start()

    for index, own in ((QUERY, w_query), (OUT, w_out)):
        for lanes in (
            y_lanes,
            pl.ds(pl.multiple_of(z_first + lax.rem(here.z, COLOURS) * LANES, LANES), LANES),
            pl.ds(pl.multiple_of(x_first + here.xl * x_part, LANES), x_part),
        ):
            load(own.at[:, lanes], weights.at[index, here.y, here.xh, here.c, :, lanes])
    for index, own in enumerate((w_key, w_value)):
        load(own, pair_weights.at[index, parity, here.xh, here.c])
    for src, dst in (
        (head_mod_in, head_mod),
        (w_head_in, w_head),
        (latents_in, latents),
        (target_in, target),
    ):
        load(src, dst)
    text_load = load_sem.at[len(loads)]

    @pl.when(here.xl == 0)
    def _():
        pltpu.make_async_copy(prompt_in, either, text_load).start()

    @pl.when(here.xl == 1)
    def _():
        pltpu.make_async_copy(null_in, either, text_load).start()

    for copy in loads[:6]:
        copy.wait()
    pl.semaphore_wait(barrier, len(partners))

    text_ring = RingY(here, text, slice(None), here.other_tokens(), text_recv, text_send)
    rings = []
    for index in (QUERY, OUT):
        base = weights.at[index]
        rings.append(
            (
                RingFour(here, base, x_first, x_part, "x", recv_x.at[index], send_x.at[index]),
                RingFour(here, base, z_first, LANES, "z", recv_z.at[index], send_z.at[index]),
                RingY(
                    here, base, y_lanes, here.other_columns(), recv_y.at[index], send_y.at[index]
                ),
            )
        )
    key_value = Pair(here, pair_weights, pair_recv, pair_send)

    x_query, z_query, y_query = rings[QUERY]
    x_out, z_out, y_out = rings[OUT]

    def small_round(index, k):
        for ring in rings[index][:2]:
            ring.round(k)
            if k == pairs:
                ring.begin_four()

    def go_four(index, k):
        for ring in rings[index][:2]:
            ring.four(k)

    def all_here(index):
        for ring in rings[index][:2]:
            ring.from_sibling()
        for y in range(ny):
            rings[index][2].from_sibling(y)

    for ring in rings[QUERY]:
        ring.start()

    def text_row(index):
        place = lax.shift_right_logical(index, log2(own_rows)) & (pairs - 1)
        place = place * 2 + (lax.shift_right_logical(index, log2(quarter)) & 1)
        place = place * 2 + (lax.shift_right_logical(index, log2(eighth)) & 1)
        place = place * 2 + (lax.shift_right_logical(index, log2(half)) & 1)
        return place * own_rows + (index & (own_rows - 1))

    square_iota = functools.partial(lax.broadcasted_iota, jnp.int32, (text_rows, text_rows))
    order = jnp.where(text_row(square_iota(0)) == square_iota(1), 1.0, 0.0).astype(BF16)

    pltpu.make_async_copy(prompt_in, either, text_load).wait()
    context[...] = dot(order, either[...]).astype(BF16)
    for copy in loads[6:8]:
        copy.wait()
    own_key = pair_weights[0, parity, here.xh, here.c]
    own_value = pair_weights[1, parity, here.xh, here.c]
    text[here.y, here.xh, here.c, :rows] = dot_lanes(own_key, context[...]).astype(BF16)
    text[here.y, here.xh, here.c, rows:] = dot_lanes(own_value, context[...]).astype(BF16)
    text_ring.start()
    z_query.over_x()
    y_query.over_x()

    for copy in loads[8:]:
        copy.wait()
    modulation = head_mod[step_ref[0]]
    stack = jnp.concatenate(
        [
            row(cross_gain),
            row(cross_bias),
            row(q_gain),
            row(k_gain),
            1.0 + modulation[1:2],
            modulation[0:1],
            jnp.concatenate([row(head_bias), jnp.zeros((1, width - patch), F32)], axis=1),
            jnp.zeros((LANES - 7, width), F32),
        ],
        axis=0,
    )
    for block in range(blocks):
        lanes = slice(block * LANES, (block + 1) * LANES)
        columns[lanes, :] = stack[:, lanes].T
        w_head_rows[lanes, :] = w_head[:, lanes].T

    def turn(block, total):
        at = rows_of(block, LANES)
        for t in range(token_blocks):
            lanes = slice(t * LANES, (t + 1) * LANES)
            tokens[at, lanes] = latents[lanes, at].T
        return total + gather_down(tokens[at, :].astype(F32))

    zero_row = jnp.zeros((8, token_count), F32)
    unroll = 4 if blocks % 4 == 0 else 1
    mean = down(lax.fori_loop(0, blocks, turn, zero_row, unroll=unroll)) / width

    small_round(QUERY, 1)
    text_ring.over_x()
    x_out.start()
    z_out.start()

    def spread(block, total):
        centred = tokens[rows_of(block, LANES), :].astype(F32) - mean
        return total + gather_down(centred * centred)

    variance = down(lax.fori_loop(0, blocks, spread, zero_row, unroll=unroll)) / width
    inverse = lax.rsqrt(variance + NORM_EPS)

    def normalise(block, carry):
        at = rows_of(block, LANES)
        unit = (tokens[at, :].astype(F32) - mean) * inverse
        cross_in[at, :] = (unit * columns[at, 0:1] + columns[at, 1:2]).astype(BF16)
        return carry

    y_query.round(1)
    z_out.over_x()
    if pairs > 1:
        small_round(QUERY, 2)
    text_ring.round(1)
    lax.fori_loop(0, blocks, normalise, 0, unroll=unroll)

    y_out.start()
    key_value.start()
    for k in range(3, pairs + 1):
        small_round(QUERY, k)
        small_round(OUT, k - 2)
        if k == 3:
            y_out.over_x()
            y_query.round(2)
            text_ring.round(2)
    if pairs < 3:
        y_out.over_x()
        if pairs > 1:
            y_query.round(2)
            text_ring.round(2)
    if pairs > 2:
        y_query.round(3)
        text_ring.round(3)
    if pairs > 1:
        small_round(OUT, pairs - 1)
        y_out.round(1)
    go_four(QUERY, 1)
    small_round(OUT, pairs)
    if pairs > 3:
        text_ring.round(4)
        y_query.round(4)
    if pairs > 1:
        y_out.round(2)
    else:
        y_out.round(1)
    go_four(QUERY, 2)
    key_value.over_x()
    for y in range(ny):
        text_ring.from_sibling(y)

    keys = text[:, :, :, :rows, :].reshape(width, text_rows).astype(F32)
    values = text[:, :, :, rows:, :].reshape(width, text_rows).astype(F32)
    key_inverse = lax.rsqrt(down(keys * keys) / width + NORM_EPS)
    for h in range(heads):
        lanes = slice(h * LANES, (h + 1) * LANES)
        one = keys[lanes]
        key_raw[:, lanes] = one.T.astype(BF16)
        key_normed[h] = (one * key_inverse * columns[lanes, 3:4]).T.astype(BF16)
        value_rows[h] = values[lanes].T.astype(BF16)

    go_four(OUT, 1)
    all_here(QUERY)

    def project(i, total):
        raw = dot(weights[QUERY, pl.ds(i * 2, 2)].reshape(2 * band, width), cross_in[...])
        query_raw[rows_of(i, 2 * band), :] = raw
        return total + gather_down(raw * raw)

    square = lax.fori_loop(0, pairs // 2, project, zero_row)
    if pairs > 2:
        y_out.round(3)
    key_value.begin_y()
    square = lax.fori_loop(pairs // 2, pairs, project, square)
    query_inverse = lax.rsqrt(down(square) / width + NORM_EPS)

    length = here.xl * text_rows + (1 - here.xl) * length_ref[0]
    visible = text_row(lax.broadcasted_iota(jnp.int32, (text_rows, token_count), 0)) < length

    def attend(h, carry):
        at = rows_of(h, LANES)
        query[at, :] = (query_raw[at, :] * query_inverse * columns[at, 2:3]).astype(BF16)
        scores = dot(key_normed[h], query[at, :]) * root
        masked = jnp.where(visible, scores, -1e30)
        terms = jnp.where(visible, jnp.exp(masked - jnp.max(masked, axis=0, keepdims=True)), 0.0)
        shares = terms / down(terms)
        attn[h] = shares
        attended[at, :] = lax.dot_general(
            value_rows[h],
            shares.astype(BF16),
            (((0,), (0,)), ((), ())),
            preferred_element_type=F32,
        ).astype(BF16)
        return carry

    lax.fori_loop(0, heads // 4, attend, 0, unroll=True)
    go_four(OUT, 2)
    lax.fori_loop(heads // 4, heads // 2, attend, 0, unroll=True)
    if pairs > 3:
        y_out.round(4)
    lax.fori_loop(heads // 2, heads, attend, 0, unroll=True)
    all_here(OUT)

    cutting = (token_blocks + 1) // 2 * LANES
    parts = [slice(0, cutting)] + ([slice(cutting, token_count)] if cutting < token_count else [])

    def swap(number, branch):
        ref = noise.at[branch, :, parts[number]]
        return remote(
            ref, ref, swap_sem.at[0, number], swap_sem.at[1, number], here.other_branch()
        )

    def head_forward(number):
        lanes = parts[number]
        start = jnp.zeros((8, lanes.stop - lanes.start), F32)

        def project_out(i, total):
            at = rows_of(i, 2 * band)
            matrix = weights[OUT, pl.ds(i * 2, 2)].reshape(2 * band, width)
            rows_after = dot(matrix, attended[:, lanes]) + tokens[at, lanes].astype(F32)
            after[at, lanes] = rows_after
            return total + gather_down(rows_after)

        head_mean = down(lax.fori_loop(0, pairs, project_out, start)) / width

        def head_spread(block, total):
            centred = after[rows_of(block, LANES), lanes] - head_mean
            return total + gather_down(centred * centred)

        variance = down(lax.fori_loop(0, blocks, head_spread, start, unroll=unroll)) / width
        head_inverse = lax.rsqrt(variance + NORM_EPS)

        def modulate(block, carry):
            at = rows_of(block, LANES)
            unit = (after[at, lanes] - head_mean) * head_inverse
            head_in[at, lanes] = (unit * columns[at, 4:5] + columns[at, 5:6]).astype(BF16)
            return carry

        lax.fori_loop(0, blocks, modulate, 0, unroll=unroll)
        noise[here.xl, :, lanes] = dot(w_head[...], head_in[:, lanes]) + columns[:patch, 6:7]
        swap(number, here.xl).start()
        return head_mean, head_inverse

    factor = GUIDE_SCALE - (2.0 * GUIDE_SCALE - 1.0) * here.xl.astype(F32)

    def head_backward(number, head_mean, head_inverse):
        lanes = parts[number]
        start = jnp.zeros((8, lanes.stop - lanes.start), F32)
        swap(number, 1 - here.xl).wait_recv()
        cond, null = noise[0, :, lanes], noise[1, :, lanes]
        guided = null + GUIDE_SCALE * (cond - null)
        guided_ref[:, lanes] = guided
        d_noise = (factor * (guided - target[:, lanes].astype(F32))).astype(BF16)

        def head_back(block, sums):
            at = rows_of(block, LANES)
            unit = (after[at, lanes] - head_mean) * head_inverse
            part_unit = dot(w_head_rows[at, :], d_noise) * columns[at, 4:5]
            d_unit[at, lanes] = part_unit
            return (sums[0] + gather_down(part_unit), sums[1] + gather_down(part_unit * unit))

        first_sum, second_sum = lax.fori_loop(
            0, blocks, head_back, (start, start), unroll=unroll
        )
        first_mean, second_mean = down(first_sum) / width, down(second_sum) / width

        def norm_back(block, carry):
            at = rows_of(block, LANES)
            unit = (after[at, lanes] - head_mean) * head_inverse
            grads = (head_inverse * (d_unit[at, lanes] - first_mean - unit * second_mean)).astype(
                BF16
            )
            for t in range(lanes.start, lanes.stop, LANES):
                d_after[t : t + LANES, at] = grads[:, t - lanes.start : t - lanes.start + LANES].T
            return carry

        lax.fori_loop(0, blocks, norm_back, 0, unroll=unroll)

    stats = [head_forward(number) for number in range(len(parts))]
    def fold(values):
        return jnp.concatenate(
            [values[:, q * middle : (q + 1) * middle] for q in range(4)], axis=0
        )

    def split(values):
        high = values.astype(BF16)
        low = (values - high.astype(F32)).astype(BF16)
        return jnp.concatenate([high, low], axis=0)

    first_row = here.c * half + parity * quarter + here.xh * eighth
    own_span = pl.ds(pl.multiple_of(first_row, eighth), eighth)
    own_lanes = rows_of(pair, wide)
    near = key_raw[own_span, :].astype(F32)
    near_inverse = lax.rsqrt(jnp.mean(near * near, axis=-1, keepdims=True) + NORM_EPS)
    near_unit = key_raw[own_span, own_lanes].astype(F32) * near_inverse

    def multiply(left, lead):
        both = split(left)

        def columns_of(block, carry):
            at = rows_of(block, 2 * LANES)
            if lead:
                matrix = pair_weights[:, :, :, :, :, at].reshape(2 * wide, 2 * LANES)
            else:
                matrix = pair_weights[0, :, :, :, :, at].reshape(wide, 2 * LANES)
            result = dot(both, matrix)
            product[:, at] = result[:eighth] + result[eighth:]
            return carry

        lax.fori_loop(0, blocks // 2, columns_of, 0, unroll=2)

    def exchange(send, recv, lane):
        for d in range(1, pairs):
            q = lax.rem(pair + d, pairs)
            remote(
                send.at[q],
                recv.at[pair],
                tail_sem.at[lane],
                tail_sem.at[lane + 1],
                here.device(y=q * 2 + parity),
            ).start()
        ref = recv.at[pl.ds(0, max(1, pairs - 1))]
        return remote(ref, ref, tail_sem.at[lane], tail_sem.at[lane + 1], here.sibling())

    def collect(send, recv):
        total = send[pair].astype(F32)
        for d in range(1, pairs):
            total = total + recv[lax.rem(pair + d, pairs)].astype(F32)
        return total

    for number, (head_mean, head_inverse) in enumerate(stats):
        head_backward(number, head_mean, head_inverse)

    def out_back(block, carry):
        at = rows_of(block, 2 * LANES)
        matrix = weights[OUT, :, :, :, :, at].reshape(width, 2 * LANES)
        d_attended[:, at] = dot(d_after[...], matrix).astype(BF16)
        return carry

    lax.fori_loop(0, blocks // 2, out_back, 0, unroll=2)
    key_value.over_y()

    def attend_back(h, carry):
        at = rows_of(h, LANES)
        grads = d_attended[:, at]
        shares = attn[h]
        d_shares = dot_lanes(value_rows[h], grads)
        d_scores = shares * (d_shares - down(d_shares * shares))
        d_text[0, :, at] = dot_lanes((d_scores * root).astype(BF16), query[at, :])
        d_text[1, :, at] = dot(shares.astype(BF16), grads)
        return carry

    def group(i):
        return lax.rem(pair + (i + 1), pairs)

    def core_span(c):
        return pl.ds(pl.multiple_of(c * half, half), half)

    def to_sibling(i):
        lanes = rows_of(group(i), wide)
        return remote(
            d_text.at[:, core_span(1 - here.c), lanes],
            d_sibling.at[:, :, lanes],
            sibling_sem.at[0, i],
            sibling_sem.at[1, i],
            here.sibling(),
        )

    def to_row(i, odd, xh):
        lanes = rows_of(group(i), wide)
        span = pl.ds(pl.multiple_of(odd * quarter + xh * eighth, eighth), eighth)
        return remote(
            y_send.at[:, span, lanes],
            y_recv.at[here.y, here.xh],
            y_send_sem.at[i],
            y_recv_sem.at[here.y * 2 + here.xh],
            here.device(y=group(i) * 2 + odd, xh=xh),
        )

    def sum_cores(i):
        lanes = rows_of(group(i), wide)
        to_sibling(i).wait_recv()
        both = d_text[:, core_span(here.c), lanes] + d_sibling[:, :, lanes]
        y_send[:, :, lanes] = both.astype(BF16)
        if i < pairs - 1:
            for odd in (0, 1):
                for xh in (0, 1):
                    to_row(i, jnp.int32(odd), jnp.int32(xh)).start()
        else:
            to_row(i, 1 - parity, here.xh).start()
            to_row(i, 1 - parity, 1 - here.xh).start()
            to_row(i, parity, 1 - here.xh).start()
            d_sibling[:, :, lanes] = both

    for i in range(pairs):
        for j in range(heads // pairs):
            attend_back(group(i) * (heads // pairs) + j, 0)
        to_sibling(i).start()
        if i > 0:
            sum_cores(i - 1)
        if i == pairs - 2 or pairs == 1:
            key_value.from_sibling()
            multiply(near_unit * near_inverse, False)
            for q in range(pairs):
                unit_send[q] = fold(product[q * own_rows : (q + 1) * own_rows, :])
            units = exchange(unit_send, unit_recv, 2)
    sum_cores(pairs - 1)

    eighth_span = pl.ds(
        pl.multiple_of(parity * quarter + here.xh * eighth, eighth), eighth
    )
    own_sum = d_sibling[:, eighth_span, own_lanes]
    near_y = here.y + 1 - 2 * parity
    sources = [(lax.rem(pair * 2 + d, ny), xh) for d in range(2, ny) for xh in (0, 1)]
    sources += [(here.y, 1 - here.xh), (near_y, here.xh), (near_y, 1 - here.xh)]
    for y, xh in sources:
        ref = y_recv.at[y, xh]
        remote(
            ref, ref, y_send_sem.at[0], y_recv_sem.at[y * 2 + xh], here.sibling()
        ).wait_recv()
        own_sum = own_sum + y_recv[y, xh].astype(F32)
    if pairs > 1:
        units.wait_recv()
    unit_total = collect(unit_send, unit_recv)
    lane_gain[...] = row(k_gain)
    own_gain = lane_gain[:, own_lanes]
    gained = own_sum[0] * own_gain
    statistic = jnp.sum(gained * near_unit, axis=-1, keepdims=True) / width
    multiply(jnp.concatenate([near_inverse * gained, own_sum[1]], axis=1), True)
    for q in range(pairs):
        span = slice(q * own_rows, (q + 1) * own_rows)
        grad_send[q, :, :middle] = fold(product[span, :]).astype(BF16)
        both = jnp.broadcast_to(statistic[span], (own_rows, LANES))
        rounded = both.astype(BF16).astype(F32)
        low_half = lax.broadcasted_iota(jnp.int32, (own_rows, LANES), 1) < LANES // 2
        both = jnp.where(low_half, rounded, both - rounded)
        grad_send[q, :, middle:] = jnp.concatenate([both] * 4, axis=0).astype(BF16)
    grads = exchange(grad_send, grad_recv, 4)
    if pairs > 1:
        grads.wait_recv()
    total = collect(grad_send, grad_recv)
    both = total[:, middle : middle + 1] + total[:, middle + LANES // 2 : middle + LANES // 2 + 1]
    own_grad = total[:, :middle] - both * unit_total

    def unfold(values):
        for q in range(4):
            grad_ref[:, q * middle : (q + 1) * middle] = values[q * own_rows : (q + 1) * own_rows]

    @pl.when(here.xl == 0)
    def _():
        unfold(own_grad)

    @pl.when(here.xl == 1)
    def _():
        z_send[...] = own_grad.astype(BF16)
        for d in range(1, nz):
            remote(
                z_send, z_recv.at[here.z], tail_sem.at[6], tail_sem.at[7], here.at_z(d)
            ).start()
        ref = z_recv.at[pl.ds(0, nz - 1)]
        gathered = remote(ref, ref, tail_sem.at[6], tail_sem.at[7], here.sibling())
        gathered.wait_recv()
        others = z_recv[here.up_z(1)].astype(F32)
        for d in range(2, nz):
            others = others + z_recv[here.up_z(d)].astype(F32)
        unfold((own_grad + others) / nz)
        gathered.wait_send()

    for number in range(len(parts)):
        swap(number, here.xl).wait_send()
    if pairs > 1:
        units.wait_send()
        grads.wait_send()
    for i in range(pairs):
        to_sibling(i).wait_send()
        ref = y_send.at[:, :, rows_of(group(i), wide)]
        if i == pairs - 1:
            ref = y_send.at[:, pl.ds(0, 3 * eighth), rows_of(group(i), wide)]
        remote(ref, ref, y_send_sem.at[i], y_recv_sem.at[0], here.sibling()).wait_send()
    text_ring.finish()
    key_value.finish()
    for three in rings:
        for ring in three:
            ring.finish()


def hand_over(guided_in, grad_in, guided_ref, grad_ref):
    guided_ref[...] = guided_in[...]
    grad_ref[...] = grad_in[...]


def on_device(
    latents,
    prompt,
    null_embed,
    text_lengths,
    timesteps,
    head_mod,
    cross_gain,
    cross_bias,
    q_gain,
    k_gain,
    w_query,
    w_key,
    w_value,
    w_out,
    w_head,
    head_bias,
    target,
):
    nz = lax.axis_size("clip")
    ny = lax.axis_size("seq") // 4
    tokens = latents[0, 0]
    count, width = tokens.shape
    text_rows = null_embed.shape[0]
    rows = w_query.shape[1]
    patch = w_head.shape[1]
    heads = width // LANES
    pairs = ny // 2
    wide = width // pairs
    middle = width // 4
    half, quarter, eighth = text_rows // 2, text_rows // 4, text_rows // 8
    own_rows = text_rows // ny // 4
    dma = pltpu.SemaphoreType.DMA
    vmem = pl.BlockSpec(memory_space=pltpu.VMEM)
    smem = pl.BlockSpec(memory_space=pltpu.SMEM)
    guided, grad = pl.pallas_call(
        kernel,
        out_shape=(
            jax.ShapeDtypeStruct((patch, count), F32),
            jax.ShapeDtypeStruct((own_rows, width), F32),
        ),
        in_specs=[smem, smem]
        + [pl.BlockSpec(memory_space=pl.ANY)] * 4
        + [vmem] * 4
        + [pl.BlockSpec(memory_space=pl.ANY)] * 5
        + [vmem]
        + [pl.BlockSpec(memory_space=pl.ANY)],
        out_specs=(vmem, vmem),
        scratch_shapes=[
            pltpu.VMEM((count, width), BF16),
            pltpu.VMEM((text_rows, width), BF16),
            pltpu.VMEM(head_mod.shape, F32),
            pltpu.VMEM((patch, width), BF16),
            pltpu.VMEM((patch, count), BF16),
            pltpu.VMEM((2, ny, 2, 2, rows, width), BF16),
            pltpu.VMEM((2, 2, 2, 2, rows, width), BF16),
            pltpu.VMEM((ny, 2, 2, 2 * rows, text_rows), BF16),
            pltpu.VMEM((text_rows, width), BF16),
            pltpu.VMEM((width, LANES), F32),
            pltpu.VMEM((width, patch), BF16),
            pltpu.VMEM((width, count), BF16),
            pltpu.VMEM((width, count), BF16),
            pltpu.VMEM((width, count), F32),
            pltpu.VMEM((width, count), BF16),
            pltpu.VMEM((heads, text_rows, LANES), BF16),
            pltpu.VMEM((heads, text_rows, LANES), BF16),
            pltpu.VMEM((text_rows, width), BF16),
            pltpu.VMEM((heads, text_rows, count), F32),
            pltpu.VMEM((width, count), BF16),
            pltpu.VMEM((width, count), F32),
            pltpu.VMEM((width, count), BF16),
            pltpu.VMEM((width, count), F32),
            pltpu.VMEM((count, width), BF16),
            pltpu.VMEM((count, width), BF16),
            pltpu.VMEM((2, patch, count), F32),
            pltpu.VMEM((2, text_rows, width), F32),
            pltpu.VMEM((2, half, width), F32),
            pltpu.VMEM((2, half, width), BF16),
            pltpu.VMEM((ny, 2, 2, eighth, wide), BF16),
            pltpu.VMEM((eighth, width), F32),
            pltpu.VMEM((1, width), F32),
            pltpu.VMEM((pairs, 4 * own_rows, middle), F32),
            pltpu.VMEM((pairs, 4 * own_rows, middle), F32),
            pltpu.VMEM((pairs, 4 * own_rows, middle + LANES), BF16),
            pltpu.VMEM((pairs, 4 * own_rows, middle + LANES), BF16),
            pltpu.VMEM((4 * own_rows, middle), BF16),
            pltpu.VMEM((nz, 4 * own_rows, middle), BF16),
            dma((4 * ny,)),
            dma((3,)),
            dma((2, 4 * ny)),
            dma((2, 3)),
            dma((2, ny + 17)),
            dma((2, 4)),
            dma((2, ny + 16)),
            dma((2, 3)),
            dma((8,)),
            dma((3,)),
            dma((2, 2)),
            dma((2, pairs)),
            dma((2 * ny,)),
            dma((pairs,)),
            dma((8,)),
            dma((14,)),
        ],
        compiler_params=pltpu.CompilerParams(
            collective_id=0, has_side_effects=True, vmem_limit_bytes=60 * 1024 * 1024
        ),
        cost_estimate=pl.CostEstimate(
            flops=8 * count * width * width, bytes_accessed=8 * count * width, transcendentals=0
        ),
    )(
        text_lengths,
        timesteps,
        tokens,
        prompt[0],
        null_embed,
        head_mod,
        cross_gain,
        cross_bias,
        q_gain,
        k_gain,
        w_query.T,
        w_key.T,
        w_value.T,
        w_out.T,
        w_head.T,
        head_bias,
        target[0].T,
    )
    guided, grad = pl.pallas_call(
        hand_over,
        out_shape=(
            jax.ShapeDtypeStruct((patch, count), F32),
            jax.ShapeDtypeStruct((own_rows, width), F32),
        ),
        in_specs=[vmem, vmem],
        out_specs=(vmem, vmem),
    )(guided, grad)
    return (guided.T[None], grad.reshape(1, 1, own_rows, width))


def solution(mesh):
    return jax.shard_map(
        on_device,
        mesh=mesh,
        in_specs=(
            P("clip", "guide", "seq", None),
            P("clip", None, None),
            P(),
            P("clip"),
            P("clip"),
            P(),
            P(),
            P(),
            P(),
            P(),
            P(None, "seq"),
            P(None, "seq"),
            P(None, "seq"),
            P(None, "seq"),
            P(),
            P(),
            P("clip", "seq", None),
        ),
        out_specs=(P("clip", "seq", None), P("clip", "guide", "seq", None)),
        check_vma=False,
    )
```
